32 devices in a mesh: comp: 2 (over core), tile: 4 (over y, x), row: 4 (over z).
Axes of the slice: x: 2, y: 2, z: 4, core: 2. Of those that a mesh axis runs over, the one named last changes fastest.
Arguments:
- state: bfloat16 [2, 4, 512, 12288], P('comp', 'tile', 'row'), may hold values from -8 to 8
- pairs: int32 [2, 512], replicated, may hold values from 0 to 511, as said below
- wet: int32 [4], P('tile'), may hold values 0 or 1
- mix_weight: bfloat16 [2, 8, 32, 16], replicated, may hold values from -1 to 1
- depth_weight: float32 [3, 7, 7, 192], replicated, may hold values from -0.875 to 0.875
- norm_gain: float32 [3, 192], replicated, may hold values from 0.1 to 1.9
- inner_weight: bfloat16 [3, 192, 768], replicated, may hold values from -0.4375 to 0.4375
- outer_weight: bfloat16 [3, 768, 192], replicated, may hold values from -0.21875 to 0.21875
Outputs:
- next_state: bfloat16 [2, 4, 512, 12288], P('comp', 'tile', 'row')
The draws below stay inside these ranges and needn't reach their ends.
Inputs may be any that keep to these rules, and one draw needn't show every extreme that they name: Each row pairs[s] is a permutation of the 512 blocks of the other section, and a block's partner lies in the same band of 128 tile rows. Within one band, the 32 blocks of tile q of one section receive exactly 8 blocks from that band of each tile of the other section.
All inputs are finite; a program needn't handle non-finite values. No bound on the sum of `wet` on one device may be relied on, other than what follows from the above.
Results may differ from the reference program's by a relative error of at most 0.0053.
Values may be sent and summed in bfloat16 or wider, within the bound.
No kernel may reach another device: no remote copies, remote signals or barrier semaphores. Data moves between devices by JAX's collectives and lax.ppermute only.
A program may use at most 64 MiB of HBM per device.

```python
import math
import jax
import jax.numpy as jnp
from jax import lax

C = 192
HID = 768
IC = 128
G = 8
TH = 512
TW = 64
BH = 16
BW = 16
TILES_DEV = 1
RH = 128
RBD = 8
NRB = 32
NCB = 4
IG = 16
TILES = 4
NBLK = 512
N_TILE = 4


def draw_state(key, part):
    key_base, key_chan, key_cell = jax.random.split(key, 3)
    shape_full = (2, TILES, TH, TW, C)
    base = jax.random.normal(key_base, shape_full, jnp.float32)
    channel_scale = jnp.exp(jax.random.uniform(key_chan, (C,), jnp.float32, math.log(0.3), math.log(3.0)))
    cell_scale = jnp.exp(jax.random.uniform(key_cell, (2, TILES, TH, TW, 1), jnp.float32, math.log(0.3), math.log(3.0)))
    values = jnp.clip(base * channel_scale * cell_scale, -8.0, 8.0)
    return values.reshape(2, TILES, TH, TW * C).astype(jnp.bfloat16)


def draw_pairs(key, part):
    per_dev = TILES_DEV * RBD * NCB
    peer = per_dev // N_TILE
    total = per_dev * N_TILE
    bands = TH // RH

    def band_ids(band):
        position = jnp.arange(total, dtype=jnp.int32)
        owner = position // per_dev
        local = position % per_dev
        tile_local = local // (RBD * NCB)
        block_row = local // NCB % RBD
        block_col = local % NCB
        return ((owner * TILES_DEV + tile_local) * NRB + band * RBD + block_row) * NCB + block_col

    def one_band(band_key):
        key_src, key_slot = jax.random.split(band_key)
        src_perm = jax.vmap(lambda single: jax.random.permutation(single, per_dev))(jax.random.split(key_src, N_TILE))
        sources = (jnp.arange(N_TILE, dtype=jnp.int32)[:, None] * per_dev + src_perm.astype(jnp.int32)).reshape(N_TILE, N_TILE, peer)
        incoming = sources.transpose(1, 0, 2).reshape(N_TILE, per_dev)
        slot_perm = jax.vmap(lambda single: jax.random.permutation(single, per_dev))(jax.random.split(key_slot, N_TILE))
        return jnp.take_along_axis(incoming, slot_perm.astype(jnp.int32), 1).reshape(total)

    def one_section(section_key):
        row_out = jnp.zeros((NBLK,), jnp.int32)
        band_keys = jax.random.split(section_key, bands)
        for band in range(bands):
            ids = band_ids(band)
            picked = one_band(band_keys[band])
            row_out = row_out.at[ids].set(jnp.take(ids, picked))
        return row_out
    section_keys = jax.random.split(jax.random.fold_in(key, 17), 2)
    return jnp.stack([one_section(section_keys[0]), one_section(section_keys[1])]).astype(jnp.int32)


def place_ends(result, key, least, largest):
    spot = [jax.random.randint(jax.random.fold_in(key, axis), (), 0, length) for axis, length in enumerate(result.shape)]
    main_axis = result.shape.index(max(result.shape))
    beside = spot[:main_axis] + [(spot[main_axis] + 1) % result.shape[main_axis]] + spot[main_axis + 1:]
    return result.at[tuple(spot)].set(least).at[tuple(beside)].set(largest)


def bell_draw(rng, extent, scale, bound, held_as=jnp.bfloat16):
    values = jax.random.normal(rng, extent, jnp.float32) * scale
    return jnp.minimum(jnp.maximum(values, -bound), bound).astype(held_as)


def setup_inputs(seed: int = 0) -> dict:
    arg_keys = jax.random.split(jax.random.key(seed), 9)
    state = draw_state(jax.random.fold_in(arg_keys[8], 71), 0)
    pairs = draw_pairs(jax.random.fold_in(arg_keys[8], 71), 0)
    wet = place_ends((jax.random.randint(arg_keys[2], (TILES,), 0, 3) < 2).astype(jnp.int32), jax.random.fold_in(arg_keys[2], 1), 0, 1)
    mix_weight = bell_draw(arg_keys[3], (2, G, 2 * IG, IG), (2 * IG) ** -0.5, 1.0)
    depth_weight = bell_draw(arg_keys[4], (3, 7, 7, C), 49 ** -0.5, 0.875, jnp.float32)
    norm_gain = jnp.clip(1.0 + 0.18 * jax.random.normal(arg_keys[5], (3, C), jnp.float32), 0.1, 1.9)
    inner_weight = bell_draw(arg_keys[6], (3, C, HID), C ** -0.5, 0.4375)
    outer_weight = bell_draw(arg_keys[7], (3, HID, C), HID ** -0.5, 0.21875)
    return {"state": state, "pairs": pairs, "wet": wet, "mix_weight": mix_weight, "depth_weight": depth_weight, "norm_gain": norm_gain, "inner_weight": inner_weight, "outer_weight": outer_weight}


def block_view(section_state):
    cells = section_state.reshape(TILES, NRB, BH, NCB, BW, C)[..., :IC]
    return cells.transpose(0, 1, 3, 2, 4, 5).reshape(NBLK, BH, BW, IC)

def spread_norm_tile(field, depth, gain):
    padded = jnp.pad(field, ((3, 3), (3, 3), (0, 0)))
    spread = jnp.zeros((TH, TW, C), jnp.float32)
    for row_off in range(7):
        for col_off in range(7):
            spread = spread + padded[row_off:row_off + TH, col_off:col_off + TW, :].astype(jnp.float32) * depth[row_off, col_off]
    average = lax.optimization_barrier(jnp.mean(spread, -1, keepdims=True))
    centred = spread - average
    variance = lax.optimization_barrier(jnp.mean(centred * centred, -1, keepdims=True))
    normed = (centred * lax.rsqrt(variance + 1e-06) * gain).astype(jnp.bfloat16)
    return normed.reshape(TH * TW, C)

def project_rows(normed, inner, outer):
    hidden = jax.nn.gelu(jnp.dot(normed, inner, preferred_element_type=jnp.float32), approximate=True).astype(jnp.bfloat16)
    return jnp.dot(hidden, outer, preferred_element_type=jnp.float32)

def reference(state, pairs, wet, mix_weight, depth_weight, norm_gain, inner_weight, outer_weight):
    results = []
    for section in range(2):
        other_blocks = block_view(state[1 - section])
        partners = jnp.take(other_blocks, pairs[section], axis=0).reshape(TILES, NRB, NCB, BH, BW, IC)
        partners = partners.transpose(0, 1, 3, 2, 4, 5).reshape(TILES, TH, NCB, BW, IC)
        if section == 0:
            factors = jnp.ones((TILES,), jnp.float32)
            layers = [0, 1]
        else:
            factors = wet.astype(jnp.float32)
            layers = [2]
        mixing = mix_weight[section].astype(jnp.float32)

        def per_tile(inputs, layers=layers, mixing=mixing):
            tile_flat, partner_rows, factor = inputs
            cells = tile_flat.reshape(TH, NCB, BW, C)
            own_int = cells[..., :IC]
            joined = jnp.concatenate([own_int.reshape(TH, NCB, BW, G, IG), partner_rows.reshape(TH, NCB, BW, G, IG)], -1).astype(jnp.float32)
            mixed = jnp.einsum('hcbgi,gio->hcbgo', joined, mixing).reshape(TH, NCB, BW, IC)
            merged = (own_int.astype(jnp.float32) + mixed).astype(jnp.bfloat16)
            field = jnp.concatenate([merged, cells[..., IC:]], -1).reshape(TH, TW, C)
            for layer in layers:
                normed = spread_norm_tile(field, depth_weight[layer], norm_gain[layer])
                update = project_rows(normed, inner_weight[layer], outer_weight[layer])
                field = (field.reshape(TH * TW, C).astype(jnp.float32) + factor * update).astype(jnp.bfloat16).reshape(TH, TW, C)
            return field.reshape(TH, TW * C)
        results.append(lax.map(per_tile, (state[section], partners, factors)))
    return jnp.stack(results)
```

```python
import jax
import jax.numpy as jnp
from jax import lax
from jax.experimental import pallas as pl
from jax.experimental.pallas import tpu as pltpu
from jax.sharding import PartitionSpec as P

VM = pltpu.VMEM
PC = 8
LG = 16
LN = 128


def lane_bit(shape, bit):
    return (lax.broadcasted_iota(jnp.int32, shape, 1) & bit) == 0


def lroll(x, shift):
    return pltpu.roll(x, shift % LN, 1)


def swap_stage(a, b, bit, m):
    return jnp.where(m, a, lroll(b, bit)), jnp.where(m, lroll(a, -bit), b)


def to_patch(v):
    half = len(v) // 2
    shape = v[0].shape
    m64, m32, m16 = (lane_bit(shape, b) for b in (64, 32, 16))
    per = 3
    u = {}
    for j in range(4):
        for t in range(per):
            q = per * j + t
            a, b = v[q // 2], v[q // 2 + half]
            if q % 2 == 0:
                u[j, t] = jnp.where(m64, a, lroll(b, 64))
            else:
                u[j, t] = jnp.where(m64, lroll(a, 64), b)
    out = []
    for t in range(per):
        a0, b0 = swap_stage(u[0, t], u[2, t], 32, m32)
        a1, b1 = swap_stage(u[1, t], u[3, t], 32, m32)
        out += swap_stage(a0, a1, 16, m16)
        out += swap_stage(b0, b1, 16, m16)
    return out


def from_patch(z):
    half = len(z) // 2
    shape = z[0].shape
    m64, m32, m16 = (lane_bit(shape, b) for b in (64, 32, 16))
    per = len(z) // 4
    u = {}
    for t in range(per):
        a0, a1 = swap_stage(z[4 * t], z[4 * t + 1], 16, m16)
        b0, b1 = swap_stage(z[4 * t + 2], z[4 * t + 3], 16, m16)
        u[0, t], u[2, t] = swap_stage(a0, b0, 32, m32)
        u[1, t], u[3, t] = swap_stage(a1, b1, 32, m32)
    lo, hi = {}, {}
    for j in range(4):
        for t in range(per):
            q = per * j + t
            lo[q] = u[j, t]
            hi[q] = u[j, t]
    v = []
    for n in range(half):
        e, o = u[divmod(2 * n, per)], u[divmod(2 * n + 1, per)]
        v.append(jnp.where(m64, e, lroll(o, 64)))
    for n in range(half):
        e, o = u[divmod(2 * n, per)], u[divmod(2 * n + 1, per)]
        v.append(jnp.where(m64, lroll(e, 64), o))
    return v


def gelu(v):
    return 0.5 * v * (1.0 + jnp.tanh(0.7978845608028654 * (v + 0.044715 * v * v * v)))


def pack_kernel(pairs, place, x_ref, z_ref, out_ref, count):
    section, tile, band = place[0], place[1], place[2]
    nz, rows, _ = z_ref.shape
    width = x_ref.shape[1]
    per = LN * 12
    nj = width // per
    ng = nz // nj
    hold, tiles = out_ref.shape[0], count.shape[0]
    peer = hold // tiles
    of_tile = pairs.shape[1] // tiles
    ncb = nj // 2

    for j in range(nj):
        v = [x_ref[:, j * per + n * LN:j * per + (n + 1) * LN] for n in range(12)]
        for g, zz in enumerate(to_patch(v)):
            z_ref[g * nj + j] = zz
    for q in range(tiles):
        count[q] = 0

    @pl.loop(0, tiles)
    def _(q):
        @pl.loop(0, hold)
        def _(slot):
            source = pairs[1 - section, q * of_tile + band * hold + slot]

            @pl.when(source // of_tile == tile)
            def _():
                local = source % of_tile - band * hold
                rank = count[q]
                count[q] = rank + 1
                row = pl.ds(pl.multiple_of(local // ncb * 16, 16), 16)
                for g in range(out_ref.shape[1] // 2):
                    for h in range(2):
                        out_ref[q * peer + rank, 2 * g + h] = z_ref[g * nj + 2 * (local % ncb) + h, row, :]


def pack(pairs, place, x, tiles, mixed):
    rows, width = x.shape
    nj = width // (LN * 12)
    hold = rows // 16 * (nj // 2)
    vm = pl.BlockSpec(memory_space=VM)
    sm = pl.BlockSpec(memory_space=pltpu.SMEM)
    return pl.pallas_call(
        pack_kernel,
        out_shape=(
            jax.ShapeDtypeStruct((12 * nj, rows, LN), jnp.bfloat16),
            jax.ShapeDtypeStruct((hold, 2 * mixed, 16, LN), jnp.bfloat16),
        ),
        in_specs=[sm, sm, vm],
        out_specs=(vm, vm),
        scratch_shapes=[pltpu.SMEM((tiles,), jnp.int32)],
        compiler_params=pltpu.CompilerParams(vmem_limit_bytes=56 * 2**20),
        name="pack",
    )(pairs, place, x)


def mix_kernel(pairs, place, z_ref, got_ref, w_ref, out_ref, top_ref, bot_ref, zp, count):
    section, tile, band = place[0], place[1], place[2]
    nz, rows, _ = z_ref.shape
    hold, tiles = got_ref.shape[0], count.shape[0]
    mixed = w_ref.shape[0]
    nj = zp.shape[0] // mixed
    peer = hold // tiles
    of_tile = pairs.shape[1] // tiles
    ncb = nj // 2
    for q in range(tiles):
        count[q] = 0

    @pl.loop(0, hold)
    def _(slot):
        q = pairs[section, tile * of_tile + band * hold + slot] // of_tile
        rank = count[q]
        count[q] = rank + 1
        row = pl.ds(pl.multiple_of(slot // ncb * 16, 16), 16)
        for g in range(mixed):
            for h in range(2):
                zp[g * nj + 2 * (slot % ncb) + h, row, :] = got_ref[q * peer + rank, 2 * g + h]

    @pl.loop(0, mixed)
    def _(g):
        gs = pl.ds(g * nj, nj)
        own = z_ref[gs].reshape(nj * rows, LN)
        both = jnp.concatenate([own, zp[gs].reshape(nj * rows, LN)], 1)
        new = own.astype(jnp.float32) + jnp.dot(both, w_ref[g], preferred_element_type=jnp.float32)
        new = new.astype(jnp.bfloat16).reshape(nj, rows, LN)
        out_ref[gs] = new
        top_ref[gs] = new[:, :3]
        bot_ref[gs] = new[:, rows - 3:]

    for n in range(mixed * nj, nz):
        out_ref[n] = z_ref[n]
        top_ref[n] = z_ref[n, :3]
        bot_ref[n] = z_ref[n, rows - 3:]


def mix(pairs, place, z, got, w, tiles):
    nz, rows, _ = z.shape
    nj = nz // 12
    mixed = w.shape[0]
    vm = pl.BlockSpec(memory_space=VM)
    sm = pl.BlockSpec(memory_space=pltpu.SMEM)
    edge = jax.ShapeDtypeStruct((nz, 3, LN), jnp.bfloat16)
    return pl.pallas_call(
        mix_kernel,
        out_shape=(jax.ShapeDtypeStruct(z.shape, jnp.bfloat16), edge, edge),
        in_specs=[sm, sm, vm, vm, vm],
        out_specs=(vm, vm, vm),
        scratch_shapes=[VM((mixed * nj, rows, LN), jnp.bfloat16), pltpu.SMEM((tiles,), jnp.int32)],
        compiler_params=pltpu.CompilerParams(vmem_limit_bytes=56 * 2**20),
        name="mix",
    )(pairs, place, z, got, w)


def layer_kernel(z_ref, top_ref, bot_ref, fac_ref, e_ref, gain_ref, wie_ref, wio_ref, woe_ref, woo_ref,
                 out_ref, outz_ref, otop_ref, obot_ref, zf, lhs, wk, spr, nz, ssum, upd):
    ng = e_ref.shape[0]
    nj = z_ref.shape[0] // ng
    rows = z_ref.shape[1]
    hr = rows // 2
    pad = 8
    m64 = lane_bit((hr, LN), 64)
    delta = lax.broadcasted_iota(jnp.int32, (LG, LN), 0) == lax.broadcasted_iota(jnp.int32, (LG, LN), 1) % LG
    chunk = lax.broadcasted_iota(jnp.int32, (8, LN), 1) // LG

    wk[...] = jnp.zeros_like(wk)
    ssum[...] = jnp.zeros_like(ssum)

    @pl.loop(0, ng)
    def _(g):
        e = e_ref[g]
        for pos, jr in enumerate(list(range(8)) + list(range(8, 12)) + list(range(-4, 0))):
            s = jr - 3
            if abs(s) >= 8 or jr == -4 or jr == 11:
                continue
            r = lroll(e, s * LG)
            r = jnp.where((chunk >= s) & (chunk < 8 + s), r, 0.0)
            for k in range(7):
                tile = jnp.where(delta, jnp.broadcast_to(r[k:k + 1], (LG, LN)), 0.0).astype(jnp.bfloat16)
                wk[pl.ds(k * 256 + pos * LG, LG), 0:LN] = tile
                wk[pl.ds((k + 1) * 256 + pos * LG, LG), LN:2 * LN] = tile
        for j in range(nj):
            zf[j, pl.ds(pad, rows), :] = z_ref[g * nj + j].astype(jnp.float32)
            zf[j, pl.ds(pad - 3, 3), :] = top_ref[g * nj + j].astype(jnp.float32)
            zf[j, pl.ds(pad + rows, 3), :] = bot_ref[g * nj + j].astype(jnp.float32)
        zero = jnp.zeros((hr, LN), jnp.bfloat16)
        for a in range(8):
            v = [zf[j, pl.ds(pad - 3 + a, hr, stride=2), :].astype(jnp.bfloat16) for j in range(nj)]
            for j in range(nj):
                nxt = v[j + 1] if j + 1 < nj else zero
                prv = v[j - 1] if j > 0 else zero
                lhs[pl.ds(j * hr, hr), a * 256:a * 256 + LN] = v[j]
                lhs[pl.ds(j * hr, hr), a * 256 + LN:a * 256 + 256] = jnp.where(m64, nxt, prv)
        sp = jnp.dot(lhs[...], wk[...], preferred_element_type=jnp.float32)
        spr[g] = sp
        ssum[...] += sp

    count = ng * LG
    ones = (lax.broadcasted_iota(jnp.int32, (256, 256), 0) // LG == lax.broadcasted_iota(jnp.int32, (256, 256), 1) // LG)
    ones = ones.astype(jnp.float32).astype(jnp.bfloat16)

    def lane_sum(s):
        hi = s.astype(jnp.bfloat16)
        lo = (s - hi.astype(jnp.float32)).astype(jnp.bfloat16)
        return (jnp.dot(hi, ones, preferred_element_type=jnp.float32)
                + jnp.dot(lo, ones, preferred_element_type=jnp.float32))

    @pl.loop(0, nj)
    def _(j):
        js = pl.ds(pl.multiple_of(j * hr, hr), hr)
        mean = lane_sum(ssum[js, :]) * (1.0 / count)
        q = jnp.zeros((hr, 256), jnp.float32)
        for g in range(ng):
            c = spr[g, js, :] - mean
            q = q + c * c
        rstd = lax.rsqrt(lane_sum(q) * (1.0 / count) + 1e-06)
        for g in range(ng):
            nz[g, js, :] = ((spr[g, js, :] - mean) * rstd * gain_ref[g:g + 1, :]).astype(jnp.bfloat16)

        nat = [[], []]
        for p in range(2):
            nat[p] = from_patch([nz[g, js, p * LN:(p + 1) * LN] for g in range(ng)])
        nat = [jnp.concatenate([a, b], 0) for a, b in zip(*nat)]
        npair = len(nat) // 3
        xe = jnp.concatenate([jnp.concatenate([nat[3 * i], nat[3 * i + 1]], 1) for i in range(npair)], 0)
        xo = jnp.concatenate([jnp.concatenate([nat[3 * i + 1], nat[3 * i + 2]], 1) for i in range(npair)], 0)

        def mlp(x, wi, wo):
            h = gelu(jnp.dot(x, wi[...], preferred_element_type=jnp.float32)).astype(jnp.bfloat16)
            return jnp.dot(h, wo[...], preferred_element_type=jnp.float32)
        ue = mlp(xe, wie_ref, woe_ref)
        uo = mlp(xo, wio_ref, woo_ref)
        for i in range(npair):
            e = ue[i * rows:(i + 1) * rows]
            o = uo[i * rows:(i + 1) * rows]
            for t, val in enumerate((e[:, :LN], e[:, LN:] + o[:, :LN], o[:, LN:])):
                for p in range(2):
                    upd[3 * i + t, pl.ds(p, hr, stride=2), :] = val[p * hr:(p + 1) * hr]
        fac = fac_ref[0, 0]
        res = []
        own = from_patch([z_ref[g * nj + j] for g in range(ng)])
        for n in range(3 * npair):
            ls = pl.ds(pl.multiple_of(j * (3 * npair * LN) + n * LN, LN), LN)
            y = (own[n].astype(jnp.float32) + fac * upd[n]).astype(jnp.bfloat16)
            out_ref[:, ls] = y
            res.append(y)
        for g, zz in enumerate(to_patch(res)):
            outz_ref[g * nj + j] = zz
            otop_ref[g * nj + j] = zz[:3]
            obot_ref[g * nj + j] = zz[rows - 3:]


def layer(z, top, bot, fac, e, gain, wie, wio, woe, woo):
    ng = e.shape[0]
    nj = z.shape[0] // ng
    rows = z.shape[1]
    hr = rows // 2
    vm = pl.BlockSpec(memory_space=VM)
    f32, bf = jnp.float32, jnp.bfloat16
    edge = jax.ShapeDtypeStruct(top.shape, bf)
    return pl.pallas_call(
        layer_kernel,
        out_shape=(jax.ShapeDtypeStruct((rows, nj * 12 * LN), bf), jax.ShapeDtypeStruct(z.shape, bf), edge, edge),
        in_specs=[vm] * 3 + [pl.BlockSpec(memory_space=pltpu.SMEM)] + [vm] * 6,
        out_specs=(vm,) * 4,
        scratch_shapes=[
            VM((nj, rows + 16, LN), f32),
            VM((nj * hr, 2048), bf),
            VM((2048, 256), bf),
            VM((ng, nj * hr, 256), f32),
            VM((ng, nj * hr, 256), bf),
            VM((nj * hr, 256), f32),
            VM((12, rows, LN), f32),
        ],
        compiler_params=pltpu.CompilerParams(vmem_limit_bytes=56 * 2**20),
        name="layer",
    )(z, top, bot, fac, e, gain, wie, wio, woe, woo)


def prep(depth, gain, inner, outer):
    c = gain.shape[0]
    ng = c // LG
    e = jnp.pad(depth[:, ::-1, :], ((0, 1), (0, 1), (0, 0))).reshape(8, 8, ng, LG)
    e = e.transpose(2, 0, 1, 3).reshape(ng, 8, LN)
    gl = jnp.tile(gain.reshape(ng, 1, LG), (1, 16, 1)).reshape(ng, 256)
    wie = jnp.pad(inner, ((0, 64), (0, 0)))
    wio = jnp.pad(inner, ((64, 0), (0, 0)))
    woe = jnp.pad(outer, ((0, 0), (0, 64)))
    woo = jnp.pad(outer, ((0, 0), (64, 0)))
    return e, gl, wie, wio, woe, woo


def halo(top, bot):
    n = lax.axis_size("row")
    return (
        lax.ppermute(bot, "row", [(i, i + 1) for i in range(n - 1)]),
        lax.ppermute(top, "row", [(i + 1, i) for i in range(n - 1)]),
    )


def mix_prep(w):
    groups = w.shape[0]
    parts = w.reshape(groups, 2, 1, LG, 1, LG)
    eye = jnp.eye(PC, dtype=jnp.bool_).reshape(1, 1, PC, 1, PC, 1)
    return jnp.where(eye, parts, jnp.zeros((), w.dtype)).reshape(groups, 2 * LN, LN)


def on_device(state, pairs, wet, mix_weight, depth_weight, norm_gain, inner_weight, outer_weight):
    section = lax.axis_index("comp")
    tiles = lax.axis_size("tile")
    place = jnp.stack([section, lax.axis_index("tile"), lax.axis_index("row")]).astype(jnp.int32)
    x = state[0, 0]
    pick = lambda w, i: lax.dynamic_index_in_dim(w, i, 0, keepdims=False)
    z, outgoing = pack(pairs, place, x, tiles, mix_weight.shape[1])
    crossed = lax.ppermute(outgoing, "comp", [(0, 1), (1, 0)])
    received = lax.all_to_all(crossed, "tile", split_axis=0, concat_axis=0, tiled=True)
    z, top, bot = mix(pairs, place, z, received, mix_prep(pick(mix_weight, section)), tiles)
    top, bot = halo(top, bot)
    which = jnp.where(section == 0, 0, 2)
    weights = prep(pick(depth_weight, which), pick(norm_gain, which), pick(inner_weight, which), pick(outer_weight, which))
    factor = jnp.where(section == 0, 1.0, wet[0].astype(jnp.float32)).reshape(1, 1)
    _, z, top, bot = layer(z, top, bot, factor, *weights)
    top, bot = halo(top, bot)
    weights = prep(depth_weight[1], norm_gain[1], inner_weight[1], outer_weight[1])
    factor = jnp.where(section == 0, 1.0, 0.0).reshape(1, 1)
    out, _, _, _ = layer(z, top, bot, factor, *weights)
    return out[None, None]


def solution(mesh):
    return jax.shard_map(
        on_device,
        mesh=mesh,
        in_specs=(P("comp", "tile", "row", None), P(), P("tile"), P(), P(), P(), P(), P()),
        out_specs=P("comp", "tile", "row", None),
        check_vma=False,
    )
```

```python
import functools
import jax
import jax.numpy as jnp
from jax import lax
from jax.experimental import pallas as pl
from jax.experimental.pallas import tpu as pltpu
from jax.sharding import PartitionSpec as P

VM = pltpu.VMEM
PC = 8
LG = 16
LN = 128
bf, f32 = jnp.bfloat16, jnp.float32
PARAMS = pltpu.CompilerParams(vmem_limit_bytes=56 * 2**20)


def lane_bit(shape, bit):
    return (lax.broadcasted_iota(jnp.int32, shape, 1) & bit) == 0


def lroll(x, shift):
    return pltpu.roll(x, shift % LN, 1)


def swap_stage(a, b, bit, m):
    return jnp.where(m, a, lroll(b, bit)), jnp.where(m, lroll(a, -bit), b)


def to_patch(v):
    half = len(v) // 2
    shape = v[0].shape
    m64, m32, m16 = (lane_bit(shape, b) for b in (64, 32, 16))
    per = 3
    u = {}
    for j in range(4):
        for t in range(per):
            q = per * j + t
            a, b = v[q // 2], v[q // 2 + half]
            if q % 2 == 0:
                u[j, t] = jnp.where(m64, a, lroll(b, 64))
            else:
                u[j, t] = jnp.where(m64, lroll(a, 64), b)
    out = []
    for t in range(per):
        a0, b0 = swap_stage(u[0, t], u[2, t], 32, m32)
        a1, b1 = swap_stage(u[1, t], u[3, t], 32, m32)
        out += swap_stage(a0, a1, 16, m16)
        out += swap_stage(b0, b1, 16, m16)
    return out


def from_patch(z):
    half = len(z) // 2
    shape = z[0].shape
    m64, m32, m16 = (lane_bit(shape, b) for b in (64, 32, 16))
    per = len(z) // 4
    u = {}
    for t in range(per):
        a0, a1 = swap_stage(z[4 * t], z[4 * t + 1], 16, m16)
        b0, b1 = swap_stage(z[4 * t + 2], z[4 * t + 3], 16, m16)
        u[0, t], u[2, t] = swap_stage(a0, b0, 32, m32)
        u[1, t], u[3, t] = swap_stage(a1, b1, 32, m32)
    lo, hi = {}, {}
    for j in range(4):
        for t in range(per):
            q = per * j + t
            lo[q] = u[j, t]
            hi[q] = u[j, t]
    v = []
    for n in range(half):
        e, o = u[divmod(2 * n, per)], u[divmod(2 * n + 1, per)]
        v.append(jnp.where(m64, e, lroll(o, 64)))
    for n in range(half):
        e, o = u[divmod(2 * n, per)], u[divmod(2 * n + 1, per)]
        v.append(jnp.where(m64, lroll(e, 64), o))
    return v


def gelu(h):
    c = 0.7978845608028654
    inside = h * (jnp.asarray(2 * c, bf) + jnp.asarray(8 * 0.044715 * c, bf) * (h * h))
    return h + h * jnp.tanh(inside)


def part(i, n):
    if n & (n - 1) == 0:
        return lax.shift_right_logical(i, n.bit_length() - 1), i & (n - 1)
    return lax.div(i, n), lax.rem(i, n)


def pack_kernel(pairs, place, x_hbm, z_hbm, top_ref, bot_ref, *rest, mixed, tiles):
    outs = rest[:tiles]
    xs, zs, send, order, xsem, zsem, ssem = rest[tiles:]
    ng, nj, rows, _ = zs.shape
    per = x_hbm.shape[1] // nj
    hold = send.shape[0]
    peer = hold // tiles
    of_tile = pairs.shape[1] // tiles
    ncb = nj // 2
    section, tile, band_at = place[0], place[1], place[2]

    def xcopy(j):
        return pltpu.make_async_copy(x_hbm.at[:, pl.ds(pl.multiple_of(j * per, LN), per)], xs.at[j], xsem.at[j])

    def zcopy(j):
        return pltpu.make_async_copy(zs.at[:, j], z_hbm.at[:, j], zsem.at[j])

    for j in range(nj):
        xcopy(j).start()

    @pl.loop(0, tiles)
    def _(q):
        first = lax.bitwise_xor(q, tile) * peer

        def one(slot, rank):
            src_tile, src = part(pairs[1 - section, q * of_tile + band_at * hold + slot], of_tile)
            mine = src_tile == tile
            order[jnp.where(mine, first + rank, hold)] = src - band_at * hold
            return rank + mine.astype(jnp.int32)
        lax.fori_loop(0, hold, one, jnp.int32(0), unroll=8)

    @pl.loop(0, nj)
    def _(j):
        xcopy(j).wait()
        zz = to_patch([xs[j, :, n * LN:(n + 1) * LN] for n in range(12)])
        for g in range(ng):
            zs[g, j] = zz[g]
        for g in range(mixed, ng):
            for r in range(3):
                top_ref[r, pl.ds((g - mixed) * nj + j, 1), :] = zz[g][r:r + 1].astype(f32)
                bot_ref[r, pl.ds((g - mixed) * nj + j, 1), :] = zz[g][rows - 3 + r:rows - 2 + r].astype(f32)
        zcopy(j).start()

    @pl.loop(0, hold)
    def _(at):
        up, side = part(order[at], ncb)
        row = pl.ds(pl.multiple_of(up * 16, 16), 16)
        for g in range(mixed):
            for h in range(2):
                send[at, 2 * g + h] = zs[g, 2 * side + h, row, :]

    copies = [pltpu.make_async_copy(send.at[pl.ds(d * peer, peer)], outs[d], ssem.at[d]) for d in range(tiles)]
    for c in copies:
        c.start()
    for c in copies:
        c.wait()
    for j in range(nj):
        zcopy(j).wait()


def pack(pairs, place, x, tiles, mixed, ng):
    rows, width = x.shape
    per = ng * LG * PC
    nj = width // per
    hold = rows // 16 * (nj // 2)
    vm = pl.BlockSpec(memory_space=VM)
    sm = pl.BlockSpec(memory_space=pltpu.SMEM)
    hbm = pl.BlockSpec(memory_space=pl.ANY)
    edge = jax.ShapeDtypeStruct((3, (ng - mixed) * nj, LN), f32)
    return pl.pallas_call(
        functools.partial(pack_kernel, mixed=mixed, tiles=tiles),
        out_shape=(jax.ShapeDtypeStruct((ng, nj, rows, LN), bf), edge, edge)
        + (jax.ShapeDtypeStruct((hold // tiles, 2 * mixed, 16, LN), bf),) * tiles,
        in_specs=[sm, sm, hbm],
        out_specs=(hbm, vm, vm) + (hbm,) * tiles,
        scratch_shapes=[
            VM((nj, rows, per), bf),
            VM((ng, nj, rows, LN), bf),
            VM((hold, 2 * mixed, 16, LN), bf),
            pltpu.SMEM((hold + 1,), jnp.int32),
            pltpu.SemaphoreType.DMA((nj,)),
            pltpu.SemaphoreType.DMA((nj,)),
            pltpu.SemaphoreType.DMA((tiles,)),
        ],
        compiler_params=PARAMS,
        name="pack",
    )(pairs, place, x)


def mix_kernel(pairs, place, z_hbm, etop_ref, ebot_ref, w_ref, *rest, mixed, tiles):
    gots = rest[:tiles]
    out_hbm, otop_ref, obot_ref, zs, zp, got, wm, top_ref, bot_ref, count, zsem, gsem, osem = rest[tiles:]
    _, nj, rows, _ = zs.shape
    hold = got.shape[0]
    peer = hold // tiles
    of_tile = pairs.shape[1] // tiles
    ncb = nj // 2
    section, tile, band_at = place[0], place[1], place[2]

    gcopy = [pltpu.make_async_copy(gots[d], got.at[pl.ds(d * peer, peer)], gsem.at[d]) for d in range(tiles)]
    for c in gcopy:
        c.start()

    def zcopy(g):
        return pltpu.make_async_copy(z_hbm.at[g], zs.at[g], zsem.at[g])

    def ocopy(g):
        return pltpu.make_async_copy(zs.at[g], out_hbm.at[g], osem.at[g])

    for g in range(mixed):
        zcopy(g).start()
    block = lax.broadcasted_iota(jnp.int32, (LG, LN), 1) // LG

    @pl.loop(0, mixed)
    def _(g):
        for h in range(2):
            w = w_ref[g, h * LG:(h + 1) * LG, :]
            for c in range(PC):
                at = h * LN + c * LG
                wm[g, at:at + LG] = jnp.where(block == c, w, 0.0).astype(bf)
    for q in range(tiles):
        count[q] = 0
    for c in gcopy:
        c.wait()

    @pl.loop(0, hold)
    def _(slot):
        q, _ = part(pairs[section, tile * of_tile + band_at * hold + slot], of_tile)
        rank = count[q]
        count[q] = rank + 1
        at = lax.bitwise_xor(q, tile) * peer + rank
        up, side = part(slot, ncb)
        row = pl.ds(pl.multiple_of(up * 16, 16), 16)
        for g in range(mixed):
            for h in range(2):
                zp[g, 2 * side + h, row, :] = got[at, 2 * g + h]

    @pl.loop(0, mixed)
    def _(g):
        zcopy(g).wait()
        own = zs[g].reshape(nj * rows, LN)
        both = jnp.concatenate([own, zp[g].reshape(nj * rows, LN)], 1)
        new = own.astype(f32) + jnp.dot(both, wm[g], preferred_element_type=f32)
        new = new.astype(bf).reshape(nj, rows, LN)
        zs[g] = new
        ocopy(g).start()
        for j in range(nj):
            for r in range(3):
                top_ref[r, pl.ds(g * nj + j, 1), :] = new[j, r:r + 1].astype(f32)
                bot_ref[r, pl.ds(g * nj + j, 1), :] = new[j, rows - 3 + r:rows - 2 + r].astype(f32)

    top_ref[:, mixed * nj:, :] = etop_ref[...]
    bot_ref[:, mixed * nj:, :] = ebot_ref[...]
    otop_ref[...] = top_ref[...].astype(bf)
    obot_ref[...] = bot_ref[...].astype(bf)
    for g in range(mixed):
        ocopy(g).wait()


def mix(pairs, place, z, etop, ebot, w, gots):
    ng, nj, rows, _ = z.shape
    mixed = w.shape[0]
    tiles = len(gots)
    hold = gots[0].shape[0] * tiles
    vm = pl.BlockSpec(memory_space=VM)
    sm = pl.BlockSpec(memory_space=pltpu.SMEM)
    hbm = pl.BlockSpec(memory_space=pl.ANY)
    edge = jax.ShapeDtypeStruct((3, ng * nj, LN), bf)
    return pl.pallas_call(
        functools.partial(mix_kernel, mixed=mixed, tiles=tiles),
        out_shape=(jax.ShapeDtypeStruct((mixed, nj, rows, LN), bf), edge, edge),
        in_specs=[sm, sm, hbm, vm, vm, vm] + [hbm] * tiles,
        out_specs=(hbm, vm, vm),
        scratch_shapes=[
            VM((mixed, nj, rows, LN), bf),
            VM((mixed, nj, rows, LN), bf),
            VM((hold,) + gots[0].shape[1:], bf),
            VM((mixed, 2 * LN, LN), bf),
            VM(edge.shape, f32),
            VM(edge.shape, f32),
            pltpu.SMEM((tiles,), jnp.int32),
            pltpu.SemaphoreType.DMA((mixed,)),
            pltpu.SemaphoreType.DMA((tiles,)),
            pltpu.SemaphoreType.DMA((mixed,)),
        ],
        compiler_params=PARAMS,
        name="mix",
    )(pairs, place, z, etop, ebot, w, *gots)


def band_kernel(e_ref, w_ref):
    delta = lax.broadcasted_iota(jnp.int32, (LG, LN), 0) == lax.broadcasted_iota(jnp.int32, (LG, LN), 1) % LG
    chunk = lax.broadcasted_iota(jnp.int32, (8, LN), 1) // LG
    zero = jnp.zeros((LG, LN), bf)

    @pl.loop(0, e_ref.shape[0])
    def _(g):
        e = e_ref[g]
        w_ref[g, 0:256] = jnp.zeros((256, LN), bf)
        w_ref[g, 2048:2304] = jnp.zeros((256, LN), bf)
        for pos, jr in enumerate(list(range(12)) + list(range(-4, 0))):
            s = jr - 3
            r = lroll(e, s * LG)
            r = jnp.where((chunk >= s) & (chunk < 8 + s), r, 0.0)
            for k in range(7):
                row = (k + 1) * 256 + pos * LG
                if jr in (-4, 11):
                    w_ref[g, row:row + LG] = zero
                else:
                    w_ref[g, row:row + LG] = jnp.where(delta, jnp.broadcast_to(r[k:k + 1], (LG, LN)), 0.0).astype(bf)


def band(e):
    vm = pl.BlockSpec(memory_space=VM)
    n = e.shape[0]
    return pl.pallas_call(
        band_kernel,
        out_shape=jax.ShapeDtypeStruct((n, 2304, LN), bf),
        in_specs=[vm], out_specs=vm,
        compiler_params=PARAMS,
        name="band",
    )(e)


def block_kernel(*refs, parts, want_out, want_z):
    z_hbm, rest = refs[:parts], list(refs[parts:])
    top_ref, bot_ref, fac_ref, w_hbm, gain_ref, wi_hbm, woe_hbm, woo_hbm = rest[:8]
    rest = rest[8:]
    out_hbm = rest.pop(0) if want_out else None
    outz_hbm, otop_ref, obot_ref = (rest.pop(0) for _ in range(3)) if want_z else (None,) * 3
    zs, zf, lhs, wt, spr, ssum, nrm, xe, xo, upd, out, outz, wi_ref, woe_ref, woo_ref, tops, bots, zsem, wsem, osem, msem = rest
    ng, nj, rows, _ = zs.shape
    hr = rows // 2
    pad = 8
    count = ng * LG
    npair = xe.shape[0] // rows
    per = 3 * npair * LN

    def zcopy(g):
        src = z_hbm[0] if isinstance(g, int) and g < z_hbm[0].shape[0] else z_hbm[-1]
        return pltpu.make_async_copy(src.at[g], zs.at[g], zsem.at[g])

    def wcopy(g):
        return pltpu.make_async_copy(w_hbm.at[g], wt.at[g], wsem.at[g])

    for g in range(ng):
        zcopy(g).start()
        wcopy(g).start()
    weights = [pltpu.make_async_copy(a, b, msem.at[i])
               for i, (a, b) in enumerate(((wi_hbm, wi_ref), (woe_hbm, woe_ref), (woo_hbm, woo_ref)))]
    for c in weights:
        c.start()
    ssum[...] = jnp.zeros_like(ssum)

    @pl.loop(0, ng)
    def _(g):
        zcopy(g).wait()
        wcopy(g).wait()

        for j in range(nj):
            zf[j, pl.ds(pad, rows), :] = zs[g, j].astype(f32)
        for r in range(3):
            hs = pl.ds(pl.multiple_of(g * nj, nj), nj)
            zf[:, pad - 3 + r, :] = top_ref[r, hs, :].astype(f32)
            zf[:, pad + rows + r, :] = bot_ref[r, hs, :].astype(f32)
        m64 = lane_bit((hr, LN), 64)
        zero = jnp.zeros((hr, LN), bf)
        for a in range(8):
            v = [zf[j, pl.ds(pad - 3 + a, hr, stride=2), :].astype(bf) for j in range(nj)]
            for j in range(nj):
                nxt = v[j + 1] if j + 1 < nj else zero
                prv = v[j - 1] if j > 0 else zero
                lhs[j * hr:(j + 1) * hr, a * 256:a * 256 + LN] = v[j]
                lhs[j * hr:(j + 1) * hr, a * 256 + LN:a * 256 + 256] = jnp.where(m64, nxt, prv)

        rhs = jnp.concatenate([wt[g, 256:2304], wt[g, 0:2048]], 1)
        sp = jnp.dot(lhs[...], rhs, preferred_element_type=f32)
        spr[g] = sp
        ssum[...] += sp

    for c in weights:
        c.wait()
    ones = (lax.broadcasted_iota(jnp.int32, (256, 256), 0) // LG == lax.broadcasted_iota(jnp.int32, (256, 256), 1) // LG)
    ones = ones.astype(f32).astype(bf)

    def lane_mean(s):
        hi = s.astype(bf)
        lo = (s - hi.astype(f32)).astype(bf)
        return (jnp.dot(hi, ones, preferred_element_type=f32) + jnp.dot(lo, ones, preferred_element_type=f32)) * (1.0 / count)

    nrm[...] = lane_mean(ssum[...])

    @pl.loop(0, nj)
    def _(j):
        js = pl.ds(pl.multiple_of(j * hr, hr), hr)
        mean = nrm[js, :]
        q = jnp.zeros((hr, 256), f32)
        for g in range(ng):
            c = spr[g, js, :] - mean
            q = q + c * c
        ssum[js, :] = q
    ssum[...] = lax.rsqrt(lane_mean(ssum[...]) + 1e-06)

    def outcopy(j):
        ls = pl.ds(pl.multiple_of(j * per, LN), per)
        cs = []
        if want_out:
            cs.append(pltpu.make_async_copy(out.at[j], out_hbm.at[:, ls], osem.at[0, j]))
        if want_z:
            cs.append(pltpu.make_async_copy(outz.at[:, j], outz_hbm.at[:, j], osem.at[1, j]))
        return cs

    @pl.loop(0, nj)
    def _(j):
        js = pl.ds(pl.multiple_of(j * hr, hr), hr)

        mean, rstd = nrm[js, :], ssum[js, :]
        zz = [((spr[g, js, :] - mean) * rstd * gain_ref[g:g + 1, :]).astype(bf) for g in range(ng)]
        for p in range(2):
            nat = from_patch([t[:, p * LN:(p + 1) * LN] for t in zz])
            for i in range(npair):
                rs = slice(i * rows + p * hr, i * rows + (p + 1) * hr)
                xe[rs, :LN] = nat[3 * i]
                xe[rs, LN:] = nat[3 * i + 1]
                xo[rs, :LN] = nat[3 * i + 1]
                xo[rs, LN:] = nat[3 * i + 2]

        def mlp(x, wi, wo):
            h = gelu(jnp.dot(x, wi, preferred_element_type=f32).astype(bf))
            return jnp.dot(h, wo, preferred_element_type=f32)
        ue = mlp(xe[...], wi_ref[64:, :], woe_ref[...])
        uo = mlp(xo[...], wi_ref[:256, :], woo_ref[...])
        for i in range(npair):
            e = ue[i * rows:(i + 1) * rows]
            o = uo[i * rows:(i + 1) * rows]
            for t, val in enumerate((e[:, :LN], e[:, LN:] + o[:, :LN], o[:, LN:])):
                for p in range(2):
                    upd[3 * i + t, pl.ds(p, hr, stride=2), :] = val[p * hr:(p + 1) * hr]

        fac = fac_ref[0, 0]
        own = from_patch([zs[g, j] for g in range(ng)])
        res = []
        for n in range(3 * npair):
            y = (own[n].astype(f32) + fac * upd[n]).astype(bf)
            if want_out:
                out[j, :, n * LN:(n + 1) * LN] = y
            res.append(y)
        if want_z:
            for g, zz in enumerate(to_patch(res)):
                outz[g, j] = zz
                for r in range(3):
                    tops[r, pl.ds(g * nj + j, 1), :] = zz[r:r + 1].astype(f32)
                    bots[r, pl.ds(g * nj + j, 1), :] = zz[rows - 3 + r:rows - 2 + r].astype(f32)
        for c in outcopy(j):
            c.start()

    if want_z:
        otop_ref[...] = tops[...].astype(bf)
        obot_ref[...] = bots[...].astype(bf)

    @pl.loop(0, nj)
    def _(j):
        for c in outcopy(j):
            c.wait()


def block(zs, top, bot, fac, w, gain, wi, woe, woo, want_out=True, want_z=True):
    ng, nj, rows, _ = zs[-1].shape
    hr = rows // 2
    per = ng * LG * PC
    vm = pl.BlockSpec(memory_space=VM)
    hbm = pl.BlockSpec(memory_space=pl.ANY)
    shapes = []
    if want_out:
        shapes.append(jax.ShapeDtypeStruct((rows, nj * per), bf))
    if want_z:
        edge = jax.ShapeDtypeStruct(top.shape, bf)
        shapes += [jax.ShapeDtypeStruct((ng, nj, rows, LN), bf), edge, edge]
    return pl.pallas_call(
        functools.partial(block_kernel, parts=len(zs), want_out=want_out, want_z=want_z),
        out_shape=tuple(shapes),
        in_specs=[hbm] * len(zs) + [vm, vm, pl.BlockSpec(memory_space=pltpu.SMEM), hbm, vm, hbm, hbm, hbm],
        out_specs=((hbm,) if want_out else ()) + ((hbm, vm, vm) if want_z else ()),
        scratch_shapes=[
            VM((ng, nj, rows, LN), bf),
            VM((nj, rows + 16, LN), f32),
            VM((nj * hr, 2048), bf),
            VM((ng, 2304, LN), bf),
            VM((ng, nj * hr, 256), f32),
            VM((nj * hr, 256), f32),
            VM((nj * hr, 256), f32),
            VM((4 * rows, 256), bf), VM((4 * rows, 256), bf),
            VM((12, rows, LN), f32),
            VM((nj, rows, per), bf) if want_out else VM((8, LN), bf),
            VM((ng, nj, rows, LN), bf) if want_z else VM((8, LN), bf),
            VM(wi.shape, bf),
            VM(woe.shape, bf),
            VM(woo.shape, bf),
            VM(top.shape, f32),
            VM(top.shape, f32),
            pltpu.SemaphoreType.DMA((ng,)),
            pltpu.SemaphoreType.DMA((ng,)),
            pltpu.SemaphoreType.DMA((2, nj)),
            pltpu.SemaphoreType.DMA((3,)),
        ],
        compiler_params=PARAMS,
        name="block",
    )(*zs, top, bot, fac, w, gain, wi, woe, woo)


def prep_all(depth, gain, inner, outer):
    nl, c = gain.shape
    ng = c // LG
    e = jnp.pad(depth[:, :, ::-1, :], ((0, 0), (0, 1), (0, 1), (0, 0))).reshape(nl, 8, 8, ng, LG)
    e = e.transpose(0, 3, 1, 2, 4).reshape(nl, ng, 8, LN)
    gl = jnp.tile(gain.reshape(nl, ng, 1, LG), (1, 1, 16, 1)).reshape(nl, ng, 256)
    wi = jnp.pad(0.5 * inner, ((0, 0), (64, 64), (0, 0)))
    woe = jnp.pad(outer, ((0, 0), (0, 0), (0, 64)))
    woo = jnp.pad(outer, ((0, 0), (0, 0), (64, 0)))
    return e, gl, wi, woe, woo


def halo(top, bot):
    n = lax.axis_size("row")
    return (
        lax.ppermute(bot, "row", [(i, i + 1) for i in range(n - 1)]),
        lax.ppermute(top, "row", [(i + 1, i) for i in range(n - 1)]),
    )


def exchange(outs):
    n = len(outs)
    assert n & (n - 1) == 0
    return [
        lax.ppermute(o, ("comp", "tile"), [(s * n + t, (1 - s) * n + (t ^ d)) for s in range(2) for t in range(n)])
        for d, o in enumerate(outs)
    ]


def on_device(state, pairs, wet, mix_weight, depth_weight, norm_gain, inner_weight, outer_weight):
    assert state.shape[1] == 1
    section = lax.axis_index("comp")
    tiles = lax.axis_size("tile")
    place = jnp.stack([section, lax.axis_index("tile"), lax.axis_index("row")]).astype(jnp.int32)
    pick = lambda w, i: lax.dynamic_index_in_dim(w, i, 0, keepdims=False)
    z, etop, ebot, *outs = pack(pairs, place, state[0, 0], tiles, mix_weight.shape[1], norm_gain.shape[1] // LG)
    gots = exchange(outs)
    e, *weights = prep_all(depth_weight, norm_gain, inner_weight, outer_weight)
    which = jnp.where(section == 0, 0, 2)
    wmix = jnp.tile(pick(mix_weight, section).astype(f32), (1, 1, PC))
    wone, wtwo = band(pick(e, which)), band(e[1])
    zc, top, bot = mix(pairs, place, z, etop, ebot, wmix, gots)
    top, bot = halo(top, bot)
    factor = jnp.where(section == 0, 1.0, wet[0].astype(f32)).reshape(1, 1)
    _, z, top, bot = block([zc, z], top, bot, factor, wone, *(pick(w, which) for w in weights))
    top, bot = halo(top, bot)
    factor = jnp.where(section == 0, 1.0, 0.0).reshape(1, 1)
    out, = block([z], top, bot, factor, wtwo, *(w[1] for w in weights), want_z=False)
    return out[None, None]


def solution(mesh):
    return jax.shard_map(
        on_device,
        mesh=mesh,
        in_specs=(P("comp", "tile", "row", None), P(), P("tile"), P(), P(), P(), P(), P()),
        out_specs=P("comp", "tile", "row", None),
        check_vma=False,
    )
```

```python
import functools
import jax
import jax.numpy as jnp
from jax import lax
from jax.experimental import pallas as pl
from jax.experimental.pallas import tpu as pltpu
from jax.sharding import PartitionSpec as P

VM = pltpu.VMEM
PC = 8
LG = 16
LN = 128
bf, f32 = jnp.bfloat16, jnp.float32
AHEAD = 3
PARAMS = pltpu.CompilerParams(vmem_limit_bytes=56 * 2**20)


def lane_bit(shape, bit):
    return (lax.broadcasted_iota(jnp.int32, shape, 1) & bit) == 0


def lroll(x, shift):
    return pltpu.roll(x, shift % LN, 1)


def swap_stage(a, b, bit, m):
    return jnp.where(m, a, lroll(b, bit)), jnp.where(m, lroll(a, -bit), b)


def to_patch(v):
    half = len(v) // 2
    shape = v[0].shape
    m64, m32, m16 = (lane_bit(shape, b) for b in (64, 32, 16))
    per = 3
    u = {}
    for j in range(4):
        for t in range(per):
            q = per * j + t
            a, b = v[q // 2], v[q // 2 + half]
            if q % 2 == 0:
                u[j, t] = jnp.where(m64, a, lroll(b, 64))
            else:
                u[j, t] = jnp.where(m64, lroll(a, 64), b)
    out = []
    for t in range(per):
        a0, b0 = swap_stage(u[0, t], u[2, t], 32, m32)
        a1, b1 = swap_stage(u[1, t], u[3, t], 32, m32)
        out += swap_stage(a0, a1, 16, m16)
        out += swap_stage(b0, b1, 16, m16)
    return out


def from_patch(z):
    half = len(z) // 2
    shape = z[0].shape
    m64, m32, m16 = (lane_bit(shape, b) for b in (64, 32, 16))
    per = len(z) // 4
    u = {}
    for t in range(per):
        a0, a1 = swap_stage(z[4 * t], z[4 * t + 1], 16, m16)
        b0, b1 = swap_stage(z[4 * t + 2], z[4 * t + 3], 16, m16)
        u[0, t], u[2, t] = swap_stage(a0, b0, 32, m32)
        u[1, t], u[3, t] = swap_stage(a1, b1, 32, m32)
    lo, hi = {}, {}
    for j in range(4):
        for t in range(per):
            q = per * j + t
            lo[q] = u[j, t]
            hi[q] = u[j, t]
    v = []
    for n in range(half):
        e, o = u[divmod(2 * n, per)], u[divmod(2 * n + 1, per)]
        v.append(jnp.where(m64, e, lroll(o, 64)))
    for n in range(half):
        e, o = u[divmod(2 * n, per)], u[divmod(2 * n + 1, per)]
        v.append(jnp.where(m64, lroll(e, 64), o))
    return v


def gelu(h):
    c = 0.7978845608028654
    inside = h * (jnp.asarray(2 * c, bf) + jnp.asarray(8 * 0.044715 * c, bf) * (h * h))
    return h + h * jnp.tanh(inside)


def part(i, n):
    if n & (n - 1) == 0:
        return lax.shift_right_logical(i, n.bit_length() - 1), i & (n - 1)
    return lax.div(i, n), lax.rem(i, n)


def pack_kernel(pairs, place, x_hbm, z_hbm, top_ref, bot_ref, *rest, mixed, tiles):
    outs = rest[:tiles]
    xs, zs, send, order, xsem, zsem, ssem = rest[tiles:]
    ng, nj, rows, _ = zs.shape
    per = x_hbm.shape[1] // nj
    hold = send.shape[0]
    peer = hold // tiles
    of_tile = pairs.shape[1] // tiles
    ncb = nj // 2
    section, tile, band_at = place[0], place[1], place[2]

    def xcopy(j):
        return pltpu.make_async_copy(x_hbm.at[:, pl.ds(pl.multiple_of(j * per, LN), per)], xs.at[j], xsem.at[j])

    def zcopy(j):
        return pltpu.make_async_copy(zs.at[:, j], z_hbm.at[:, j], zsem.at[j])

    for j in range(nj):
        xcopy(j).start()

    @pl.loop(0, tiles)
    def _(q):
        first = lax.bitwise_xor(q, tile) * peer

        def one(slot, rank):
            src_tile, src = part(pairs[1 - section, q * of_tile + band_at * hold + slot], of_tile)
            mine = src_tile == tile
            order[jnp.where(mine, first + rank, hold)] = src - band_at * hold
            return rank + mine.astype(jnp.int32)
        lax.fori_loop(0, hold, one, jnp.int32(0), unroll=8)

    @pl.loop(0, nj)
    def _(j):
        xcopy(j).wait()
        zz = to_patch([xs[j, :, n * LN:(n + 1) * LN] for n in range(12)])
        for g in range(ng):
            zs[g, j] = zz[g]
        for g in range(mixed, ng):
            for r in range(3):
                top_ref[r, pl.ds((g - mixed) * nj + j, 1), :] = zz[g][r:r + 1].astype(f32)
                bot_ref[r, pl.ds((g - mixed) * nj + j, 1), :] = zz[g][rows - 3 + r:rows - 2 + r].astype(f32)
        zcopy(j).start()

    @pl.loop(0, hold)
    def _(at):
        up, side = part(order[at], ncb)
        row = pl.ds(pl.multiple_of(up * 16, 16), 16)
        for g in range(mixed):
            for h in range(2):
                send[at, 2 * g + h] = zs[g, 2 * side + h, row, :]

    copies = [pltpu.make_async_copy(send.at[pl.ds(d * peer, peer)], outs[d], ssem.at[d]) for d in range(tiles)]
    for c in copies:
        c.start()
    for c in copies:
        c.wait()
    for j in range(nj):
        zcopy(j).wait()


def pack(pairs, place, x, tiles, mixed, ng):
    rows, width = x.shape
    per = ng * LG * PC
    nj = width // per
    hold = rows // 16 * (nj // 2)
    vm = pl.BlockSpec(memory_space=VM)
    sm = pl.BlockSpec(memory_space=pltpu.SMEM)
    hbm = pl.BlockSpec(memory_space=pl.ANY)
    edge = jax.ShapeDtypeStruct((3, (ng - mixed) * nj, LN), f32)
    return pl.pallas_call(
        functools.partial(pack_kernel, mixed=mixed, tiles=tiles),
        out_shape=(jax.ShapeDtypeStruct((ng, nj, rows, LN), bf), edge, edge)
        + (jax.ShapeDtypeStruct((hold // tiles, 2 * mixed, 16, LN), bf),) * tiles,
        in_specs=[sm, sm, hbm],
        out_specs=(hbm, vm, vm) + (hbm,) * tiles,
        scratch_shapes=[
            VM((nj, rows, per), bf),
            VM((ng, nj, rows, LN), bf),
            VM((hold, 2 * mixed, 16, LN), bf),
            pltpu.SMEM((hold + 1,), jnp.int32),
            pltpu.SemaphoreType.DMA((nj,)),
            pltpu.SemaphoreType.DMA((nj,)),
            pltpu.SemaphoreType.DMA((tiles,)),
        ],
        compiler_params=PARAMS,
        name="pack",
    )(pairs, place, x)


def mix_kernel(pairs, place, z_hbm, *rest, mixed, tiles, edges):
    w_ref, *rest = rest
    gots, rest = rest[:tiles], rest[tiles:]
    if edges:
        etop_ref, ebot_ref, otop_ref, obot_ref, top_ref, bot_ref, *rest = rest
    else:
        out_hbm, *rest = rest
    zs, zp, got, wm, count, zsem, gsem, osem = rest
    _, nj, rows, _ = zs.shape
    whole = z_hbm.shape[2]
    hold = got.shape[0]
    peer = hold // tiles
    of_tile = pairs.shape[1] // tiles
    ncb = nj // 2
    section, tile, band_at = place[0], place[1], place[2]

    gcopy = [pltpu.make_async_copy(gots[d], got.at[pl.ds(d * peer, peer)], gsem.at[d]) for d in range(tiles)]
    for c in gcopy:
        c.start()

    def zcopy(g):
        if not edges:
            return [pltpu.make_async_copy(z_hbm.at[g], zs.at[g], zsem.at[g, 0])]
        return [
            pltpu.make_async_copy(z_hbm.at[g, :, pl.ds(at, 16), :], zs.at[g, :, pl.ds(n * 16, 16), :], zsem.at[g, n])
            for n, at in enumerate((0, whole - 16))
        ]

    def ocopy(g):
        return pltpu.make_async_copy(zs.at[g], out_hbm.at[g], osem.at[g])

    for g in range(mixed):
        for c in zcopy(g):
            c.start()
    block = lax.broadcasted_iota(jnp.int32, (LG, LN), 1) // LG

    @pl.loop(0, mixed)
    def _(g):
        for h in range(2):
            w = w_ref[g, h * LG:(h + 1) * LG, :]
            for c in range(PC):
                at = h * LN + c * LG
                wm[g, at:at + LG] = jnp.where(block == c, w, 0.0).astype(bf)
    for q in range(tiles):
        count[q] = 0
    for c in gcopy:
        c.wait()

    @pl.loop(0, hold)
    def _(slot):
        q, _ = part(pairs[section, tile * of_tile + band_at * hold + slot], of_tile)
        rank = count[q]
        count[q] = rank + 1
        at = lax.bitwise_xor(q, tile) * peer + rank
        up, side = part(slot, ncb)

        def put(up):
            row = pl.ds(pl.multiple_of(up * 16, 16), 16)
            for g in range(mixed):
                for h in range(2):
                    zp[g, 2 * side + h, row, :] = got[at, 2 * g + h]
        if edges:
            pl.when(up == 0)(lambda: put(0))
            pl.when(up == whole // 16 - 1)(lambda: put(1))
        else:
            put(up)

    @pl.loop(0, mixed)
    def _(g):
        for c in zcopy(g):
            c.wait()
        own = zs[g].reshape(nj * rows, LN)
        both = jnp.concatenate([own, zp[g].reshape(nj * rows, LN)], 1)
        new = own.astype(f32) + jnp.dot(both, wm[g], preferred_element_type=f32)
        new = new.astype(bf).reshape(nj, rows, LN)
        if not edges:
            zs[g] = new
            ocopy(g).start()
            return
        for j in range(nj):
            for r in range(3):
                top_ref[r, pl.ds(g * nj + j, 1), :] = new[j, r:r + 1].astype(f32)
                bot_ref[r, pl.ds(g * nj + j, 1), :] = new[j, rows - 3 + r:rows - 2 + r].astype(f32)

    if edges:
        top_ref[:, mixed * nj:, :] = etop_ref[...]
        bot_ref[:, mixed * nj:, :] = ebot_ref[...]
        otop_ref[...] = top_ref[...].astype(bf)
        obot_ref[...] = bot_ref[...].astype(bf)
    else:
        for g in range(mixed):
            ocopy(g).wait()


def mix(pairs, place, z, w, gots, ends=()):
    ng, nj, rows, _ = z.shape
    edges = len(ends) > 0
    mixed = w.shape[0]
    tiles = len(gots)
    hold = gots[0].shape[0] * tiles
    vm = pl.BlockSpec(memory_space=VM)
    sm = pl.BlockSpec(memory_space=pltpu.SMEM)
    hbm = pl.BlockSpec(memory_space=pl.ANY)
    edge = jax.ShapeDtypeStruct((3, ng * nj, LN), bf)
    here = 32 if edges else rows
    return pl.pallas_call(
        functools.partial(mix_kernel, mixed=mixed, tiles=tiles, edges=edges),
        out_shape=(edge, edge) if edges else jax.ShapeDtypeStruct((mixed, nj, rows, LN), bf),
        in_specs=[sm, sm, hbm, vm] + [hbm] * tiles + [vm] * len(ends),
        out_specs=(vm, vm) if edges else hbm,
        scratch_shapes=([VM(edge.shape, f32)] * 2 if edges else []) + [
            VM((mixed, nj, here, LN), bf),
            VM((mixed, nj, here, LN), bf),
            VM((hold,) + gots[0].shape[1:], bf),
            VM((mixed, 2 * LN, LN), bf),
            pltpu.SMEM((tiles,), jnp.int32),
            pltpu.SemaphoreType.DMA((mixed, 2)),
            pltpu.SemaphoreType.DMA((tiles,)),
            pltpu.SemaphoreType.DMA((mixed,)),
        ],
        compiler_params=PARAMS,
        cost_estimate=pl.CostEstimate(flops=10**9, bytes_accessed=2**23, transcendentals=0),
        name="mix_edges" if edges else "mix",
    )(pairs, place, z, w, *gots, *ends)


def band_kernel(e_ref, w_ref):
    delta = lax.broadcasted_iota(jnp.int32, (LG, LN), 0) == lax.broadcasted_iota(jnp.int32, (LG, LN), 1) % LG
    chunk = lax.broadcasted_iota(jnp.int32, (8, LN), 1) // LG
    zero = jnp.zeros((LG, LN), bf)

    @pl.loop(0, e_ref.shape[0])
    def _(g):
        e = e_ref[g]
        for pos, jr in enumerate(list(range(12)) + list(range(-4, 0))):
            s = jr - 3
            r = lroll(e, s * LG)
            r = jnp.where((chunk >= s) & (chunk < 8 + s), r, 0.0)
            for k in range(7):
                row = k * 256 + pos * LG
                if jr in (-4, 11):
                    w_ref[g, row:row + LG] = zero
                else:
                    w_ref[g, row:row + LG] = jnp.where(delta, jnp.broadcast_to(r[k:k + 1], (LG, LN)), 0.0).astype(bf)


def band(e):
    vm = pl.BlockSpec(memory_space=VM)
    n = e.shape[0]
    return pl.pallas_call(
        band_kernel,
        out_shape=jax.ShapeDtypeStruct((n, 1792, LN), bf),
        in_specs=[vm], out_specs=vm,
        cost_estimate=pl.CostEstimate(flops=10**9, bytes_accessed=n * 1792 * LN * 4, transcendentals=0),
        compiler_params=PARAMS,
        name="band",
    )(e)


def block_kernel(*refs, parts, layer, want_out, want_z):
    z_hbm, rest = refs[:parts], list(refs[parts:])
    top_ref, bot_ref, fac_ref, w_hbm, gain_ref, wi_hbm, woe_hbm, woo_hbm = rest[:8]
    rest = rest[8:]
    out_hbm = rest.pop(0) if want_out else None
    outz_hbm, otop_ref, obot_ref = (rest.pop(0) for _ in range(3)) if want_z else (None,) * 3
    zs, zf, lhs, wt, spr, ssum, nrm, xe, xo, upd, out, outz, wi_ref, woe_ref, woo_ref, tops, bots, zsem, wsem, osem, msem = rest
    ng, nj, rows, _ = zs.shape
    hr = rows // 2
    pad = 8
    count = ng * LG
    npair = xe.shape[0] // rows
    per = 3 * npair * LN

    def zcopy(g, source):
        return pltpu.make_async_copy(source.at[g], zs.at[g], zsem.at[g])

    def wcopy(g):
        return pltpu.make_async_copy(w_hbm.at[layer * ng + g], wt.at[g], wsem.at[g])

    def fetch(g):
        for n, source in enumerate(z_hbm):
            inside = g < z_hbm[0].shape[0]
            if len(z_hbm) > 1:
                pl.when(inside if n == 0 else jnp.logical_not(inside))(zcopy(g, source).start)
            else:
                zcopy(g, source).start()
        wcopy(g).start()

    for g in range(AHEAD):
        fetch(jnp.int32(g))
    weights = [pltpu.make_async_copy(a, b, msem.at[i])
               for i, (a, b) in enumerate(((wi_hbm, wi_ref), (woe_hbm, woe_ref), (woo_hbm, woo_ref)))]
    ssum[...] = jnp.zeros_like(ssum)

    @pl.loop(0, ng)
    def _(g):
        pl.when(g + AHEAD < ng)(lambda: fetch(g + AHEAD))

        @pl.when(g == ng // 2)
        def _():
            for c in weights:
                c.start()
        zcopy(g, z_hbm[-1]).wait()
        wcopy(g).wait()

        for j in range(nj):
            zf[j, pl.ds(pad, rows), :] = zs[g, j].astype(f32)
        for r in range(3):
            hs = pl.ds(pl.multiple_of(g * nj, nj), nj)
            zf[:, pad - 3 + r, :] = top_ref[r, hs, :].astype(f32)
            zf[:, pad + rows + r, :] = bot_ref[r, hs, :].astype(f32)
        m64 = lane_bit((hr, LN), 64)
        zero = jnp.zeros((hr, LN), bf)
        for a in range(8):
            v = [zf[j, pl.ds(pad - 3 + a, hr, stride=2), :].astype(bf) for j in range(nj)]
            for j in range(nj):
                nxt = v[j + 1] if j + 1 < nj else zero
                prv = v[j - 1] if j > 0 else zero
                lhs[j * hr:(j + 1) * hr, a * 256:a * 256 + LN] = v[j]
                lhs[j * hr:(j + 1) * hr, a * 256 + LN:a * 256 + 256] = jnp.where(m64, nxt, prv)

        band_g, zero_g = wt[g], jnp.zeros((256, LN), bf)
        rhs = jnp.concatenate([jnp.concatenate([band_g, zero_g], 0), jnp.concatenate([zero_g, band_g], 0)], 1)
        sp = jnp.dot(lhs[...], rhs, preferred_element_type=f32)
        spr[g] = sp
        ssum[...] += sp

    for c in weights:
        c.wait()
    ones = (lax.broadcasted_iota(jnp.int32, (256, 256), 0) // LG == lax.broadcasted_iota(jnp.int32, (256, 256), 1) // LG)
    ones = ones.astype(f32).astype(bf)

    def lane_mean(s):
        hi = s.astype(bf)
        lo = (s - hi.astype(f32)).astype(bf)
        return (jnp.dot(hi, ones, preferred_element_type=f32) + jnp.dot(lo, ones, preferred_element_type=f32)) * (1.0 / count)

    nrm[...] = lane_mean(ssum[...])

    @pl.loop(0, nj)
    def _(j):
        js = pl.ds(pl.multiple_of(j * hr, hr), hr)
        mean = nrm[js, :]
        q = jnp.zeros((hr, 256), f32)
        for g in range(ng):
            c = spr[g, js, :] - mean
            q = q + c * c
        ssum[js, :] = q
    ssum[...] = lax.rsqrt(lane_mean(ssum[...]) + 1e-06)

    def outcopy(j):
        ls = pl.ds(pl.multiple_of(j * per, LN), per)
        cs = []
        if want_out:
            cs.append(pltpu.make_async_copy(out.at[j], out_hbm.at[:, ls], osem.at[0, j]))
        if want_z:
            cs.append(pltpu.make_async_copy(outz.at[:, j], outz_hbm.at[:, j], osem.at[1, j]))
        return cs

    @pl.loop(0, nj)
    def _(j):
        js = pl.ds(pl.multiple_of(j * hr, hr), hr)

        mean, rstd = nrm[js, :], ssum[js, :]
        zz = [((spr[g, js, :] - mean) * rstd * gain_ref[g:g + 1, :]).astype(bf) for g in range(ng)]
        for p in range(2):
            nat = from_patch([t[:, p * LN:(p + 1) * LN] for t in zz])
            for i in range(npair):
                rs = slice(i * rows + p * hr, i * rows + (p + 1) * hr)
                xe[rs, :LN] = nat[3 * i]
                xe[rs, LN:] = nat[3 * i + 1]
                xo[rs, :LN] = nat[3 * i + 1]
                xo[rs, LN:] = nat[3 * i + 2]

        def mlp(x, wi, wo):
            h = gelu(jnp.dot(x, wi, preferred_element_type=f32).astype(bf))
            return jnp.dot(h, wo, preferred_element_type=f32)
        ue = mlp(xe[...], wi_ref[64:, :], woe_ref[...])
        uo = mlp(xo[...], wi_ref[:256, :], woo_ref[...])
        for i in range(npair):
            e = ue[i * rows:(i + 1) * rows]
            o = uo[i * rows:(i + 1) * rows]
            for t, val in enumerate((e[:, :LN], e[:, LN:] + o[:, :LN], o[:, LN:])):
                for p in range(2):
                    upd[3 * i + t, pl.ds(p, hr, stride=2), :] = val[p * hr:(p + 1) * hr]

        fac = fac_ref[0, 0]
        if want_out:
            own = from_patch([zs[g, j] for g in range(ng)])
            for n in range(3 * npair):
                out[j, :, n * LN:(n + 1) * LN] = (own[n].astype(f32) + fac * upd[n]).astype(bf)
        if want_z:
            for g, part_of in enumerate(to_patch([(fac * upd[n]).astype(bf) for n in range(3 * npair)])):
                zz = (zs[g, j].astype(f32) + part_of.astype(f32)).astype(bf)
                outz[g, j] = zz
                for r in range(3):
                    tops[r, pl.ds(g * nj + j, 1), :] = zz[r:r + 1].astype(f32)
                    bots[r, pl.ds(g * nj + j, 1), :] = zz[rows - 3 + r:rows - 2 + r].astype(f32)
        for c in outcopy(j):
            c.start()

    if want_z:
        otop_ref[...] = tops[...].astype(bf)
        obot_ref[...] = bots[...].astype(bf)

    @pl.loop(0, nj)
    def _(j):
        for c in outcopy(j):
            c.wait()


def block(zs, top, bot, fac, w, gain, wi, woe, woo, layer=0, want_out=True, want_z=True):
    ng, nj, rows, _ = zs[-1].shape
    hr = rows // 2
    per = ng * LG * PC
    vm = pl.BlockSpec(memory_space=VM)
    hbm = pl.BlockSpec(memory_space=pl.ANY)
    shapes = []
    if want_out:
        shapes.append(jax.ShapeDtypeStruct((rows, nj * per), bf))
    if want_z:
        edge = jax.ShapeDtypeStruct(top.shape, bf)
        shapes += [jax.ShapeDtypeStruct((ng, nj, rows, LN), bf), edge, edge]
    return pl.pallas_call(
        functools.partial(block_kernel, parts=len(zs), layer=layer, want_out=want_out, want_z=want_z),
        out_shape=tuple(shapes),
        in_specs=[hbm] * len(zs) + [vm, vm, pl.BlockSpec(memory_space=pltpu.SMEM), hbm, vm, hbm, hbm, hbm],
        out_specs=((hbm,) if want_out else ()) + ((hbm, vm, vm) if want_z else ()),
        scratch_shapes=[
            VM((ng, nj, rows, LN), bf),
            VM((nj, rows + 16, LN), f32),
            VM((nj * hr, 2048), bf),
            VM((ng, 1792, LN), bf),
            VM((ng, nj * hr, 256), f32),
            VM((nj * hr, 256), f32),
            VM((nj * hr, 256), f32),
            VM((4 * rows, 256), bf), VM((4 * rows, 256), bf),
            VM((12, rows, LN), f32),
            VM((nj, rows, per), bf) if want_out else VM((8, LN), bf),
            VM((ng, nj, rows, LN), bf) if want_z else VM((8, LN), bf),
            VM(wi.shape, bf),
            VM(woe.shape, bf),
            VM(woo.shape, bf),
            VM(top.shape, f32),
            VM(top.shape, f32),
            pltpu.SemaphoreType.DMA((ng,)),
            pltpu.SemaphoreType.DMA((ng,)),
            pltpu.SemaphoreType.DMA((2, nj)),
            pltpu.SemaphoreType.DMA((3,)),
        ],
        compiler_params=PARAMS,
        name="block",
    )(*zs, top, bot, fac, w, gain, wi, woe, woo)


def prep_all(depth, gain, inner, outer):
    nl, c = gain.shape
    ng = c // LG
    e = jnp.pad(depth[:, :, ::-1, :], ((0, 0), (0, 1), (0, 1), (0, 0))).reshape(nl, 8, 8, ng, LG)
    e = e.transpose(0, 3, 1, 2, 4).reshape(nl, ng, 8, LN)
    gl = jnp.tile(gain.reshape(nl, ng, 1, LG), (1, 1, 16, 1)).reshape(nl, ng, 256)
    wi = jnp.pad(0.5 * inner, ((0, 0), (64, 64), (0, 0)))
    woe = jnp.pad(outer, ((0, 0), (0, 0), (0, 64)))
    woo = jnp.pad(outer, ((0, 0), (0, 0), (64, 0)))
    return e, gl, wi, woe, woo


def halo(top, bot):
    n = lax.axis_size("row")
    return (
        lax.ppermute(bot, "row", [(i, i + 1) for i in range(n - 1)]),
        lax.ppermute(top, "row", [(i + 1, i) for i in range(n - 1)]),
    )


def exchange(outs):
    n = len(outs)
    assert n & (n - 1) == 0
    return [
        lax.ppermute(o, ("comp", "tile"), [(s * n + t, (1 - s) * n + (t ^ d)) for s in range(2) for t in range(n)])
        for d, o in enumerate(outs)
    ]


def on_device(state, pairs, wet, mix_weight, depth_weight, norm_gain, inner_weight, outer_weight):
    assert state.shape[1] == 1
    section = lax.axis_index("comp")
    tiles = lax.axis_size("tile")
    place = jnp.stack([section, lax.axis_index("tile"), lax.axis_index("row")]).astype(jnp.int32)
    pick = lambda w, i: lax.dynamic_index_in_dim(w, i, 0, keepdims=False)
    z, etop, ebot, *outs = pack(pairs, place, state[0, 0], tiles, mix_weight.shape[1], norm_gain.shape[1] // LG)
    gots = exchange(outs)
    e, *weights = prep_all(depth_weight, norm_gain, inner_weight, outer_weight)
    which = jnp.where(section == 0, 0, 2)
    wmix = jnp.tile(pick(mix_weight, section).astype(f32), (1, 1, PC))
    bands = band(jnp.concatenate([pick(e, which), e[1]]))
    gots, bands = lax.optimization_barrier((gots, bands))
    top, bot = halo(*mix(pairs, place, z, wmix, gots, (etop, ebot)))
    zc = mix(pairs, place, z, wmix, gots)
    factor = jnp.where(section == 0, 1.0, wet[0].astype(f32)).reshape(1, 1)
    z, top, bot = block([zc, z], top, bot, factor, bands, *(pick(w, which) for w in weights), want_out=False)
    top, bot = halo(top, bot)
    factor = jnp.where(section == 0, 1.0, 0.0).reshape(1, 1)
    out, = block([z], top, bot, factor, bands, *(w[1] for w in weights), layer=1, want_z=False)
    return out[None, None]


def solution(mesh):
    return jax.shard_map(
        on_device,
        mesh=mesh,
        in_specs=(P("comp", "tile", "row", None), P(), P("tile"), P(), P(), P(), P(), P()),
        out_specs=P("comp", "tile", "row", None),
        check_vma=False,
    )
```

```python
import functools
import jax
import jax.numpy as jnp
from jax import lax
from jax.experimental import pallas as pl
from jax.experimental.pallas import tpu as pltpu
from jax.sharding import PartitionSpec as P

VM = pltpu.VMEM
PC = 8
LG = 16
LN = 128
bf, f32 = jnp.bfloat16, jnp.float32
HALO = 3
AHEAD = 3
PARAMS = pltpu.CompilerParams(vmem_limit_bytes=56 * 2**20)


def lane_bit(shape, bit):
    return (lax.broadcasted_iota(jnp.int32, shape, 1) & bit) == 0


def lroll(x, shift):
    return pltpu.roll(x, shift % LN, 1)


def swap_stage(a, b, bit, m):
    return jnp.where(m, a, lroll(b, bit)), jnp.where(m, lroll(a, -bit), b)


def to_patch(v):
    half = len(v) // 2
    shape = v[0].shape
    m64, m32, m16 = (lane_bit(shape, b) for b in (64, 32, 16))
    per = 3
    u = {}
    for j in range(4):
        for t in range(per):
            q = per * j + t
            a, b = v[q // 2], v[q // 2 + half]
            if q % 2 == 0:
                u[j, t] = jnp.where(m64, a, lroll(b, 64))
            else:
                u[j, t] = jnp.where(m64, lroll(a, 64), b)
    out = []
    for t in range(per):
        a0, b0 = swap_stage(u[0, t], u[2, t], 32, m32)
        a1, b1 = swap_stage(u[1, t], u[3, t], 32, m32)
        out += swap_stage(a0, a1, 16, m16)
        out += swap_stage(b0, b1, 16, m16)
    return out


def from_patch(z):
    half = len(z) // 2
    shape = z[0].shape
    m64, m32, m16 = (lane_bit(shape, b) for b in (64, 32, 16))
    per = len(z) // 4
    u = {}
    for t in range(per):
        a0, a1 = swap_stage(z[4 * t], z[4 * t + 1], 16, m16)
        b0, b1 = swap_stage(z[4 * t + 2], z[4 * t + 3], 16, m16)
        u[0, t], u[2, t] = swap_stage(a0, b0, 32, m32)
        u[1, t], u[3, t] = swap_stage(a1, b1, 32, m32)
    lo, hi = {}, {}
    for j in range(4):
        for t in range(per):
            q = per * j + t
            lo[q] = u[j, t]
            hi[q] = u[j, t]
    v = []
    for n in range(half):
        e, o = u[divmod(2 * n, per)], u[divmod(2 * n + 1, per)]
        v.append(jnp.where(m64, e, lroll(o, 64)))
    for n in range(half):
        e, o = u[divmod(2 * n, per)], u[divmod(2 * n + 1, per)]
        v.append(jnp.where(m64, lroll(e, 64), o))
    return v


def gelu(h):
    c = 0.7978845608028654
    inside = h * (jnp.asarray(2 * c, bf) + jnp.asarray(8 * 0.044715 * c, bf) * (h * h))
    return h + h * jnp.tanh(inside)


def part(i, n):
    if n & (n - 1) == 0:
        return lax.shift_right_logical(i, n.bit_length() - 1), i & (n - 1)
    return lax.div(i, n), lax.rem(i, n)


def pack_kernel(pairs, place, x_hbm, z_hbm, top_ref, bot_ref, *rest, mixed, tiles):
    outs = rest[:tiles]
    xs, zs, send, order, xsem, zsem, ssem = rest[tiles:]
    ng, nj, rows, _ = zs.shape
    per = x_hbm.shape[1] // nj
    hold = send.shape[0]
    peer = hold // tiles
    of_tile = pairs.shape[1] // tiles
    ncb = nj // 2
    section, tile, band_at = place[0], place[1], place[2]

    def xcopy(j):
        return pltpu.make_async_copy(x_hbm.at[:, pl.ds(pl.multiple_of(j * per, LN), per)], xs.at[j], xsem.at[j])

    def zcopy(j):
        return pltpu.make_async_copy(zs.at[:, j], z_hbm.at[:, j], zsem.at[j])

    for j in range(nj):
        xcopy(j).start()

    @pl.loop(0, tiles)
    def _(q):
        first = lax.bitwise_xor(q, tile) * peer

        def one(slot, rank):
            src_tile, src = part(pairs[1 - section, q * of_tile + band_at * hold + slot], of_tile)
            mine = src_tile == tile
            order[jnp.where(mine, first + rank, hold)] = src - band_at * hold
            return rank + mine.astype(jnp.int32)
        lax.fori_loop(0, hold, one, jnp.int32(0), unroll=8)

    @pl.loop(0, nj)
    def _(j):
        xcopy(j).wait()
        zz = to_patch([xs[j, :, n * LN:(n + 1) * LN] for n in range(12)])
        for g in range(ng):
            zs[g, j] = zz[g]
        for g in range(mixed, ng):
            for r in range(2 * HALO):
                top_ref[r, pl.ds((g - mixed) * nj + j, 1), :] = zz[g][r:r + 1].astype(f32)
                bot_ref[r, pl.ds((g - mixed) * nj + j, 1), :] = zz[g][rows - 2 * HALO + r:rows - 2 * HALO + r + 1].astype(f32)
        zcopy(j).start()

    @pl.loop(0, hold)
    def _(at):
        up, side = part(order[at], ncb)
        row = pl.ds(pl.multiple_of(up * 16, 16), 16)
        for g in range(mixed):
            for h in range(2):
                send[at, 2 * g + h] = zs[g, 2 * side + h, row, :]

    copies = [pltpu.make_async_copy(send.at[pl.ds(d * peer, peer)], outs[d], ssem.at[d]) for d in range(tiles)]
    for c in copies:
        c.start()
    for c in copies:
        c.wait()
    for j in range(nj):
        zcopy(j).wait()


def pack(pairs, place, x, tiles, mixed, ng):
    rows, width = x.shape
    per = ng * LG * PC
    nj = width // per
    hold = rows // 16 * (nj // 2)
    vm = pl.BlockSpec(memory_space=VM)
    sm = pl.BlockSpec(memory_space=pltpu.SMEM)
    hbm = pl.BlockSpec(memory_space=pl.ANY)
    edge = jax.ShapeDtypeStruct((2 * HALO, (ng - mixed) * nj, LN), f32)
    return pl.pallas_call(
        functools.partial(pack_kernel, mixed=mixed, tiles=tiles),
        out_shape=(jax.ShapeDtypeStruct((ng, nj, rows, LN), bf), edge, edge)
        + (jax.ShapeDtypeStruct((hold // tiles, 2 * mixed, 16, LN), bf),) * tiles,
        in_specs=[sm, sm, hbm],
        out_specs=(hbm, vm, vm) + (hbm,) * tiles,
        scratch_shapes=[
            VM((nj, rows, per), bf),
            VM((ng, nj, rows, LN), bf),
            VM((hold, 2 * mixed, 16, LN), bf),
            pltpu.SMEM((hold + 1,), jnp.int32),
            pltpu.SemaphoreType.DMA((nj,)),
            pltpu.SemaphoreType.DMA((nj,)),
            pltpu.SemaphoreType.DMA((tiles,)),
        ],
        compiler_params=PARAMS,
        name="pack",
    )(pairs, place, x)


def mix_kernel(pairs, place, z_hbm, *rest, mixed, tiles, edges):
    w_ref, *rest = rest
    gots, rest = rest[:tiles], rest[tiles:]
    if edges:
        etop_ref, ebot_ref, otop_ref, obot_ref, top_ref, bot_ref, *rest = rest
    else:
        out_hbm, *rest = rest
    zs, zp, got, wm, count, zsem, gsem, osem = rest
    _, nj, rows, _ = zs.shape
    whole = z_hbm.shape[2]
    hold = got.shape[0]
    peer = hold // tiles
    of_tile = pairs.shape[1] // tiles
    ncb = nj // 2
    section, tile, band_at = place[0], place[1], place[2]

    gcopy = [pltpu.make_async_copy(gots[d], got.at[pl.ds(d * peer, peer)], gsem.at[d]) for d in range(tiles)]
    for c in gcopy:
        c.start()

    def zcopy(g):
        if not edges:
            return [pltpu.make_async_copy(z_hbm.at[g], zs.at[g], zsem.at[g, 0])]
        return [
            pltpu.make_async_copy(z_hbm.at[g, :, pl.ds(at, 16), :], zs.at[g, :, pl.ds(n * 16, 16), :], zsem.at[g, n])
            for n, at in enumerate((0, whole - 16))
        ]

    def ocopy(g):
        return pltpu.make_async_copy(zs.at[g], out_hbm.at[g], osem.at[g])

    for g in range(mixed):
        for c in zcopy(g):
            c.start()
    block = lax.broadcasted_iota(jnp.int32, (LG, LN), 1) // LG

    @pl.loop(0, mixed)
    def _(g):
        for h in range(2):
            w = w_ref[g, h * LG:(h + 1) * LG, :]
            for c in range(PC):
                at = h * LN + c * LG
                wm[g, at:at + LG] = jnp.where(block == c, w, 0.0).astype(bf)
    for q in range(tiles):
        count[q] = 0
    for c in gcopy:
        c.wait()

    @pl.loop(0, hold)
    def _(slot):
        q, _ = part(pairs[section, tile * of_tile + band_at * hold + slot], of_tile)
        rank = count[q]
        count[q] = rank + 1
        at = lax.bitwise_xor(q, tile) * peer + rank
        up, side = part(slot, ncb)

        def put(up):
            row = pl.ds(pl.multiple_of(up * 16, 16), 16)
            for g in range(mixed):
                for h in range(2):
                    zp[g, 2 * side + h, row, :] = got[at, 2 * g + h]
        if edges:
            pl.when(up == 0)(lambda: put(0))
            pl.when(up == whole // 16 - 1)(lambda: put(1))
        else:
            put(up)

    @pl.loop(0, mixed)
    def _(g):
        for c in zcopy(g):
            c.wait()
        own = zs[g].reshape(nj * rows, LN)
        both = jnp.concatenate([own, zp[g].reshape(nj * rows, LN)], 1)
        new = own.astype(f32) + jnp.dot(both, wm[g], preferred_element_type=f32)
        new = new.astype(bf).reshape(nj, rows, LN)
        if not edges:
            zs[g] = new
            ocopy(g).start()
            return
        for j in range(nj):
            for r in range(2 * HALO):
                low = rows - 2 * HALO + r
                top_ref[r, pl.ds(g * nj + j, 1), :] = new[j, r:r + 1].astype(f32)
                bot_ref[r, pl.ds(g * nj + j, 1), :] = new[j, low:low + 1].astype(f32)

    if edges:
        top_ref[:, mixed * nj:, :] = etop_ref[...]
        bot_ref[:, mixed * nj:, :] = ebot_ref[...]
        otop_ref[...] = top_ref[...].astype(bf)
        obot_ref[...] = bot_ref[...].astype(bf)
    else:
        for g in range(mixed):
            ocopy(g).wait()


def mix(pairs, place, z, w, gots, ends=()):
    ng, nj, rows, _ = z.shape
    edges = len(ends) > 0
    mixed = w.shape[0]
    tiles = len(gots)
    hold = gots[0].shape[0] * tiles
    vm = pl.BlockSpec(memory_space=VM)
    sm = pl.BlockSpec(memory_space=pltpu.SMEM)
    hbm = pl.BlockSpec(memory_space=pl.ANY)
    edge = jax.ShapeDtypeStruct((2 * HALO, ng * nj, LN), bf)
    here = 32 if edges else rows
    return pl.pallas_call(
        functools.partial(mix_kernel, mixed=mixed, tiles=tiles, edges=edges),
        out_shape=(edge, edge) if edges else jax.ShapeDtypeStruct((mixed, nj, rows, LN), bf),
        in_specs=[sm, sm, hbm, vm] + [hbm] * tiles + [vm] * len(ends),
        out_specs=(vm, vm) if edges else hbm,
        scratch_shapes=([VM(edge.shape, f32)] * 2 if edges else []) + [
            VM((mixed, nj, here, LN), bf),
            VM((mixed, nj, here, LN), bf),
            VM((hold,) + gots[0].shape[1:], bf),
            VM((mixed, 2 * LN, LN), bf),
            pltpu.SMEM((tiles,), jnp.int32),
            pltpu.SemaphoreType.DMA((mixed, 2)),
            pltpu.SemaphoreType.DMA((tiles,)),
            pltpu.SemaphoreType.DMA((mixed,)),
        ],
        compiler_params=PARAMS,
        cost_estimate=pl.CostEstimate(flops=10**9, bytes_accessed=2**23, transcendentals=0),
        name="mix_edges" if edges else "mix",
    )(pairs, place, z, w, *gots, *ends)


def band_kernel(e_ref, w_ref):
    delta = lax.broadcasted_iota(jnp.int32, (LG, LN), 0) == lax.broadcasted_iota(jnp.int32, (LG, LN), 1) % LG
    chunk = lax.broadcasted_iota(jnp.int32, (8, LN), 1) // LG
    zero = jnp.zeros((LG, LN), bf)

    @pl.loop(0, e_ref.shape[0])
    def _(g):
        e = e_ref[g]
        for pos, jr in enumerate(list(range(12)) + list(range(-4, 0))):
            s = jr - 3
            r = lroll(e, s * LG)
            r = jnp.where((chunk >= s) & (chunk < 8 + s), r, 0.0)
            for k in range(7):
                row = k * 256 + pos * LG
                if jr in (-4, 11):
                    w_ref[g, row:row + LG] = zero
                else:
                    w_ref[g, row:row + LG] = jnp.where(delta, jnp.broadcast_to(r[k:k + 1], (LG, LN)), 0.0).astype(bf)


def band(e):
    vm = pl.BlockSpec(memory_space=VM)
    n = e.shape[0]
    return pl.pallas_call(
        band_kernel,
        out_shape=jax.ShapeDtypeStruct((n, 1792, LN), bf),
        in_specs=[vm], out_specs=vm,
        cost_estimate=pl.CostEstimate(flops=10**9, bytes_accessed=n * 1792 * LN * 4, transcendentals=0),
        compiler_params=PARAMS,
        name="band",
    )(e)


def block_kernel(*refs, parts, layer, want_out, want_z):
    z_hbm, rest = refs[:parts], list(refs[parts:])
    top_ref, bot_ref, fac_ref, w_hbm, gain_ref, wi_hbm, woe_hbm, woo_hbm = rest[:8]
    rest = rest[8:]
    out_hbm = rest.pop(0) if want_out else None
    outz_hbm, otop_ref, obot_ref = (rest.pop(0) for _ in range(3)) if want_z else (None,) * 3
    zs, zf, lhs, wt, spr, ssum, nrm, upd, out, outz, wi_ref, woe_ref, woo_ref, tops, bots, zsem, wsem, osem, msem = rest
    ng, nj, rows, _ = zs.shape
    hr = rows // 2
    pad = 8
    have = top_ref.shape[0]
    extra = have > HALO
    ends = (-2, -1, hr, hr + 1)
    beyond = slice(nj * hr, nj * hr + 4 * nj)
    count = ng * LG
    npair = PC // 2
    per = 3 * npair * LN

    def zcopy(g, source):
        return pltpu.make_async_copy(source.at[g], zs.at[g], zsem.at[g])

    def wcopy(g):
        return pltpu.make_async_copy(w_hbm.at[layer * ng + g], wt.at[g], wsem.at[g])

    def fetch(g):
        for n, source in enumerate(z_hbm):
            inside = g < z_hbm[0].shape[0]
            if len(z_hbm) > 1:
                pl.when(inside if n == 0 else jnp.logical_not(inside))(zcopy(g, source).start)
            else:
                zcopy(g, source).start()
        wcopy(g).start()

    for g in range(AHEAD):
        fetch(jnp.int32(g))
    weights = [pltpu.make_async_copy(a, b, msem.at[i])
               for i, (a, b) in enumerate(((wi_hbm, wi_ref), (woe_hbm, woe_ref), (woo_hbm, woo_ref)))]
    ssum[...] = jnp.zeros_like(ssum)

    @pl.loop(0, ng)
    def _(g):
        pl.when(g + AHEAD < ng)(lambda: fetch(g + AHEAD))

        @pl.when(g == ng // 2)
        def _():
            for c in weights:
                c.start()
        zcopy(g, z_hbm[-1]).wait()
        wcopy(g).wait()

        for j in range(nj):
            zf[j, pl.ds(pad, rows), :] = zs[g, j].astype(f32)
        for r in range(3):
            hs = pl.ds(pl.multiple_of(g * nj, nj), nj)
            zf[:, pad - 3 + r, :] = top_ref[have - 3 + r, hs, :].astype(f32)
            zf[:, pad + rows + r, :] = bot_ref[r, hs, :].astype(f32)
        m64 = lane_bit((hr, LN), 64)
        zero = jnp.zeros((hr, LN), bf)
        for a in range(8):
            v = [zf[j, pl.ds(pad - 3 + a, hr, stride=2), :].astype(bf) for j in range(nj)]
            for j in range(nj):
                nxt = v[j + 1] if j + 1 < nj else zero
                prv = v[j - 1] if j > 0 else zero
                lhs[j * hr:(j + 1) * hr, a * 256:a * 256 + LN] = v[j]
                lhs[j * hr:(j + 1) * hr, a * 256 + LN:a * 256 + 256] = jnp.where(m64, nxt, prv)

        if extra:
            m64 = lane_bit((nj, LN), 64)
            sub = lax.broadcasted_iota(jnp.int32, (nj, LN), 0)
            got = {}

            def row_of(at):
                if at not in got:
                    if 0 <= at < rows:
                        v = zf[:, pad + at, :]
                    elif -have <= at < 0:
                        v = top_ref[at + have, hs, :].astype(f32)
                    elif rows <= at < rows + have:
                        v = bot_ref[at - rows, hs, :].astype(f32)
                    else:
                        v = jnp.zeros((nj, LN), f32)
                    nxt = jnp.where(sub < nj - 1, pltpu.roll(v, nj - 1, 0), 0.0)
                    prv = jnp.where(sub > 0, pltpu.roll(v, 1, 0), 0.0)
                    got[at] = v, jnp.where(m64, nxt, prv)
                return got[at]
            for a in range(8):
                for n in range(2):
                    v = jnp.concatenate([row_of(2 * r - 3 + a)[n] for r in ends], 0).astype(bf)
                    lhs[beyond, a * 256 + n * LN:a * 256 + (n + 1) * LN] = v
        band_g, zero_g = wt[g], jnp.zeros((256, LN), bf)
        rhs = jnp.concatenate([jnp.concatenate([band_g, zero_g], 0), jnp.concatenate([zero_g, band_g], 0)], 1)
        sp = jnp.dot(lhs[...], rhs, preferred_element_type=f32)
        spr[g] = sp
        ssum[...] += sp

    for c in weights:
        c.wait()
    ones = (lax.broadcasted_iota(jnp.int32, (256, 256), 0) // LG == lax.broadcasted_iota(jnp.int32, (256, 256), 1) // LG)
    ones = ones.astype(f32).astype(bf)

    def lane_mean(s):
        hi = s.astype(bf)
        lo = (s - hi.astype(f32)).astype(bf)
        return (jnp.dot(hi, ones, preferred_element_type=f32) + jnp.dot(lo, ones, preferred_element_type=f32)) * (1.0 / count)

    nrm[...] = lane_mean(ssum[...])

    @pl.loop(0, ssum.shape[0] // 32)
    def _(n):
        rs = pl.ds(pl.multiple_of(n * 32, 32), 32)
        mean = nrm[rs, :]
        q = jnp.zeros((32, 256), f32)
        for g in range(ng):
            c = spr[g, rs, :] - mean
            q = q + c * c
        ssum[rs, :] = q
    ssum[...] = lax.rsqrt(lane_mean(ssum[...]) + 1e-06)

    def outcopy(j):
        ls = pl.ds(pl.multiple_of(j * per, LN), per)
        cs = []
        if want_out:
            cs.append(pltpu.make_async_copy(out.at[j], out_hbm.at[:, ls], osem.at[0, j]))
        if want_z:
            cs.append(pltpu.make_async_copy(outz.at[:, j], outz_hbm.at[:, j], osem.at[1, j]))
        return cs

    fac = fac_ref[0, 0]

    def update(js):
        mean, rstd = nrm[js, :], ssum[js, :]
        zz = [((spr[g, js, :] - mean) * rstd * gain_ref[g:g + 1, :]).astype(bf) for g in range(ng)]
        nat = [from_patch([t[:, p * LN:(p + 1) * LN] for t in zz]) for p in range(2)]
        nat = [jnp.concatenate([a, b], 0) for a, b in zip(*nat)]
        many = nat[0].shape[0]
        xe = jnp.concatenate([jnp.concatenate([nat[3 * i], nat[3 * i + 1]], 1) for i in range(npair)], 0)
        xo = jnp.concatenate([jnp.concatenate([nat[3 * i + 1], nat[3 * i + 2]], 1) for i in range(npair)], 0)

        def mlp(x, wi, wo):
            h = gelu(jnp.dot(x, wi, preferred_element_type=f32).astype(bf))
            return jnp.dot(h, wo, preferred_element_type=f32)
        ue = mlp(xe, wi_ref[64:, :], woe_ref[...])
        uo = mlp(xo, wi_ref[:256, :], woo_ref[...])
        res = []
        for i in range(npair):
            e, o = ue[i * many:(i + 1) * many], uo[i * many:(i + 1) * many]
            res += [e[:, :LN], e[:, LN:] + o[:, :LN], o[:, LN:]]
        return res

    @pl.loop(0, nj)
    def _(j):
        for n, val in enumerate(update(pl.ds(pl.multiple_of(j * hr, hr), hr))):
            for p in range(2):
                upd[n, pl.ds(p, hr, stride=2), :] = val[p * hr:(p + 1) * hr]
        if want_out:
            own = from_patch([zs[g, j] for g in range(ng)])
            for n in range(3 * npair):
                out[j, :, n * LN:(n + 1) * LN] = (own[n].astype(f32) + fac * upd[n]).astype(bf)
        if want_z:
            for g, part_of in enumerate(to_patch([(fac * upd[n]).astype(bf) for n in range(3 * npair)])):
                zz = (zs[g, j].astype(f32) + part_of.astype(f32)).astype(bf)
                outz[g, j] = zz
        for c in outcopy(j):
            c.start()

    if extra:
        more = to_patch([(fac * val).astype(bf) for val in update(pl.ds(nj * hr, 4 * nj))])
        for g in range(ng):
            gs = pl.ds(g * nj, nj)
            for r in range(HALO):
                for at, keep, own, to in ((r - HALO, 1, top_ref[have - HALO + r, gs, :], tops), (rows + r, 2, bot_ref[r, gs, :], bots)):
                    n = at % 2 * 4 * nj + ends.index(at // 2) * nj
                    to[r, gs, :] = fac_ref[0, keep] * (own.astype(f32) + more[g][n:n + nj].astype(f32))
        otop_ref[...] = tops[...].astype(bf)
        obot_ref[...] = bots[...].astype(bf)

    @pl.loop(0, nj)
    def _(j):
        for c in outcopy(j):
            c.wait()


def block(zs, top, bot, fac, w, gain, wi, woe, woo, layer=0, want_out=True, want_z=True):
    ng, nj, rows, _ = zs[-1].shape
    hr = rows // 2
    many = nj * hr + (4 * nj if want_z else 0)
    assert want_z == (top.shape[0] == 2 * HALO)
    per = ng * LG * PC
    vm = pl.BlockSpec(memory_space=VM)
    hbm = pl.BlockSpec(memory_space=pl.ANY)
    shapes = []
    if want_out:
        shapes.append(jax.ShapeDtypeStruct((rows, nj * per), bf))
    if want_z:
        edge = jax.ShapeDtypeStruct((HALO,) + top.shape[1:], bf)
        shapes += [jax.ShapeDtypeStruct((ng, nj, rows, LN), bf), edge, edge]
    return pl.pallas_call(
        functools.partial(block_kernel, parts=len(zs), layer=layer, want_out=want_out, want_z=want_z),
        out_shape=tuple(shapes),
        in_specs=[hbm] * len(zs) + [vm, vm, pl.BlockSpec(memory_space=pltpu.SMEM), hbm, vm, hbm, hbm, hbm],
        out_specs=((hbm,) if want_out else ()) + ((hbm, vm, vm) if want_z else ()),
        scratch_shapes=[
            VM((ng, nj, rows, LN), bf),
            VM((nj, rows + 16, LN), f32),
            VM((many, 2048), bf),
            VM((ng, 1792, LN), bf),
            VM((ng, many, 256), f32),
            VM((many, 256), f32),
            VM((many, 256), f32),
            VM((12, rows, LN), f32),
            VM((nj, rows, per), bf) if want_out else VM((8, LN), bf),
            VM((ng, nj, rows, LN), bf) if want_z else VM((8, LN), bf),
            VM(wi.shape, bf),
            VM(woe.shape, bf),
            VM(woo.shape, bf),
            VM((HALO,) + top.shape[1:], f32),
            VM((HALO,) + top.shape[1:], f32),
            pltpu.SemaphoreType.DMA((ng,)),
            pltpu.SemaphoreType.DMA((ng,)),
            pltpu.SemaphoreType.DMA((2, nj)),
            pltpu.SemaphoreType.DMA((3,)),
        ],
        compiler_params=PARAMS,
        name="block",
    )(*zs, top, bot, fac, w, gain, wi, woe, woo)


def prep_all(depth, gain, inner, outer):
    nl, c = gain.shape
    ng = c // LG
    e = jnp.pad(depth[:, :, ::-1, :], ((0, 0), (0, 1), (0, 1), (0, 0))).reshape(nl, 8, 8, ng, LG)
    e = e.transpose(0, 3, 1, 2, 4).reshape(nl, ng, 8, LN)
    gl = jnp.tile(gain.reshape(nl, ng, 1, LG), (1, 1, 16, 1)).reshape(nl, ng, 256)
    wi = jnp.pad(0.5 * inner, ((0, 0), (64, 64), (0, 0)))
    woe = jnp.pad(outer, ((0, 0), (0, 0), (0, 64)))
    woo = jnp.pad(outer, ((0, 0), (0, 0), (64, 0)))
    return e, gl, wi, woe, woo


def halo(top, bot):
    n = lax.axis_size("row")
    return (
        lax.ppermute(bot, "row", [(i, i + 1) for i in range(n - 1)]),
        lax.ppermute(top, "row", [(i + 1, i) for i in range(n - 1)]),
    )


def exchange(outs):
    n = len(outs)
    assert n & (n - 1) == 0
    return [
        lax.ppermute(o, ("comp", "tile"), [(s * n + t, (1 - s) * n + (t ^ d)) for s in range(2) for t in range(n)])
        for d, o in enumerate(outs)
    ]


def on_device(state, pairs, wet, mix_weight, depth_weight, norm_gain, inner_weight, outer_weight):
    assert state.shape[1] == 1
    section = lax.axis_index("comp")
    tiles = lax.axis_size("tile")
    place = jnp.stack([section, lax.axis_index("tile"), lax.axis_index("row")]).astype(jnp.int32)
    pick = lambda w, i: lax.dynamic_index_in_dim(w, i, 0, keepdims=False)
    z, etop, ebot, *outs = pack(pairs, place, state[0, 0], tiles, mix_weight.shape[1], norm_gain.shape[1] // LG)
    gots = exchange(outs)
    e, *weights = prep_all(depth_weight, norm_gain, inner_weight, outer_weight)
    which = jnp.where(section == 0, 0, 2)
    wmix = jnp.tile(pick(mix_weight, section).astype(f32), (1, 1, PC))
    bands = band(jnp.concatenate([pick(e, which), e[1]]))
    gots, bands = lax.optimization_barrier((gots, bands))
    top, bot = halo(*mix(pairs, place, z, wmix, gots, (etop, ebot)))
    zc = mix(pairs, place, z, wmix, gots)
    factor = jnp.where(section == 0, 1.0, wet[0].astype(f32))
    inside = jnp.stack([place[2] > 0, place[2] < lax.axis_size("row") - 1]).astype(f32)
    factors = jnp.concatenate([factor.reshape(1, 1), inside.reshape(1, 2)], 1)
    z, top, bot = block([zc, z], top, bot, factors, bands, *(pick(w, which) for w in weights), want_out=False)
    factor = jnp.where(section == 0, 1.0, 0.0).reshape(1, 1)
    out, = block([z], top, bot, factor, bands, *(w[1] for w in weights), layer=1, want_z=False)
    return out[None, None]


def solution(mesh):
    return jax.shard_map(
        on_device,
        mesh=mesh,
        in_specs=(P("comp", "tile", "row", None), P(), P("tile"), P(), P(), P(), P(), P()),
        out_specs=P("comp", "tile", "row", None),
        check_vma=False,
    )
```

```python
import functools
import jax
import jax.numpy as jnp
from jax import lax
from jax.experimental import pallas as pl
from jax.experimental.pallas import tpu as pltpu
from jax.sharding import PartitionSpec as P

VM = pltpu.VMEM
PC = 8
LG = 16
LN = 128
bf, f32 = jnp.bfloat16, jnp.float32
HALO = 3
AHEAD = 3
PARAMS = pltpu.CompilerParams(vmem_limit_bytes=56 * 2**20)


def lane_bit(shape, bit):
    return (lax.broadcasted_iota(jnp.int32, shape, 1) & bit) == 0


def lroll(x, shift):
    return pltpu.roll(x, shift % LN, 1)


def swap_stage(a, b, bit, m):
    return jnp.where(m, a, lroll(b, bit)), jnp.where(m, lroll(a, -bit), b)


def to_patch(v):
    half = len(v) // 2
    shape = v[0].shape
    m64, m32, m16 = (lane_bit(shape, b) for b in (64, 32, 16))
    per = 3
    u = {}
    for j in range(4):
        for t in range(per):
            q = per * j + t
            a, b = v[q // 2], v[q // 2 + half]
            if q % 2 == 0:
                u[j, t] = jnp.where(m64, a, lroll(b, 64))
            else:
                u[j, t] = jnp.where(m64, lroll(a, 64), b)
    out = []
    for t in range(per):
        a0, b0 = swap_stage(u[0, t], u[2, t], 32, m32)
        a1, b1 = swap_stage(u[1, t], u[3, t], 32, m32)
        out += swap_stage(a0, a1, 16, m16)
        out += swap_stage(b0, b1, 16, m16)
    return out


def from_patch(z):
    half = len(z) // 2
    shape = z[0].shape
    m64, m32, m16 = (lane_bit(shape, b) for b in (64, 32, 16))
    per = len(z) // 4
    u = {}
    for t in range(per):
        a0, a1 = swap_stage(z[4 * t], z[4 * t + 1], 16, m16)
        b0, b1 = swap_stage(z[4 * t + 2], z[4 * t + 3], 16, m16)
        u[0, t], u[2, t] = swap_stage(a0, b0, 32, m32)
        u[1, t], u[3, t] = swap_stage(a1, b1, 32, m32)
    lo, hi = {}, {}
    for j in range(4):
        for t in range(per):
            q = per * j + t
            lo[q] = u[j, t]
            hi[q] = u[j, t]
    v = []
    for n in range(half):
        e, o = u[divmod(2 * n, per)], u[divmod(2 * n + 1, per)]
        v.append(jnp.where(m64, e, lroll(o, 64)))
    for n in range(half):
        e, o = u[divmod(2 * n, per)], u[divmod(2 * n + 1, per)]
        v.append(jnp.where(m64, lroll(e, 64), o))
    return v


def gelu(h):
    c = 0.7978845608028654
    inside = h * (jnp.asarray(2 * c, bf) + jnp.asarray(8 * 0.044715 * c, bf) * (h * h))
    return h + h * jnp.tanh(inside)


def part(i, n):
    if n & (n - 1) == 0:
        return lax.shift_right_logical(i, n.bit_length() - 1), i & (n - 1)
    return lax.div(i, n), lax.rem(i, n)


def pack_kernel(pairs, place, x_hbm, z_hbm, top_ref, bot_ref, *rest, mixed, tiles):
    outs = rest[:tiles]
    xs, zs, send, order, xsem, zsem, ssem = rest[tiles:]
    ng, nj, rows, _ = zs.shape
    per = x_hbm.shape[1] // nj
    hold = send.shape[0]
    peer = hold // tiles
    of_tile = pairs.shape[1] // tiles
    ncb = nj // 2
    section, tile, band_at = place[0], place[1], place[2]

    def xcopy(j):
        return pltpu.make_async_copy(x_hbm.at[:, pl.ds(pl.multiple_of(j * per, LN), per)], xs.at[j], xsem.at[j])

    def zcopy(j):
        return pltpu.make_async_copy(zs.at[:, j], z_hbm.at[:, j], zsem.at[j])

    for j in range(nj):
        xcopy(j).start()

    @pl.loop(0, tiles)
    def _(q):
        first = lax.bitwise_xor(q, tile) * peer

        def one(slot, rank):
            src_tile, src = part(pairs[1 - section, q * of_tile + band_at * hold + slot], of_tile)
            mine = src_tile == tile
            order[jnp.where(mine, first + rank, hold)] = src - band_at * hold
            return rank + mine.astype(jnp.int32)
        lax.fori_loop(0, hold, one, jnp.int32(0), unroll=8)

    @pl.loop(0, nj)
    def _(j):
        xcopy(j).wait()
        zz = to_patch([xs[j, :, n * LN:(n + 1) * LN] for n in range(12)])
        for g in range(ng):
            zs[g, j] = zz[g]
        for g in range(mixed, ng):
            for r in range(2 * HALO):
                top_ref[r, pl.ds((g - mixed) * nj + j, 1), :] = zz[g][r:r + 1].astype(f32)
                bot_ref[r, pl.ds((g - mixed) * nj + j, 1), :] = zz[g][rows - 2 * HALO + r:rows - 2 * HALO + r + 1].astype(f32)
        zcopy(j).start()

    @pl.loop(0, hold)
    def _(at):
        up, side = part(order[at], ncb)
        row = pl.ds(pl.multiple_of(up * 16, 16), 16)
        for g in range(mixed):
            for h in range(2):
                send[at, 2 * g + h] = zs[g, 2 * side + h, row, :]

    copies = [pltpu.make_async_copy(send.at[pl.ds(d * peer, peer)], outs[d], ssem.at[d]) for d in range(tiles)]
    for c in copies:
        c.start()
    for c in copies:
        c.wait()
    for j in range(nj):
        zcopy(j).wait()


def pack(pairs, place, x, tiles, mixed, ng):
    rows, width = x.shape
    per = ng * LG * PC
    nj = width // per
    hold = rows // 16 * (nj // 2)
    vm = pl.BlockSpec(memory_space=VM)
    sm = pl.BlockSpec(memory_space=pltpu.SMEM)
    hbm = pl.BlockSpec(memory_space=pl.ANY)
    edge = jax.ShapeDtypeStruct((2 * HALO, (ng - mixed) * nj, LN), f32)
    return pl.pallas_call(
        functools.partial(pack_kernel, mixed=mixed, tiles=tiles),
        out_shape=(jax.ShapeDtypeStruct((ng, nj, rows, LN), bf), edge, edge)
        + (jax.ShapeDtypeStruct((hold // tiles, 2 * mixed, 16, LN), bf),) * tiles,
        in_specs=[sm, sm, hbm],
        out_specs=(hbm, vm, vm) + (hbm,) * tiles,
        scratch_shapes=[
            VM((nj, rows, per), bf),
            VM((ng, nj, rows, LN), bf),
            VM((hold, 2 * mixed, 16, LN), bf),
            pltpu.SMEM((hold + 1,), jnp.int32),
            pltpu.SemaphoreType.DMA((nj,)),
            pltpu.SemaphoreType.DMA((nj,)),
            pltpu.SemaphoreType.DMA((tiles,)),
        ],
        compiler_params=PARAMS,
        name="pack",
    )(pairs, place, x)


def mix_kernel(pairs, place, z_hbm, *rest, mixed, tiles, edges):
    w_ref, *rest = rest
    gots, rest = rest[:tiles], rest[tiles:]
    if edges:
        etop_ref, ebot_ref, otop_ref, obot_ref, top_ref, bot_ref, *rest = rest
    else:
        out_hbm, *rest = rest
    zs, zp, got, wm, count, zsem, gsem, osem = rest
    _, nj, rows, _ = zs.shape
    whole = z_hbm.shape[2]
    hold = got.shape[0]
    peer = hold // tiles
    of_tile = pairs.shape[1] // tiles
    ncb = nj // 2
    section, tile, band_at = place[0], place[1], place[2]

    gcopy = [pltpu.make_async_copy(gots[d], got.at[pl.ds(d * peer, peer)], gsem.at[d]) for d in range(tiles)]
    for c in gcopy:
        c.start()

    def zcopy(g):
        if not edges:
            return [pltpu.make_async_copy(z_hbm.at[g], zs.at[g], zsem.at[g, 0])]
        return [
            pltpu.make_async_copy(z_hbm.at[g, :, pl.ds(at, 16), :], zs.at[g, :, pl.ds(n * 16, 16), :], zsem.at[g, n])
            for n, at in enumerate((0, whole - 16))
        ]

    def ocopy(g):
        return pltpu.make_async_copy(zs.at[g], out_hbm.at[g], osem.at[g])

    for g in range(mixed):
        for c in zcopy(g):
            c.start()
    block = lax.broadcasted_iota(jnp.int32, (LG, LN), 1) // LG

    @pl.loop(0, mixed)
    def _(g):
        for h in range(2):
            w = w_ref[g, h * LG:(h + 1) * LG, :]
            for c in range(PC):
                at = h * LN + c * LG
                wm[g, at:at + LG] = jnp.where(block == c, w, 0.0).astype(bf)
    for q in range(tiles):
        count[q] = 0
    for c in gcopy:
        c.wait()

    @pl.loop(0, hold)
    def _(slot):
        q, _ = part(pairs[section, tile * of_tile + band_at * hold + slot], of_tile)
        rank = count[q]
        count[q] = rank + 1
        at = lax.bitwise_xor(q, tile) * peer + rank
        up, side = part(slot, ncb)

        def put(up):
            row = pl.ds(pl.multiple_of(up * 16, 16), 16)
            for g in range(mixed):
                for h in range(2):
                    zp[g, 2 * side + h, row, :] = got[at, 2 * g + h]
        if edges:
            pl.when(up == 0)(lambda: put(0))
            pl.when(up == whole // 16 - 1)(lambda: put(1))
        else:
            put(up)

    @pl.loop(0, mixed)
    def _(g):
        for c in zcopy(g):
            c.wait()
        own = zs[g].reshape(nj * rows, LN)
        both = jnp.concatenate([own, zp[g].reshape(nj * rows, LN)], 1)
        new = own.astype(f32) + jnp.dot(both, wm[g], preferred_element_type=f32)
        new = new.astype(bf).reshape(nj, rows, LN)
        if not edges:
            zs[g] = new
            ocopy(g).start()
            return
        for j in range(nj):
            for r in range(2 * HALO):
                low = rows - 2 * HALO + r
                top_ref[r, pl.ds(g * nj + j, 1), :] = new[j, r:r + 1].astype(f32)
                bot_ref[r, pl.ds(g * nj + j, 1), :] = new[j, low:low + 1].astype(f32)

    if edges:
        top_ref[:, mixed * nj:, :] = etop_ref[...]
        bot_ref[:, mixed * nj:, :] = ebot_ref[...]
        otop_ref[...] = top_ref[...].astype(bf)
        obot_ref[...] = bot_ref[...].astype(bf)
    else:
        for g in range(mixed):
            ocopy(g).wait()


def mix(pairs, place, z, w, gots, ends=()):
    ng, nj, rows, _ = z.shape
    edges = len(ends) > 0
    mixed = w.shape[0]
    tiles = len(gots)
    hold = gots[0].shape[0] * tiles
    vm = pl.BlockSpec(memory_space=VM)
    sm = pl.BlockSpec(memory_space=pltpu.SMEM)
    hbm = pl.BlockSpec(memory_space=pl.ANY)
    edge = jax.ShapeDtypeStruct((2 * HALO, ng * nj, LN), bf)
    here = 32 if edges else rows
    return pl.pallas_call(
        functools.partial(mix_kernel, mixed=mixed, tiles=tiles, edges=edges),
        out_shape=(edge, edge) if edges else jax.ShapeDtypeStruct((mixed, nj, rows, LN), bf),
        in_specs=[sm, sm, hbm, vm] + [hbm] * tiles + [vm] * len(ends),
        out_specs=(vm, vm) if edges else hbm,
        scratch_shapes=([VM(edge.shape, f32)] * 2 if edges else []) + [
            VM((mixed, nj, here, LN), bf),
            VM((mixed, nj, here, LN), bf),
            VM((hold,) + gots[0].shape[1:], bf),
            VM((mixed, 2 * LN, LN), bf),
            pltpu.SMEM((tiles,), jnp.int32),
            pltpu.SemaphoreType.DMA((mixed, 2)),
            pltpu.SemaphoreType.DMA((tiles,)),
            pltpu.SemaphoreType.DMA((mixed,)),
        ],
        compiler_params=PARAMS,
        cost_estimate=pl.CostEstimate(flops=10**9, bytes_accessed=2**23, transcendentals=0),
        name="mix_edges" if edges else "mix",
    )(pairs, place, z, w, *gots, *ends)


def band_kernel(place, e_ref, w_ref):
    delta = lax.broadcasted_iota(jnp.int32, (LG, LN), 0) == lax.broadcasted_iota(jnp.int32, (LG, LN), 1) % LG
    chunk = lax.broadcasted_iota(jnp.int32, (8, LN), 1) // LG
    zero = jnp.zeros((LG, LN), bf)

    ng = e_ref.shape[1]
    first = jnp.where(place[0] == 0, 0, 2)

    @pl.loop(0, 2 * ng)
    def _(g):
        e = e_ref[jnp.where(g < ng, first, 1), jnp.where(g < ng, g, g - ng)]
        for pos, jr in enumerate(list(range(12)) + list(range(-4, 0))):
            s = jr - 3
            r = lroll(e, s * LG)
            r = jnp.where((chunk >= s) & (chunk < 8 + s), r, 0.0)
            for k in range(7):
                row = k * 256 + pos * LG
                if jr in (-4, 11):
                    w_ref[g, row:row + LG] = zero
                else:
                    w_ref[g, row:row + LG] = jnp.where(delta, jnp.broadcast_to(r[k:k + 1], (LG, LN)), 0.0).astype(bf)


def band(place, e):
    vm = pl.BlockSpec(memory_space=VM)
    n = 2 * e.shape[1]
    return pl.pallas_call(
        band_kernel,
        out_shape=jax.ShapeDtypeStruct((n, 1792, LN), bf),
        in_specs=[pl.BlockSpec(memory_space=pltpu.SMEM), vm], out_specs=vm,
        cost_estimate=pl.CostEstimate(flops=10**9, bytes_accessed=n * 1792 * LN * 4, transcendentals=0),
        compiler_params=PARAMS,
        name="band",
    )(place, e)


def blocks_kernel(place, fac_ref, zc_hbm, z_hbm, top_ref, bot_ref, w_hbm, gain_ref, wi_hbm, woe_hbm, woo_hbm, out_hbm,
                  zs, zn, zf, lhs, wt, spr, ssum, nrm, upd, out, wi_ref, woe_ref, woo_ref, tops, bots, zsem, wsem, osem, msem):
    ng, nj, rows, _ = zs.shape
    hr = rows // 2
    pad = 8
    ends = (-2, -1, hr, hr + 1)
    count = ng * LG
    npair = PC // 2
    per = 3 * npair * LN
    mixed = zc_hbm.shape[0]
    which = jnp.where(place[0] == 0, 0, 2), 1

    def zcopy(g, source):
        return pltpu.make_async_copy(source.at[g], zs.at[g], zsem.at[g])

    def wcopy(g, layer):
        return pltpu.make_async_copy(w_hbm.at[layer * ng + g], wt.at[g], wsem.at[g])

    def mcopies(layer):
        pairs = (wi_hbm, wi_ref), (woe_hbm, woe_ref), (woo_hbm, woo_ref)
        return [pltpu.make_async_copy(a.at[which[layer]], b.at[layer], msem.at[layer, i]) for i, (a, b) in enumerate(pairs)]

    def fetch(g):
        pl.when(g < mixed)(lambda: zcopy(g, zc_hbm).start())
        pl.when(g >= mixed)(lambda: zcopy(g, z_hbm).start())
        wcopy(g, 0).start()

    def outcopy(j):
        return pltpu.make_async_copy(out.at[j], out_hbm.at[:, pl.ds(pl.multiple_of(j * per, LN), per)], osem.at[j])

    ones = (lax.broadcasted_iota(jnp.int32, (256, 256), 0) // LG == lax.broadcasted_iota(jnp.int32, (256, 256), 1) // LG)
    ones = ones.astype(f32).astype(bf)

    def lane_mean(s):
        hi = s.astype(bf)
        lo = (s - hi.astype(f32)).astype(bf)
        return (jnp.dot(hi, ones, preferred_element_type=f32) + jnp.dot(lo, ones, preferred_element_type=f32)) * (1.0 / count)

    for g in range(AHEAD):
        fetch(jnp.int32(g))

    for layer in range(2):
        src = (zs, zn)[layer]
        above, below = ((top_ref, bot_ref), (tops, bots))[layer]
        have = above.shape[0]
        many = nj * hr + (4 * nj if layer == 0 else 0)
        ssum[...] = jnp.zeros_like(ssum)

        @pl.loop(0, ng)
        def _(g):
            if layer == 0:
                pl.when(g + AHEAD < ng)(lambda: fetch(g + AHEAD))

                @pl.when(g == ng // 2)
                def _():
                    for c in mcopies(0) + mcopies(1):
                        c.start()
                zcopy(g, z_hbm).wait()
            wcopy(g, layer).wait()

            for j in range(nj):
                zf[j, pl.ds(pad, rows), :] = src[g, j].astype(f32)
            hs = pl.ds(pl.multiple_of(g * nj, nj), nj)
            for r in range(HALO):
                zf[:, pad - HALO + r, :] = above[have - HALO + r, hs, :].astype(f32)
                zf[:, pad + rows + r, :] = below[r, hs, :].astype(f32)
            m64 = lane_bit((hr, LN), 64)
            zero = jnp.zeros((hr, LN), bf)
            for a in range(8):
                v = [zf[j, pl.ds(pad - HALO + a, hr, stride=2), :].astype(bf) for j in range(nj)]
                for j in range(nj):
                    nxt = v[j + 1] if j + 1 < nj else zero
                    prv = v[j - 1] if j > 0 else zero
                    lhs[j * hr:(j + 1) * hr, a * 256:a * 256 + LN] = v[j]
                    lhs[j * hr:(j + 1) * hr, a * 256 + LN:a * 256 + 256] = jnp.where(m64, nxt, prv)

            if layer == 0:
                m64 = lane_bit((nj, LN), 64)
                sub = lax.broadcasted_iota(jnp.int32, (nj, LN), 0)
                got = {}

                def row_of(at):
                    if at not in got:
                        if 0 <= at < rows:
                            v = zf[:, pad + at, :]
                        elif -have <= at < 0:
                            v = above[at + have, hs, :].astype(f32)
                        elif rows <= at < rows + have:
                            v = below[at - rows, hs, :].astype(f32)
                        else:
                            v = jnp.zeros((nj, LN), f32)
                        nxt = jnp.where(sub < nj - 1, pltpu.roll(v, nj - 1, 0), 0.0)
                        prv = jnp.where(sub > 0, pltpu.roll(v, 1, 0), 0.0)
                        got[at] = v, jnp.where(m64, nxt, prv)
                    return got[at]
                for a in range(8):
                    for n in range(2):
                        v = jnp.concatenate([row_of(2 * r - HALO + a)[n] for r in ends], 0).astype(bf)
                        lhs[nj * hr:many, a * 256 + n * LN:a * 256 + (n + 1) * LN] = v
            band_g, zero_g = wt[g], jnp.zeros((256, LN), bf)
            rhs = jnp.concatenate([jnp.concatenate([band_g, zero_g], 0), jnp.concatenate([zero_g, band_g], 0)], 1)
            sp = jnp.dot(lhs[:many], rhs, preferred_element_type=f32)
            spr[g, :many] = sp
            ssum[:many] += sp
            if layer == 0:
                wcopy(g, 1).start()

        if layer == 0:
            for c in mcopies(0) + mcopies(1):
                c.wait()
        nrm[:many] = lane_mean(ssum[:many])

        @pl.loop(0, many // 32)
        def _(n):
            rs = pl.ds(pl.multiple_of(n * 32, 32), 32)
            mean = nrm[rs, :]
            q = jnp.zeros((32, 256), f32)
            for g in range(ng):
                c = spr[g, rs, :] - mean
                q = q + c * c
            ssum[rs, :] = q
        ssum[:many] = lax.rsqrt(lane_mean(ssum[:many]) + 1e-06)
        fac = fac_ref[0, layer]
        gains = gain_ref[which[layer]]

        def update(js):
            mean, rstd = nrm[js, :], ssum[js, :]
            zz = [((spr[g, js, :] - mean) * rstd * gains[g:g + 1, :]).astype(bf) for g in range(ng)]
            nat = [from_patch([t[:, p * LN:(p + 1) * LN] for t in zz]) for p in range(2)]
            nat = [jnp.concatenate([a, b], 0) for a, b in zip(*nat)]
            size = nat[0].shape[0]
            xe = jnp.concatenate([jnp.concatenate([nat[3 * i], nat[3 * i + 1]], 1) for i in range(npair)], 0)
            xo = jnp.concatenate([jnp.concatenate([nat[3 * i + 1], nat[3 * i + 2]], 1) for i in range(npair)], 0)

            def mlp(x, wi, wo):
                h = gelu(jnp.dot(x, wi, preferred_element_type=f32).astype(bf))
                return jnp.dot(h, wo, preferred_element_type=f32)
            ue = mlp(xe, wi_ref[layer, 64:, :], woe_ref[layer])
            uo = mlp(xo, wi_ref[layer, :256, :], woo_ref[layer])
            res = []
            for i in range(npair):
                e, o = ue[i * size:(i + 1) * size], uo[i * size:(i + 1) * size]
                res += [e[:, :LN], e[:, LN:] + o[:, :LN], o[:, LN:]]
            return res

        @pl.loop(0, nj)
        def _(j):
            for n, val in enumerate(update(pl.ds(pl.multiple_of(j * hr, hr), hr))):
                for p in range(2):
                    upd[n, pl.ds(p, hr, stride=2), :] = val[p * hr:(p + 1) * hr]
            if layer == 0:
                for g, more in enumerate(to_patch([(fac * upd[n]).astype(bf) for n in range(3 * npair)])):
                    zn[g, j] = (zs[g, j].astype(f32) + more.astype(f32)).astype(bf)
            else:
                own = from_patch([zn[g, j] for g in range(ng)])
                for n in range(3 * npair):
                    out[j, :, n * LN:(n + 1) * LN] = (own[n].astype(f32) + fac * upd[n]).astype(bf)
                outcopy(j).start()

        if layer == 0:
            more = to_patch([(fac * val).astype(bf) for val in update(pl.ds(nj * hr, 4 * nj))])
            for g in range(ng):
                gs = pl.ds(g * nj, nj)
                for r in range(HALO):
                    for at, keep, own, to in ((r - HALO, 2, above[have - HALO + r, gs, :], tops), (rows + r, 3, below[r, gs, :], bots)):
                        n = at % 2 * 4 * nj + ends.index(at // 2) * nj
                        new = (own.astype(f32) + more[g][n:n + nj].astype(f32)).astype(bf)
                        to[r, gs, :] = fac_ref[0, keep] * new.astype(f32)

    @pl.loop(0, nj)
    def _(j):
        outcopy(j).wait()


def blocks(place, fac, zc, z, top, bot, w, gain, wi, woe, woo):
    ng, nj, rows, _ = z.shape
    hr = rows // 2
    many = nj * hr + 4 * nj
    per = ng * LG * PC
    vm = pl.BlockSpec(memory_space=VM)
    sm = pl.BlockSpec(memory_space=pltpu.SMEM)
    hbm = pl.BlockSpec(memory_space=pl.ANY)
    return pl.pallas_call(
        blocks_kernel,
        out_shape=jax.ShapeDtypeStruct((rows, nj * per), bf),
        in_specs=[sm, sm, hbm, hbm, vm, vm, hbm, vm, hbm, hbm, hbm],
        out_specs=hbm,
        scratch_shapes=[
            VM((ng, nj, rows, LN), bf),
            VM((ng, nj, rows, LN), bf),
            VM((nj, rows + 16, LN), f32),
            VM((many, 2048), bf),
            VM((ng, 1792, LN), bf),
            VM((ng, many, 256), f32),
            VM((many, 256), f32),
            VM((many, 256), f32),
            VM((12, rows, LN), f32),
            VM((nj, rows, per), bf),
            VM((2,) + wi.shape[1:], bf),
            VM((2,) + woe.shape[1:], bf),
            VM((2,) + woo.shape[1:], bf),
            VM((HALO,) + top.shape[1:], f32),
            VM((HALO,) + top.shape[1:], f32),
            pltpu.SemaphoreType.DMA((ng,)),
            pltpu.SemaphoreType.DMA((ng,)),
            pltpu.SemaphoreType.DMA((nj,)),
            pltpu.SemaphoreType.DMA((2, 3)),
        ],
        compiler_params=PARAMS,
        name="blocks",
    )(place, fac, zc, z, top, bot, w, gain, wi, woe, woo)


def prep_all(depth, gain, inner, outer):
    nl, c = gain.shape
    ng = c // LG
    e = jnp.pad(depth[:, :, ::-1, :], ((0, 0), (0, 1), (0, 1), (0, 0))).reshape(nl, 8, 8, ng, LG)
    e = e.transpose(0, 3, 1, 2, 4).reshape(nl, ng, 8, LN)
    gl = jnp.tile(gain.reshape(nl, ng, 1, LG), (1, 1, 16, 1)).reshape(nl, ng, 256)
    wi = jnp.pad(0.5 * inner, ((0, 0), (64, 64), (0, 0)))
    woe = jnp.pad(outer, ((0, 0), (0, 0), (0, 64)))
    woo = jnp.pad(outer, ((0, 0), (0, 0), (64, 0)))
    return e, gl, wi, woe, woo


def halo(top, bot):
    n = lax.axis_size("row")
    return (
        lax.ppermute(bot, "row", [(i, i + 1) for i in range(n - 1)]),
        lax.ppermute(top, "row", [(i + 1, i) for i in range(n - 1)]),
    )


def exchange(outs):
    n = len(outs)
    assert n & (n - 1) == 0
    return [
        lax.ppermute(o, ("comp", "tile"), [(s * n + t, (1 - s) * n + (t ^ d)) for s in range(2) for t in range(n)])
        for d, o in enumerate(outs)
    ]


def on_device(state, pairs, wet, mix_weight, depth_weight, norm_gain, inner_weight, outer_weight):
    assert state.shape[1] == 1
    section = lax.axis_index("comp")
    tiles = lax.axis_size("tile")
    place = jnp.stack([section, lax.axis_index("tile"), lax.axis_index("row")]).astype(jnp.int32)
    pick = lambda w, i: lax.dynamic_index_in_dim(w, i, 0, keepdims=False)
    z, etop, ebot, *outs = pack(pairs, place, state[0, 0], tiles, mix_weight.shape[1], norm_gain.shape[1] // LG)
    gots = exchange(outs)
    e, *weights = prep_all(depth_weight, norm_gain, inner_weight, outer_weight)
    wmix = jnp.tile(pick(mix_weight, section).astype(f32), (1, 1, PC))
    factor = jnp.where(section == 0, 1.0, wet[0].astype(f32))
    inside = jnp.stack([place[2] > 0, place[2] < lax.axis_size("row") - 1]).astype(f32)
    factors = jnp.concatenate([jnp.stack([factor, (section == 0).astype(f32)]), inside]).reshape(1, 4)
    gots, bands, weights, wmix, factors = lax.optimization_barrier((gots, band(place, e), weights, wmix, factors))
    top, bot = halo(*mix(pairs, place, z, wmix, gots, (etop, ebot)))
    zc = mix(pairs, place, z, wmix, gots)
    out = blocks(place, factors, zc, z, top, bot, bands, *weights)
    return out[None, None]


def solution(mesh):
    return jax.shard_map(
        on_device,
        mesh=mesh,
        in_specs=(P("comp", "tile", "row", None), P(), P("tile"), P(), P(), P(), P(), P()),
        out_specs=P("comp", "tile", "row", None),
        check_vma=False,
    )
```

```python
import functools
import jax
import jax.numpy as jnp
from jax import lax
from jax.experimental import pallas as pl
from jax.experimental.pallas import tpu as pltpu
from jax.sharding import PartitionSpec as P

VM = pltpu.VMEM
PC = 8
LG = 16
LN = 128
bf, f32 = jnp.bfloat16, jnp.float32
HALO = 3
SIDE = 8
AHEAD = 3
PARAMS = pltpu.CompilerParams(vmem_limit_bytes=56 * 2**20)


def lane_bit(shape, bit):
    return (lax.broadcasted_iota(jnp.int32, shape, 1) & bit) == 0


def lroll(x, shift):
    return pltpu.roll(x, shift % LN, 1)


def swap_stage(a, b, bit, m):
    return jnp.where(m, a, lroll(b, bit)), jnp.where(m, lroll(a, -bit), b)


def to_patch(v):
    half = len(v) // 2
    shape = v[0].shape
    m64, m32, m16 = (lane_bit(shape, b) for b in (64, 32, 16))
    per = 3
    u = {}
    for j in range(4):
        for t in range(per):
            q = per * j + t
            a, b = v[q // 2], v[q // 2 + half]
            if q % 2 == 0:
                u[j, t] = jnp.where(m64, a, lroll(b, 64))
            else:
                u[j, t] = jnp.where(m64, lroll(a, 64), b)
    out = []
    for t in range(per):
        a0, b0 = swap_stage(u[0, t], u[2, t], 32, m32)
        a1, b1 = swap_stage(u[1, t], u[3, t], 32, m32)
        out += swap_stage(a0, a1, 16, m16)
        out += swap_stage(b0, b1, 16, m16)
    return out


def from_patch(z):
    half = len(z) // 2
    shape = z[0].shape
    m64, m32, m16 = (lane_bit(shape, b) for b in (64, 32, 16))
    per = len(z) // 4
    u = {}
    for t in range(per):
        a0, a1 = swap_stage(z[4 * t], z[4 * t + 1], 16, m16)
        b0, b1 = swap_stage(z[4 * t + 2], z[4 * t + 3], 16, m16)
        u[0, t], u[2, t] = swap_stage(a0, b0, 32, m32)
        u[1, t], u[3, t] = swap_stage(a1, b1, 32, m32)
    lo, hi = {}, {}
    for j in range(4):
        for t in range(per):
            q = per * j + t
            lo[q] = u[j, t]
            hi[q] = u[j, t]
    v = []
    for n in range(half):
        e, o = u[divmod(2 * n, per)], u[divmod(2 * n + 1, per)]
        v.append(jnp.where(m64, e, lroll(o, 64)))
    for n in range(half):
        e, o = u[divmod(2 * n, per)], u[divmod(2 * n + 1, per)]
        v.append(jnp.where(m64, lroll(e, 64), o))
    return v


def gelu(h):
    c = 0.7978845608028654
    inside = h * (jnp.asarray(2 * c, bf) + jnp.asarray(8 * 0.044715 * c, bf) * (h * h))
    return h + h * jnp.tanh(inside)


def part(i, n):
    if n & (n - 1) == 0:
        return lax.shift_right_logical(i, n.bit_length() - 1), i & (n - 1)
    return lax.div(i, n), lax.rem(i, n)


def pack_kernel(pairs, place, x_hbm, z_hbm, top_ref, bot_ref, *rest, mixed, tiles):
    outs = rest[:tiles]
    xs, zs, send, order, xsem, zsem, ssem = rest[tiles:]
    ng, nj, rows, _ = zs.shape
    per = x_hbm.shape[1] // nj
    hold = send.shape[0]
    peer = hold // tiles
    of_tile = pairs.shape[1] // tiles
    ncb = nj // 2
    section, tile, band_at = place[0], place[1], place[2]

    def xcopy(j):
        return pltpu.make_async_copy(x_hbm.at[:, pl.ds(pl.multiple_of(j * per, LN), per)], xs.at[j], xsem.at[j])

    def zcopy(j):
        return pltpu.make_async_copy(zs.at[:, j], z_hbm.at[:, j], zsem.at[j])

    for j in range(nj):
        xcopy(j).start()

    @pl.loop(0, tiles)
    def _(q):
        first = lax.bitwise_xor(q, tile) * peer

        def one(slot, rank):
            src_tile, src = part(pairs[1 - section, q * of_tile + band_at * hold + slot], of_tile)
            mine = src_tile == tile
            order[jnp.where(mine, first + rank, hold)] = src - band_at * hold
            return rank + mine.astype(jnp.int32)
        lax.fori_loop(0, hold, one, jnp.int32(0), unroll=8)

    @pl.loop(0, nj)
    def _(j):
        xcopy(j).wait()
        zz = to_patch([xs[j, :, n * LN:(n + 1) * LN] for n in range(12)])
        for g in range(ng):
            zs[g, j] = zz[g]
        for g in range(mixed, ng):
            for r in range(2 * HALO):
                top_ref[r, pl.ds((g - mixed) * nj + j, 1), :] = zz[g][r:r + 1].astype(f32)
                bot_ref[r, pl.ds((g - mixed) * nj + j, 1), :] = zz[g][rows - 2 * HALO + r:rows - 2 * HALO + r + 1].astype(f32)
        zcopy(j).start()

    @pl.loop(0, hold)
    def _(at):
        up, side = part(order[at], ncb)
        row = pl.ds(pl.multiple_of(up * 16, 16), 16)
        for g in range(mixed):
            for h in range(2):
                send[at, 2 * g + h] = zs[g, 2 * side + h, row, :]

    copies = [pltpu.make_async_copy(send.at[pl.ds(d * peer, peer)], outs[d], ssem.at[d]) for d in range(tiles)]
    for c in copies:
        c.start()
    for c in copies:
        c.wait()
    for j in range(nj):
        zcopy(j).wait()


def pack(pairs, place, x, tiles, mixed, ng):
    rows, width = x.shape
    per = ng * LG * PC
    nj = width // per
    hold = rows // 16 * (nj // 2)
    vm = pl.BlockSpec(memory_space=VM)
    sm = pl.BlockSpec(memory_space=pltpu.SMEM)
    hbm = pl.BlockSpec(memory_space=pl.ANY)
    edge = jax.ShapeDtypeStruct((2 * HALO, (ng - mixed) * nj, LN), f32)
    return pl.pallas_call(
        functools.partial(pack_kernel, mixed=mixed, tiles=tiles),
        out_shape=(jax.ShapeDtypeStruct((ng, nj, rows, LN), bf), edge, edge)
        + (jax.ShapeDtypeStruct((hold // tiles, 2 * mixed, 16, LN), bf),) * tiles,
        in_specs=[sm, sm, hbm],
        out_specs=(hbm, vm, vm) + (hbm,) * tiles,
        scratch_shapes=[
            VM((nj, rows, per), bf),
            VM((ng, nj, rows, LN), bf),
            VM((hold, 2 * mixed, 16, LN), bf),
            pltpu.SMEM((hold + 1,), jnp.int32),
            pltpu.SemaphoreType.DMA((nj,)),
            pltpu.SemaphoreType.DMA((nj,)),
            pltpu.SemaphoreType.DMA((tiles,)),
        ],
        compiler_params=PARAMS,
        name="pack",
    )(pairs, place, x)


def mix_kernel(pairs, place, z_hbm, *rest, mixed, tiles, edges):
    wm, *rest = rest
    gots, rest = rest[:tiles], rest[tiles:]
    if edges:
        etop_ref, ebot_ref, otop_ref, obot_ref, top_ref, bot_ref, *rest = rest
    else:
        out_hbm, *rest = rest
    zs, zp, got, count, zsem, gsem, osem = rest
    _, nj, rows, _ = zs.shape
    whole = z_hbm.shape[2]
    hold = got.shape[0]
    peer = hold // tiles
    of_tile = pairs.shape[1] // tiles
    ncb = nj // 2
    section, tile, band_at = place[0], place[1], place[2]

    gcopy = [pltpu.make_async_copy(gots[d], got.at[pl.ds(d * peer, peer)], gsem.at[d]) for d in range(tiles)]
    for c in gcopy:
        c.start()

    def zcopy(g):
        if not edges:
            return [pltpu.make_async_copy(z_hbm.at[g], zs.at[g], zsem.at[g, 0])]
        return [
            pltpu.make_async_copy(z_hbm.at[g, :, pl.ds(at, 16), :], zs.at[g, :, pl.ds(n * 16, 16), :], zsem.at[g, n])
            for n, at in enumerate((0, whole - 16))
        ]

    def ocopy(g):
        return pltpu.make_async_copy(zs.at[g], out_hbm.at[g], osem.at[g])

    for g in range(mixed):
        for c in zcopy(g):
            c.start()
    for q in range(tiles):
        count[q] = 0
    for c in gcopy:
        c.wait()

    @pl.loop(0, hold)
    def _(slot):
        q, _ = part(pairs[section, tile * of_tile + band_at * hold + slot], of_tile)
        rank = count[q]
        count[q] = rank + 1
        at = lax.bitwise_xor(q, tile) * peer + rank
        up, side = part(slot, ncb)

        def put(up):
            row = pl.ds(pl.multiple_of(up * 16, 16), 16)
            for g in range(mixed):
                for h in range(2):
                    zp[g, 2 * side + h, row, :] = got[at, 2 * g + h]
        if edges:
            pl.when(up == 0)(lambda: put(0))
            pl.when(up == whole // 16 - 1)(lambda: put(1))
        else:
            put(up)

    side = 4 if edges else 1

    @pl.loop(0, mixed // side)
    def _(gg):
        for s in range(side):
            g = gg * side + s
            for c in zcopy(g):
                c.wait()
            own = zs[g].reshape(nj * rows, LN)
            both = jnp.concatenate([own, zp[g].reshape(nj * rows, LN)], 1)
            new = own.astype(f32) + jnp.dot(both, wm[g], preferred_element_type=f32)
            new = new.astype(bf).reshape(nj, rows, LN)
            if not edges:
                zs[g] = new
                ocopy(g).start()
            for j in range(nj if edges else 0):
                for r in range(2 * HALO):
                    low = rows - 2 * HALO + r
                    top_ref[r, pl.ds(g * nj + j, 1), :] = new[j, r:r + 1].astype(f32)
                    bot_ref[r, pl.ds(g * nj + j, 1), :] = new[j, low:low + 1].astype(f32)

    if edges:
        top_ref[:, mixed * nj:, :] = etop_ref[...]
        bot_ref[:, mixed * nj:, :] = ebot_ref[...]
        otop_ref[...] = top_ref[...].astype(bf)
        obot_ref[...] = bot_ref[...].astype(bf)
    else:
        for g in range(mixed):
            ocopy(g).wait()


def mix(pairs, place, z, w, gots, ends=()):
    ng, nj, rows, _ = z.shape
    edges = len(ends) > 0
    mixed = w.shape[0]
    tiles = len(gots)
    hold = gots[0].shape[0] * tiles
    vm = pl.BlockSpec(memory_space=VM)
    sm = pl.BlockSpec(memory_space=pltpu.SMEM)
    hbm = pl.BlockSpec(memory_space=pl.ANY)
    edge = jax.ShapeDtypeStruct((2 * HALO, ng * nj, LN), bf)
    here = 32 if edges else rows
    return pl.pallas_call(
        functools.partial(mix_kernel, mixed=mixed, tiles=tiles, edges=edges),
        out_shape=(edge, edge) if edges else jax.ShapeDtypeStruct((mixed, nj, rows, LN), bf),
        in_specs=[sm, sm, hbm, vm] + [hbm] * tiles + [vm] * len(ends),
        out_specs=(vm, vm) if edges else hbm,
        scratch_shapes=([VM(edge.shape, f32)] * 2 if edges else []) + [
            VM((mixed, nj, here, LN), bf),
            VM((mixed, nj, here, LN), bf),
            VM((hold,) + gots[0].shape[1:], bf),
            pltpu.SMEM((tiles,), jnp.int32),
            pltpu.SemaphoreType.DMA((mixed, 2)),
            pltpu.SemaphoreType.DMA((tiles,)),
            pltpu.SemaphoreType.DMA((mixed,)),
        ],
        compiler_params=PARAMS,
        cost_estimate=pl.CostEstimate(flops=10**9, bytes_accessed=2**23, transcendentals=0),
        name="mix_edges" if edges else "mix",
    )(pairs, place, z, w, *gots, *ends)


def band_kernel(place, e_ref, mix_ref, w_ref, wm_ref):
    delta = lax.broadcasted_iota(jnp.int32, (LG, LN), 0) == lax.broadcasted_iota(jnp.int32, (LG, LN), 1) % LG
    chunk = lax.broadcasted_iota(jnp.int32, (8, LN), 1) // LG
    zero = jnp.zeros((LG, LN), bf)

    for g in range(mix_ref.shape[0]):
        for h in range(2):
            w = mix_ref[g, h * LG:(h + 1) * LG, :]
            for c in range(PC):
                at = h * LN + c * LG
                wm_ref[g, at:at + LG] = jnp.where(lax.broadcasted_iota(jnp.int32, (LG, LN), 1) // LG == c, w, 0.0).astype(bf)
    ng = e_ref.shape[1]
    first = jnp.where(place[0] == 0, 0, 2)

    @pl.loop(0, 2 * ng)
    def _(g):
        e = e_ref[jnp.where(g < ng, first, 1), jnp.where(g < ng, g, g - ng)]
        for pos, jr in enumerate(list(range(12)) + list(range(-4, 0))):
            s = jr - 3
            r = lroll(e, s * LG)
            r = jnp.where((chunk >= s) & (chunk < 8 + s), r, 0.0)
            for k in range(7):
                row = k * 256 + pos * LG
                if jr in (-4, 11):
                    w_ref[g, row:row + LG] = zero
                else:
                    w_ref[g, row:row + LG] = jnp.where(delta, jnp.broadcast_to(r[k:k + 1], (LG, LN)), 0.0).astype(bf)


def band(place, e, wmix):
    vm = pl.BlockSpec(memory_space=VM)
    n = 2 * e.shape[1]
    return pl.pallas_call(
        band_kernel,
        out_shape=(jax.ShapeDtypeStruct((n, 1792, LN), bf), jax.ShapeDtypeStruct((wmix.shape[0], 2 * LN, LN), bf)),
        in_specs=[pl.BlockSpec(memory_space=pltpu.SMEM), vm, vm], out_specs=(vm, vm),
        cost_estimate=pl.CostEstimate(flops=10**9, bytes_accessed=n * 1792 * LN * 4, transcendentals=0),
        compiler_params=PARAMS,
        name="band",
    )(place, e, wmix)


def blocks_kernel(place, fac_ref, zc_hbm, z_hbm, top_ref, bot_ref, w_hbm, gain_ref, wi_hbm, woe_hbm, woo_hbm, out_hbm,
                  zs, zn, zf, lhs, wt, spr, ssum, nrm, upd, out, wi_ref, woe_ref, woo_ref, tops, bots, zsem, wsem, osem, msem):
    ng, nj, rows, _ = zs.shape
    hr = rows // 2
    pad = 8
    ends = (-2, -1, hr, hr + 1)
    count = ng * LG
    npair = PC // 2
    per = 3 * npair * LN
    mixed = zc_hbm.shape[0]
    which = jnp.where(place[0] == 0, 0, 2), 1

    def zcopy(g, source):
        return pltpu.make_async_copy(source.at[g], zs.at[g], zsem.at[g])

    def wcopy(g, layer):
        return pltpu.make_async_copy(w_hbm.at[layer * ng + g], wt.at[g], wsem.at[g])

    def mcopies(layer):
        pairs = (wi_hbm, wi_ref), (woe_hbm, woe_ref), (woo_hbm, woo_ref)
        return [pltpu.make_async_copy(a.at[which[layer]], b.at[layer], msem.at[layer, i]) for i, (a, b) in enumerate(pairs)]

    def fetch(g):
        pl.when(g < mixed)(lambda: zcopy(g, zc_hbm).start())
        pl.when(g >= mixed)(lambda: zcopy(g, z_hbm).start())
        wcopy(g, 0).start()

    def outcopy(j):
        return pltpu.make_async_copy(out.at[j], out_hbm.at[:, pl.ds(pl.multiple_of(j * per, LN), per)], osem.at[j])

    ones = (lax.broadcasted_iota(jnp.int32, (256, 256), 0) // LG == lax.broadcasted_iota(jnp.int32, (256, 256), 1) // LG)
    ones = ones.astype(f32).astype(bf)

    def lane_mean(s):
        hi = s.astype(bf)
        lo = (s - hi.astype(f32)).astype(bf)
        return (jnp.dot(hi, ones, preferred_element_type=f32) + jnp.dot(lo, ones, preferred_element_type=f32)) * (1.0 / count)

    for g in range(AHEAD):
        fetch(jnp.int32(g))

    for layer in range(2):
        src = (zs, zn)[layer]
        above, below = ((top_ref, bot_ref), (tops, bots))[layer]
        have = above.shape[0]
        many = nj * hr + (4 * nj if layer == 0 else 0)
        ssum[...] = jnp.zeros_like(ssum)

        @pl.loop(0, ng)
        def _(g):
            if layer == 0:
                pl.when(g + AHEAD < ng)(lambda: fetch(g + AHEAD))

                @pl.when(g == ng // 2)
                def _():
                    for c in mcopies(0) + mcopies(1):
                        c.start()
                zcopy(g, z_hbm).wait()
            wcopy(g, layer).wait()

            for j in range(nj):
                zf[j, pl.ds(pad, rows), :] = src[g, j].astype(f32)
            hs = pl.ds(pl.multiple_of(g * nj, nj), nj)
            for r in range(HALO):
                zf[:, pad - HALO + r, :] = above[have - HALO + r, hs, :].astype(f32)
                zf[:, pad + rows + r, :] = below[r, hs, :].astype(f32)
            m64 = lane_bit((hr, LN), 64)
            zero = jnp.zeros((hr, LN), bf)
            for a in range(8):
                v = [zf[j, pl.ds(pad - HALO + a, hr, stride=2), :].astype(bf) for j in range(nj)]
                for j in range(nj):
                    nxt = v[j + 1] if j + 1 < nj else zero
                    prv = v[j - 1] if j > 0 else zero
                    lhs[j * hr:(j + 1) * hr, a * 256:a * 256 + LN] = v[j]
                    lhs[j * hr:(j + 1) * hr, a * 256 + LN:a * 256 + 256] = jnp.where(m64, nxt, prv)

            if layer == 0:
                m64 = lane_bit((nj, LN), 64)
                sub = lax.broadcasted_iota(jnp.int32, (nj, LN), 0)
                got = {}

                def row_of(at):
                    if at not in got:
                        if 0 <= at < rows:
                            v = zf[:, pad + at, :]
                        elif -have <= at < 0:
                            v = above[at + have, hs, :].astype(f32)
                        elif rows <= at < rows + have:
                            v = below[at - rows, hs, :].astype(f32)
                        else:
                            v = jnp.zeros((nj, LN), f32)
                        nxt = jnp.where(sub < nj - 1, pltpu.roll(v, nj - 1, 0), 0.0)
                        prv = jnp.where(sub > 0, pltpu.roll(v, 1, 0), 0.0)
                        got[at] = v, jnp.where(m64, nxt, prv)
                    return got[at]
                for a in range(8):
                    for n in range(2):
                        v = jnp.concatenate([row_of(2 * r - HALO + a)[n] for r in ends], 0).astype(bf)
                        lhs[nj * hr:many, a * 256 + n * LN:a * 256 + (n + 1) * LN] = v
            band_g, zero_g = wt[g], jnp.zeros((256, LN), bf)
            rhs = jnp.concatenate([jnp.concatenate([band_g, zero_g], 0), jnp.concatenate([zero_g, band_g], 0)], 1)
            sp = jnp.dot(lhs[:many], rhs, preferred_element_type=f32)
            spr[g, :many] = sp
            ssum[:many] += sp
            if layer == 0:
                wcopy(g, 1).start()

        if layer == 0:
            for c in mcopies(0) + mcopies(1):
                c.wait()
        nrm[:many] = lane_mean(ssum[:many])

        @pl.loop(0, many // 32)
        def _(n):
            rs = pl.ds(pl.multiple_of(n * 32, 32), 32)
            mean = nrm[rs, :]
            q = jnp.zeros((32, 256), f32)
            for g in range(ng):
                c = spr[g, rs, :] - mean
                q = q + c * c
            ssum[rs, :] = q
        ssum[:many] = lax.rsqrt(lane_mean(ssum[:many]) + 1e-06)
        fac = fac_ref[0, layer]
        gains = gain_ref[which[layer]]

        def update(js):
            mean, rstd = nrm[js, :], ssum[js, :]
            zz = [((spr[g, js, :] - mean) * rstd * gains[g:g + 1, :]).astype(bf) for g in range(ng)]
            nat = [from_patch([t[:, p * LN:(p + 1) * LN] for t in zz]) for p in range(2)]
            nat = [jnp.concatenate([a, b], 0) for a, b in zip(*nat)]
            size = nat[0].shape[0]
            xe = jnp.concatenate([jnp.concatenate([nat[3 * i], nat[3 * i + 1]], 1) for i in range(npair)], 0)
            xo = jnp.concatenate([jnp.concatenate([nat[3 * i + 1], nat[3 * i + 2]], 1) for i in range(npair)], 0)

            def mlp(x, wi, wo):
                h = gelu(jnp.dot(x, wi, preferred_element_type=f32).astype(bf))
                return jnp.dot(h, wo, preferred_element_type=f32)
            ue = mlp(xe, wi_ref[layer, 64:, :], woe_ref[layer])
            uo = mlp(xo, wi_ref[layer, :256, :], woo_ref[layer])
            res = []
            for i in range(npair):
                e, o = ue[i * size:(i + 1) * size], uo[i * size:(i + 1) * size]
                res += [e[:, :LN], e[:, LN:] + o[:, :LN], o[:, LN:]]
            return res

        @pl.loop(0, nj // SIDE)
        def _(jj):
            for s in range(SIDE):
                j = jj * SIDE + s
                for n, val in enumerate(update(pl.ds(pl.multiple_of(j * hr, hr), hr))):
                    for p in range(2):
                        upd[s, n, pl.ds(p, hr, stride=2), :] = val[p * hr:(p + 1) * hr]
                if layer == 0:
                    for g, more in enumerate(to_patch([(fac * upd[s, n]).astype(bf) for n in range(3 * npair)])):
                        zn[g, j] = (zs[g, j].astype(f32) + more.astype(f32)).astype(bf)
                else:
                    own = from_patch([zn[g, j] for g in range(ng)])
                    for n in range(3 * npair):
                        out[j, :, n * LN:(n + 1) * LN] = (own[n].astype(f32) + fac * upd[s, n]).astype(bf)
                    outcopy(j).start()

        if layer == 0:
            more = to_patch([(fac * val).astype(bf) for val in update(pl.ds(nj * hr, 4 * nj))])
            for g in range(ng):
                gs = pl.ds(g * nj, nj)
                for r in range(HALO):
                    for at, keep, own, to in ((r - HALO, 2, above[have - HALO + r, gs, :], tops), (rows + r, 3, below[r, gs, :], bots)):
                        n = at % 2 * 4 * nj + ends.index(at // 2) * nj
                        new = (own.astype(f32) + more[g][n:n + nj].astype(f32)).astype(bf)
                        to[r, gs, :] = fac_ref[0, keep] * new.astype(f32)

    @pl.loop(0, nj)
    def _(j):
        outcopy(j).wait()


def blocks(place, fac, zc, z, top, bot, w, gain, wi, woe, woo):
    ng, nj, rows, _ = z.shape
    hr = rows // 2
    many = nj * hr + 4 * nj
    per = ng * LG * PC
    vm = pl.BlockSpec(memory_space=VM)
    sm = pl.BlockSpec(memory_space=pltpu.SMEM)
    hbm = pl.BlockSpec(memory_space=pl.ANY)
    return pl.pallas_call(
        blocks_kernel,
        out_shape=jax.ShapeDtypeStruct((rows, nj * per), bf),
        in_specs=[sm, sm, hbm, hbm, vm, vm, hbm, vm, hbm, hbm, hbm],
        out_specs=hbm,
        scratch_shapes=[
            VM((ng, nj, rows, LN), bf),
            VM((ng, nj, rows, LN), bf),
            VM((nj, rows + 16, LN), f32),
            VM((many, 2048), bf),
            VM((ng, 1792, LN), bf),
            VM((ng, many, 256), f32),
            VM((many, 256), f32),
            VM((many, 256), f32),
            VM((SIDE, 12, rows, LN), f32),
            VM((nj, rows, per), bf),
            VM((2,) + wi.shape[1:], bf),
            VM((2,) + woe.shape[1:], bf),
            VM((2,) + woo.shape[1:], bf),
            VM((HALO,) + top.shape[1:], f32),
            VM((HALO,) + top.shape[1:], f32),
            pltpu.SemaphoreType.DMA((ng,)),
            pltpu.SemaphoreType.DMA((ng,)),
            pltpu.SemaphoreType.DMA((nj,)),
            pltpu.SemaphoreType.DMA((2, 3)),
        ],
        compiler_params=PARAMS,
        name="blocks",
    )(place, fac, zc, z, top, bot, w, gain, wi, woe, woo)


def prep_all(depth, gain, inner, outer):
    nl, c = gain.shape
    ng = c // LG
    e = jnp.pad(depth[:, :, ::-1, :], ((0, 0), (0, 1), (0, 1), (0, 0))).reshape(nl, 8, 8, ng, LG)
    e = e.transpose(0, 3, 1, 2, 4).reshape(nl, ng, 8, LN)
    gl = jnp.tile(gain.reshape(nl, ng, 1, LG), (1, 1, 16, 1)).reshape(nl, ng, 256)
    wi = jnp.pad(0.5 * inner, ((0, 0), (64, 64), (0, 0)))
    woe = jnp.pad(outer, ((0, 0), (0, 0), (0, 64)))
    woo = jnp.pad(outer, ((0, 0), (0, 0), (64, 0)))
    return e, gl, wi, woe, woo


def halo(top, bot):
    n = lax.axis_size("row")
    return (
        lax.ppermute(bot, "row", [(i, i + 1) for i in range(n - 1)]),
        lax.ppermute(top, "row", [(i + 1, i) for i in range(n - 1)]),
    )


def exchange(outs):
    n = len(outs)
    assert n & (n - 1) == 0
    return [
        lax.ppermute(o, ("comp", "tile"), [(s * n + t, (1 - s) * n + (t ^ d)) for s in range(2) for t in range(n)])
        for d, o in enumerate(outs)
    ]


def on_device(state, pairs, wet, mix_weight, depth_weight, norm_gain, inner_weight, outer_weight):
    assert state.shape[1] == 1
    section = lax.axis_index("comp")
    tiles = lax.axis_size("tile")
    place = jnp.stack([section, lax.axis_index("tile"), lax.axis_index("row")]).astype(jnp.int32)
    pick = lambda w, i: lax.dynamic_index_in_dim(w, i, 0, keepdims=False)
    z, etop, ebot, *outs = pack(pairs, place, state[0, 0], tiles, mix_weight.shape[1], norm_gain.shape[1] // LG)
    gots = exchange(outs)
    e, *weights = prep_all(depth_weight, norm_gain, inner_weight, outer_weight)
    wmix = jnp.tile(pick(mix_weight, section).astype(f32), (1, 1, PC))
    factor = jnp.where(section == 0, 1.0, wet[0].astype(f32))
    inside = jnp.stack([place[2] > 0, place[2] < lax.axis_size("row") - 1]).astype(f32)
    factors = jnp.concatenate([jnp.stack([factor, (section == 0).astype(f32)]), inside]).reshape(1, 4)
    gots, (bands, wmix), weights, factors = lax.optimization_barrier((gots, band(place, e, wmix), weights, factors))
    top, bot = halo(*mix(pairs, place, z, wmix, gots, (etop, ebot)))
    zc = mix(pairs, place, z, wmix, gots)
    out = blocks(place, factors, zc, z, top, bot, bands, *weights)
    return out[None, None]


def solution(mesh):
    return jax.shard_map(
        on_device,
        mesh=mesh,
        in_specs=(P("comp", "tile", "row", None), P(), P("tile"), P(), P(), P(), P(), P()),
        out_specs=P("comp", "tile", "row", None),
        check_vma=False,
    )
```

```python
import functools
import jax
import jax.numpy as jnp
from jax import lax
from jax.experimental import pallas as pl
from jax.experimental.pallas import tpu as pltpu
from jax.sharding import PartitionSpec as P

VM = pltpu.VMEM
PC = 8
LG = 16
LN = 128
bf, f32 = jnp.bfloat16, jnp.float32
HALO = 3
SIDE = 8
AHEAD = 3
PARAMS = pltpu.CompilerParams(vmem_limit_bytes=56 * 2**20)


def lane_bit(shape, bit):
    return (lax.broadcasted_iota(jnp.int32, shape, 1) & bit) == 0


def lroll(x, shift):
    return pltpu.roll(x, shift % LN, 1)


def swap_stage(a, b, bit, m):
    return jnp.where(m, a, lroll(b, bit)), jnp.where(m, lroll(a, -bit), b)


def to_patch(v):
    half = len(v) // 2
    shape = v[0].shape
    m64, m32, m16 = (lane_bit(shape, b) for b in (64, 32, 16))
    per = 3
    u = {}
    for j in range(4):
        for t in range(per):
            q = per * j + t
            a, b = v[q // 2], v[q // 2 + half]
            if q % 2 == 0:
                u[j, t] = jnp.where(m64, a, lroll(b, 64))
            else:
                u[j, t] = jnp.where(m64, lroll(a, 64), b)
    out = []
    for t in range(per):
        a0, b0 = swap_stage(u[0, t], u[2, t], 32, m32)
        a1, b1 = swap_stage(u[1, t], u[3, t], 32, m32)
        out += swap_stage(a0, a1, 16, m16)
        out += swap_stage(b0, b1, 16, m16)
    return out


def from_patch(z):
    half = len(z) // 2
    shape = z[0].shape
    m64, m32, m16 = (lane_bit(shape, b) for b in (64, 32, 16))
    per = len(z) // 4
    u = {}
    for t in range(per):
        a0, a1 = swap_stage(z[4 * t], z[4 * t + 1], 16, m16)
        b0, b1 = swap_stage(z[4 * t + 2], z[4 * t + 3], 16, m16)
        u[0, t], u[2, t] = swap_stage(a0, b0, 32, m32)
        u[1, t], u[3, t] = swap_stage(a1, b1, 32, m32)
    lo, hi = {}, {}
    for j in range(4):
        for t in range(per):
            q = per * j + t
            lo[q] = u[j, t]
            hi[q] = u[j, t]
    v = []
    for n in range(half):
        e, o = u[divmod(2 * n, per)], u[divmod(2 * n + 1, per)]
        v.append(jnp.where(m64, e, lroll(o, 64)))
    for n in range(half):
        e, o = u[divmod(2 * n, per)], u[divmod(2 * n + 1, per)]
        v.append(jnp.where(m64, lroll(e, 64), o))
    return v


def gelu(h):
    c = 0.7978845608028654
    inside = h * (jnp.asarray(2 * c, bf) + jnp.asarray(8 * 0.044715 * c, bf) * (h * h))
    return h + h * jnp.tanh(inside)


def part(i, n):
    if n & (n - 1) == 0:
        return lax.shift_right_logical(i, n.bit_length() - 1), i & (n - 1)
    return lax.div(i, n), lax.rem(i, n)


def pack_kernel(pairs, x_hbm, z_hbm, top_ref, bot_ref, *rest, mixed, tiles):
    outs = rest[:tiles]
    xs, zs, send, order, xsem, zsem, ssem = rest[tiles:]
    ng, nj, rows, _ = zs.shape
    per = x_hbm.shape[1] // nj
    hold = send.shape[0]
    peer = hold // tiles
    of_tile = pairs.shape[1] // tiles
    ncb = nj // 2
    section, tile, band_at = lax.axis_index("comp"), lax.axis_index("tile"), lax.axis_index("row")

    def xcopy(j):
        return pltpu.make_async_copy(x_hbm.at[:, pl.ds(pl.multiple_of(j * per, LN), per)], xs.at[j], xsem.at[j])

    def zcopy(j):
        return pltpu.make_async_copy(zs.at[:, j], z_hbm.at[:, j], zsem.at[j])

    for j in range(nj):
        xcopy(j).start()

    @pl.loop(0, tiles)
    def _(q):
        first = lax.bitwise_xor(q, tile) * peer

        def one(slot, rank):
            src_tile, src = part(pairs[1 - section, q * of_tile + band_at * hold + slot], of_tile)
            mine = src_tile == tile
            order[jnp.where(mine, first + rank, hold)] = src - band_at * hold
            return rank + mine.astype(jnp.int32)
        lax.fori_loop(0, hold, one, jnp.int32(0), unroll=8)

    @pl.loop(0, nj)
    def _(j):
        xcopy(j).wait()
        zz = to_patch([xs[j, :, n * LN:(n + 1) * LN] for n in range(12)])
        for g in range(ng):
            zs[g, j] = zz[g]
        for g in range(mixed, ng):
            for r in range(2 * HALO):
                top_ref[r, pl.ds((g - mixed) * nj + j, 1), :] = zz[g][r:r + 1].astype(f32)
                bot_ref[r, pl.ds((g - mixed) * nj + j, 1), :] = zz[g][rows - 2 * HALO + r:rows - 2 * HALO + r + 1].astype(f32)
        zcopy(j).start()

    copies = [pltpu.make_async_copy(send.at[pl.ds(d * peer, peer)], outs[d], ssem.at[d]) for d in range(tiles)]
    for d in range(tiles):
        @pl.loop(d * peer, (d + 1) * peer)
        def _(at):
            up, side = part(order[at], ncb)
            row = pl.ds(pl.multiple_of(up * 16, 16), 16)
            for g in range(mixed):
                for h in range(2):
                    send[at, 2 * g + h] = zs[g, 2 * side + h, row, :]
        copies[d].start()
    for c in copies:
        c.wait()
    for j in range(nj):
        zcopy(j).wait()


def pack(pairs, x, tiles, mixed, ng):
    rows, width = x.shape
    per = ng * LG * PC
    nj = width // per
    hold = rows // 16 * (nj // 2)
    vm = pl.BlockSpec(memory_space=VM)
    sm = pl.BlockSpec(memory_space=pltpu.SMEM)
    hbm = pl.BlockSpec(memory_space=pl.ANY)
    edge = jax.ShapeDtypeStruct((2 * HALO, (ng - mixed) * nj, LN), f32)
    return pl.pallas_call(
        functools.partial(pack_kernel, mixed=mixed, tiles=tiles),
        out_shape=(jax.ShapeDtypeStruct((ng, nj, rows, LN), bf), edge, edge)
        + (jax.ShapeDtypeStruct((hold // tiles, 2 * mixed, 16, LN), bf),) * tiles,
        in_specs=[sm, hbm],
        out_specs=(hbm, vm, vm) + (hbm,) * tiles,
        scratch_shapes=[
            VM((nj, rows, per), bf),
            VM((ng, nj, rows, LN), bf),
            VM((hold, 2 * mixed, 16, LN), bf),
            pltpu.SMEM((hold + 1,), jnp.int32),
            pltpu.SemaphoreType.DMA((nj,)),
            pltpu.SemaphoreType.DMA((nj,)),
            pltpu.SemaphoreType.DMA((tiles,)),
        ],
        compiler_params=PARAMS,
        name="pack",
    )(pairs, x)


def mix_kernel(pairs, place, z_hbm, wm, *rest, mixed, tiles):
    gots, rest = rest[:tiles], rest[tiles:]
    etop_ref, ebot_ref, out_hbm, otop_ref, obot_ref, top_ref, bot_ref, zs, zp, got, count, zsem, gsem, osem = rest
    _, nj, rows, _ = zs.shape
    hold = got.shape[0]
    peer = hold // tiles
    of_tile = pairs.shape[1] // tiles
    ncb = nj // 2
    section, tile, band_at = place[0], place[1], place[2]

    gcopy = [pltpu.make_async_copy(gots[d], got.at[pl.ds(d * peer, peer)], gsem.at[d]) for d in range(tiles)]
    for c in gcopy:
        c.start()

    def zcopy(g):
        return pltpu.make_async_copy(z_hbm.at[g], zs.at[g], zsem.at[g])

    def ocopy(g):
        return pltpu.make_async_copy(zs.at[g], out_hbm.at[g], osem.at[g])

    for g in range(mixed):
        zcopy(g).start()
    for q in range(tiles):
        count[q] = 0
    for c in gcopy:
        c.wait()

    @pl.loop(0, hold)
    def _(slot):
        q, _ = part(pairs[section, tile * of_tile + band_at * hold + slot], of_tile)
        rank = count[q]
        count[q] = rank + 1
        at = lax.bitwise_xor(q, tile) * peer + rank
        up, side = part(slot, ncb)

        row = pl.ds(pl.multiple_of(up * 16, 16), 16)
        for g in range(mixed):
            for h in range(2):
                zp[g, 2 * side + h, row, :] = got[at, 2 * g + h]

    @pl.loop(0, mixed)
    def _(g):
        zcopy(g).wait()
        own = zs[g].reshape(nj * rows, LN)
        both = jnp.concatenate([own, zp[g].reshape(nj * rows, LN)], 1)
        new = own.astype(f32) + jnp.dot(both, wm[g], preferred_element_type=f32)
        new = new.astype(bf).reshape(nj, rows, LN)
        zs[g] = new
        ocopy(g).start()
        for j in range(nj):
            head, tail = new[j, :16].astype(f32), new[j, rows - 16:].astype(f32)
            for r in range(2 * HALO):
                low = 16 - 2 * HALO + r
                top_ref[r, pl.ds(g * nj + j, 1), :] = head[r:r + 1]
                bot_ref[r, pl.ds(g * nj + j, 1), :] = tail[low:low + 1]

    top_ref[:, mixed * nj:, :] = etop_ref[...]
    bot_ref[:, mixed * nj:, :] = ebot_ref[...]
    otop_ref[...] = top_ref[...].astype(bf)
    obot_ref[...] = bot_ref[...].astype(bf)
    for g in range(mixed):
        ocopy(g).wait()


def mix(pairs, place, z, w, gots, ends):
    ng, nj, rows, _ = z.shape
    mixed = w.shape[0]
    tiles = len(gots)
    hold = gots[0].shape[0] * tiles
    vm = pl.BlockSpec(memory_space=VM)
    sm = pl.BlockSpec(memory_space=pltpu.SMEM)
    hbm = pl.BlockSpec(memory_space=pl.ANY)
    edge = jax.ShapeDtypeStruct((2 * HALO, ng * nj, LN), bf)
    return pl.pallas_call(
        functools.partial(mix_kernel, mixed=mixed, tiles=tiles),
        out_shape=(jax.ShapeDtypeStruct((mixed, nj, rows, LN), bf), edge, edge),
        in_specs=[sm, sm, hbm, vm] + [hbm] * tiles + [vm] * len(ends),
        out_specs=(hbm, vm, vm),
        scratch_shapes=[
            VM(edge.shape, f32),
            VM(edge.shape, f32),
            VM((mixed, nj, rows, LN), bf),
            VM((mixed, nj, rows, LN), bf),
            VM((hold,) + gots[0].shape[1:], bf),
            pltpu.SMEM((tiles,), jnp.int32),
            pltpu.SemaphoreType.DMA((mixed,)),
            pltpu.SemaphoreType.DMA((tiles,)),
            pltpu.SemaphoreType.DMA((mixed,)),
        ],
        compiler_params=PARAMS,
        cost_estimate=pl.CostEstimate(flops=10**9, bytes_accessed=2**23, transcendentals=0),
        name="mix",
    )(pairs, place, z, w, *gots, *ends)


def band_kernel(place, e_ref, mix_ref, w_ref, wm_ref):
    delta = lax.broadcasted_iota(jnp.int32, (LG, LN), 0) == lax.broadcasted_iota(jnp.int32, (LG, LN), 1) % LG
    chunk = lax.broadcasted_iota(jnp.int32, (8, LN), 1) // LG
    zero = jnp.zeros((LG, LN), bf)

    for g in range(mix_ref.shape[0]):
        for h in range(2):
            w = mix_ref[g, h * LG:(h + 1) * LG, :]
            for c in range(PC):
                at = h * LN + c * LG
                wm_ref[g, at:at + LG] = jnp.where(lax.broadcasted_iota(jnp.int32, (LG, LN), 1) // LG == c, w, 0.0).astype(bf)
    ng = e_ref.shape[1]
    first = jnp.where(place[0] == 0, 0, 2)

    @pl.loop(0, 2 * ng)
    def _(g):
        e = e_ref[jnp.where(g < ng, first, 1), jnp.where(g < ng, g, g - ng)]
        for pos, jr in enumerate(list(range(12)) + list(range(-4, 0))):
            s = jr - 3
            r = lroll(e, s * LG)
            r = jnp.where((chunk >= s) & (chunk < 8 + s), r, 0.0)
            for k in range(7):
                row = k * 256 + pos * LG
                if jr in (-4, 11):
                    w_ref[g, row:row + LG] = zero
                else:
                    w_ref[g, row:row + LG] = jnp.where(delta, jnp.broadcast_to(r[k:k + 1], (LG, LN)), 0.0).astype(bf)


def band(place, e, wmix):
    vm = pl.BlockSpec(memory_space=VM)
    n = 2 * e.shape[1]
    return pl.pallas_call(
        band_kernel,
        out_shape=(jax.ShapeDtypeStruct((n, 1792, LN), bf), jax.ShapeDtypeStruct((wmix.shape[0], 2 * LN, LN), bf)),
        in_specs=[pl.BlockSpec(memory_space=pltpu.SMEM), vm, vm], out_specs=(vm, vm),
        cost_estimate=pl.CostEstimate(flops=10**9, bytes_accessed=n * 1792 * LN * 4, transcendentals=0),
        compiler_params=PARAMS,
        name="band",
    )(place, e, wmix)


def blocks_kernel(place, fac_ref, zc_hbm, z_hbm, top_ref, bot_ref, w_hbm, gain_ref, wi_hbm, woe_hbm, woo_hbm, out_hbm,
                  zs, zn, zf, lhs, wt, spr, ssum, nrm, upd, out, wi_ref, woe_ref, woo_ref, tops, bots, zsem, wsem, osem, msem):
    ng, nj, rows, _ = zs.shape
    hr = rows // 2
    pad = 8
    ends = (-2, -1, hr, hr + 1)
    count = ng * LG
    npair = PC // 2
    per = 3 * npair * LN
    mixed = zc_hbm.shape[0]
    which = jnp.where(place[0] == 0, 0, 2), 1

    def zcopy(g, source):
        return pltpu.make_async_copy(source.at[g], zs.at[g], zsem.at[g])

    def wcopy(g, layer):
        return pltpu.make_async_copy(w_hbm.at[layer * ng + g], wt.at[g], wsem.at[g])

    def mcopies(layer):
        pairs = (wi_hbm, wi_ref), (woe_hbm, woe_ref), (woo_hbm, woo_ref)
        return [pltpu.make_async_copy(a.at[which[layer]], b.at[layer], msem.at[layer, i]) for i, (a, b) in enumerate(pairs)]

    def fetch(g):
        pl.when(g < mixed)(lambda: zcopy(g, zc_hbm).start())
        pl.when(g >= mixed)(lambda: zcopy(g, z_hbm).start())
        wcopy(g, 0).start()

    def outcopy(j):
        return pltpu.make_async_copy(out.at[j], out_hbm.at[:, pl.ds(pl.multiple_of(j * per, LN), per)], osem.at[j])

    ones = (lax.broadcasted_iota(jnp.int32, (256, 256), 0) // LG == lax.broadcasted_iota(jnp.int32, (256, 256), 1) // LG)
    ones = ones.astype(f32).astype(bf)

    def lane_mean(s):
        hi = s.astype(bf)
        lo = (s - hi.astype(f32)).astype(bf)
        return (jnp.dot(hi, ones, preferred_element_type=f32) + jnp.dot(lo, ones, preferred_element_type=f32)) * (1.0 / count)

    for g in range(AHEAD):
        fetch(jnp.int32(g))

    for layer in range(2):
        src = (zs, zn)[layer]
        above, below = ((top_ref, bot_ref), (tops, bots))[layer]
        have = above.shape[0]
        many = nj * hr + (4 * nj if layer == 0 else 0)
        ssum[...] = jnp.zeros_like(ssum)

        @pl.loop(0, ng)
        def _(g):
            if layer == 0:
                pl.when(g + AHEAD < ng)(lambda: fetch(g + AHEAD))

                @pl.when(g == ng // 2)
                def _():
                    for c in mcopies(0) + mcopies(1):
                        c.start()
                zcopy(g, z_hbm).wait()
            wcopy(g, layer).wait()

            for j in range(nj):
                zf[j, pl.ds(pad, rows), :] = src[g, j].astype(f32)
            hs = pl.ds(pl.multiple_of(g * nj, nj), nj)
            for r in range(HALO):
                zf[:, pad - HALO + r, :] = above[have - HALO + r, hs, :].astype(f32)
                zf[:, pad + rows + r, :] = below[r, hs, :].astype(f32)
            m64 = lane_bit((hr, LN), 64)
            zero = jnp.zeros((hr, LN), bf)
            for a in range(8):
                v = [zf[j, pl.ds(pad - HALO + a, hr, stride=2), :].astype(bf) for j in range(nj)]
                for j in range(nj):
                    nxt = v[j + 1] if j + 1 < nj else zero
                    prv = v[j - 1] if j > 0 else zero
                    lhs[j * hr:(j + 1) * hr, a * 256:a * 256 + LN] = v[j]
                    lhs[j * hr:(j + 1) * hr, a * 256 + LN:a * 256 + 256] = jnp.where(m64, nxt, prv)

            if layer == 0:
                m64 = lane_bit((nj, LN), 64)
                sub = lax.broadcasted_iota(jnp.int32, (nj, LN), 0)
                got = {}

                def row_of(at):
                    if at not in got:
                        if 0 <= at < rows:
                            v = zf[:, pad + at, :]
                        elif -have <= at < 0:
                            v = above[at + have, hs, :].astype(f32)
                        elif rows <= at < rows + have:
                            v = below[at - rows, hs, :].astype(f32)
                        else:
                            v = jnp.zeros((nj, LN), f32)
                        nxt = jnp.where(sub < nj - 1, pltpu.roll(v, nj - 1, 0), 0.0)
                        prv = jnp.where(sub > 0, pltpu.roll(v, 1, 0), 0.0)
                        got[at] = v, jnp.where(m64, nxt, prv)
                    return got[at]
                for a in range(8):
                    for n in range(2):
                        v = jnp.concatenate([row_of(2 * r - HALO + a)[n] for r in ends], 0).astype(bf)
                        lhs[nj * hr:many, a * 256 + n * LN:a * 256 + (n + 1) * LN] = v
            band_g, zero_g = wt[g], jnp.zeros((256, LN), bf)
            rhs = jnp.concatenate([jnp.concatenate([band_g, zero_g], 0), jnp.concatenate([zero_g, band_g], 0)], 1)
            sp = jnp.dot(lhs[:many], rhs, preferred_element_type=f32)
            spr[g, :many] = sp
            ssum[:many] += sp
            if layer == 0:
                wcopy(g, 1).start()

        if layer == 0:
            for c in mcopies(0) + mcopies(1):
                c.wait()
        nrm[:many] = lane_mean(ssum[:many])

        @pl.loop(0, many // 32)
        def _(n):
            rs = pl.ds(pl.multiple_of(n * 32, 32), 32)
            mean = nrm[rs, :]
            q = jnp.zeros((32, 256), f32)
            for g in range(ng):
                c = spr[g, rs, :] - mean
                q = q + c * c
            ssum[rs, :] = q
        ssum[:many] = lax.rsqrt(lane_mean(ssum[:many]) + 1e-06)
        fac = fac_ref[0, layer]
        gains = gain_ref[which[layer]]

        def update(js):
            mean, rstd = nrm[js, :], ssum[js, :]
            zz = [((spr[g, js, :] - mean) * rstd * gains[g:g + 1, :]).astype(bf) for g in range(ng)]
            nat = [from_patch([t[:, p * LN:(p + 1) * LN] for t in zz]) for p in range(2)]
            nat = [jnp.concatenate([a, b], 0) for a, b in zip(*nat)]
            size = nat[0].shape[0]
            xe = jnp.concatenate([jnp.concatenate([nat[3 * i], nat[3 * i + 1]], 1) for i in range(npair)], 0)
            xo = jnp.concatenate([jnp.concatenate([nat[3 * i + 1], nat[3 * i + 2]], 1) for i in range(npair)], 0)

            def mlp(x, wi, wo):
                h = gelu(jnp.dot(x, wi, preferred_element_type=f32).astype(bf))
                return jnp.dot(h, wo, preferred_element_type=f32)
            ue = mlp(xe, wi_ref[layer, 64:, :], woe_ref[layer])
            uo = mlp(xo, wi_ref[layer, :256, :], woo_ref[layer])
            res = []
            for i in range(npair):
                e, o = ue[i * size:(i + 1) * size], uo[i * size:(i + 1) * size]
                res += [e[:, :LN], e[:, LN:] + o[:, :LN], o[:, LN:]]
            return res

        @pl.loop(0, nj // SIDE)
        def _(jj):
            for s in range(SIDE):
                j = jj * SIDE + s
                for n, val in enumerate(update(pl.ds(pl.multiple_of(j * hr, hr), hr))):
                    for p in range(2):
                        upd[s, n, pl.ds(p, hr, stride=2), :] = val[p * hr:(p + 1) * hr]
                if layer == 0:
                    for g, more in enumerate(to_patch([(fac * upd[s, n]).astype(bf) for n in range(3 * npair)])):
                        zn[g, j] = (zs[g, j].astype(f32) + more.astype(f32)).astype(bf)
                else:
                    own = from_patch([zn[g, j] for g in range(ng)])
                    for n in range(3 * npair):
                        out[j, :, n * LN:(n + 1) * LN] = (own[n].astype(f32) + fac * upd[s, n]).astype(bf)
                    outcopy(j).start()

        if layer == 0:
            more = to_patch([(fac * val).astype(bf) for val in update(pl.ds(nj * hr, 4 * nj))])
            for g in range(ng):
                gs = pl.ds(g * nj, nj)
                for r in range(HALO):
                    for at, keep, own, to in ((r - HALO, 2, above[have - HALO + r, gs, :], tops), (rows + r, 3, below[r, gs, :], bots)):
                        n = at % 2 * 4 * nj + ends.index(at // 2) * nj
                        new = (own.astype(f32) + more[g][n:n + nj].astype(f32)).astype(bf)
                        to[r, gs, :] = fac_ref[0, keep] * new.astype(f32)

    @pl.loop(0, nj)
    def _(j):
        outcopy(j).wait()


def blocks(place, fac, zc, z, top, bot, w, gain, wi, woe, woo):
    ng, nj, rows, _ = z.shape
    hr = rows // 2
    many = nj * hr + 4 * nj
    per = ng * LG * PC
    vm = pl.BlockSpec(memory_space=VM)
    sm = pl.BlockSpec(memory_space=pltpu.SMEM)
    hbm = pl.BlockSpec(memory_space=pl.ANY)
    return pl.pallas_call(
        blocks_kernel,
        out_shape=jax.ShapeDtypeStruct((rows, nj * per), bf),
        in_specs=[sm, sm, hbm, hbm, vm, vm, hbm, vm, hbm, hbm, hbm],
        out_specs=hbm,
        scratch_shapes=[
            VM((ng, nj, rows, LN), bf),
            VM((ng, nj, rows, LN), bf),
            VM((nj, rows + 16, LN), f32),
            VM((many, 2048), bf),
            VM((ng, 1792, LN), bf),
            VM((ng, many, 256), f32),
            VM((many, 256), f32),
            VM((many, 256), f32),
            VM((SIDE, 12, rows, LN), f32),
            VM((nj, rows, per), bf),
            VM((2,) + wi.shape[1:], bf),
            VM((2,) + woe.shape[1:], bf),
            VM((2,) + woo.shape[1:], bf),
            VM((HALO,) + top.shape[1:], f32),
            VM((HALO,) + top.shape[1:], f32),
            pltpu.SemaphoreType.DMA((ng,)),
            pltpu.SemaphoreType.DMA((ng,)),
            pltpu.SemaphoreType.DMA((nj,)),
            pltpu.SemaphoreType.DMA((2, 3)),
        ],
        compiler_params=PARAMS,
        name="blocks",
    )(place, fac, zc, z, top, bot, w, gain, wi, woe, woo)


def prep_all(depth, gain, inner, outer):
    nl, c = gain.shape
    ng = c // LG
    e = jnp.pad(depth[:, :, ::-1, :], ((0, 0), (0, 1), (0, 1), (0, 0))).reshape(nl, 8, 8, ng, LG)
    e = e.transpose(0, 3, 1, 2, 4).reshape(nl, ng, 8, LN)
    gl = jnp.tile(gain.reshape(nl, ng, 1, LG), (1, 1, 16, 1)).reshape(nl, ng, 256)
    wi = jnp.pad(0.5 * inner, ((0, 0), (64, 64), (0, 0)))
    woe = jnp.pad(outer, ((0, 0), (0, 0), (0, 64)))
    woo = jnp.pad(outer, ((0, 0), (0, 0), (64, 0)))
    return e, gl, wi, woe, woo


def halo(top, bot):
    n = lax.axis_size("row")
    return (
        lax.ppermute(bot, "row", [(i, i + 1) for i in range(n - 1)]),
        lax.ppermute(top, "row", [(i + 1, i) for i in range(n - 1)]),
    )


def exchange(outs):
    n = len(outs)
    assert n & (n - 1) == 0
    return [
        lax.ppermute(o, ("comp", "tile"), [(s * n + t, (1 - s) * n + (t ^ d)) for s in range(2) for t in range(n)])
        for d, o in enumerate(outs)
    ]


def on_device(state, pairs, wet, mix_weight, depth_weight, norm_gain, inner_weight, outer_weight):
    assert state.shape[1] == 1
    section = lax.axis_index("comp")
    tiles = lax.axis_size("tile")
    place = jnp.stack([section, lax.axis_index("tile"), lax.axis_index("row")]).astype(jnp.int32)
    pick = lambda w, i: lax.dynamic_index_in_dim(w, i, 0, keepdims=False)
    z, etop, ebot, *outs = pack(pairs, state[0, 0], tiles, mix_weight.shape[1], norm_gain.shape[1] // LG)
    gots = exchange(outs)
    e, *weights = prep_all(depth_weight, norm_gain, inner_weight, outer_weight)
    wmix = jnp.tile(pick(mix_weight, section).astype(f32), (1, 1, PC))
    factor = jnp.where(section == 0, 1.0, wet[0].astype(f32))
    inside = jnp.stack([place[2] > 0, place[2] < lax.axis_size("row") - 1]).astype(f32)
    factors = jnp.concatenate([jnp.stack([factor, (section == 0).astype(f32)]), inside]).reshape(1, 4)
    gots, (bands, wmix), weights, factors = lax.optimization_barrier((gots, band(place, e, wmix), weights, factors))
    zc, top, bot = mix(pairs, place, z, wmix, gots, (etop, ebot))
    top, bot = halo(top, bot)
    out = blocks(place, factors, zc, z, top, bot, bands, *weights)
    return out[None, None]


def solution(mesh):
    return jax.shard_map(
        on_device,
        mesh=mesh,
        in_specs=(P("comp", "tile", "row", None), P(), P("tile"), P(), P(), P(), P(), P()),
        out_specs=P("comp", "tile", "row", None),
        check_vma=False,
    )
```

```python
import functools
import jax
import jax.numpy as jnp
from jax import lax
from jax.experimental import pallas as pl
from jax.experimental.pallas import tpu as pltpu
from jax.sharding import PartitionSpec as P

VM = pltpu.VMEM
PC = 8
LG = 16
LN = 128
bf, f32 = jnp.bfloat16, jnp.float32
HALO = 3
SIDE = 8
AHEAD = 3
PARAMS = pltpu.CompilerParams(vmem_limit_bytes=56 * 2**20)


def lane_bit(shape, bit):
    return (lax.broadcasted_iota(jnp.int32, shape, 1) & bit) == 0


def lroll(x, shift):
    return pltpu.roll(x, shift % LN, 1)


def swap_stage(a, b, bit, m):
    return jnp.where(m, a, lroll(b, bit)), jnp.where(m, lroll(a, -bit), b)


def to_patch(v):
    half = len(v) // 2
    shape = v[0].shape
    m64, m32, m16 = (lane_bit(shape, b) for b in (64, 32, 16))
    per = 3
    u = {}
    for j in range(4):
        for t in range(per):
            q = per * j + t
            a, b = v[q // 2], v[q // 2 + half]
            if q % 2 == 0:
                u[j, t] = jnp.where(m64, a, lroll(b, 64))
            else:
                u[j, t] = jnp.where(m64, lroll(a, 64), b)
    out = []
    for t in range(per):
        a0, b0 = swap_stage(u[0, t], u[2, t], 32, m32)
        a1, b1 = swap_stage(u[1, t], u[3, t], 32, m32)
        out += swap_stage(a0, a1, 16, m16)
        out += swap_stage(b0, b1, 16, m16)
    return out


def from_patch(z):
    half = len(z) // 2
    shape = z[0].shape
    m64, m32, m16 = (lane_bit(shape, b) for b in (64, 32, 16))
    per = len(z) // 4
    u = {}
    for t in range(per):
        a0, a1 = swap_stage(z[4 * t], z[4 * t + 1], 16, m16)
        b0, b1 = swap_stage(z[4 * t + 2], z[4 * t + 3], 16, m16)
        u[0, t], u[2, t] = swap_stage(a0, b0, 32, m32)
        u[1, t], u[3, t] = swap_stage(a1, b1, 32, m32)
    lo, hi = {}, {}
    for j in range(4):
        for t in range(per):
            q = per * j + t
            lo[q] = u[j, t]
            hi[q] = u[j, t]
    v = []
    for n in range(half):
        e, o = u[divmod(2 * n, per)], u[divmod(2 * n + 1, per)]
        v.append(jnp.where(m64, e, lroll(o, 64)))
    for n in range(half):
        e, o = u[divmod(2 * n, per)], u[divmod(2 * n + 1, per)]
        v.append(jnp.where(m64, lroll(e, 64), o))
    return v


def gelu(h):
    c = 0.7978845608028654
    inside = h * (jnp.asarray(2 * c, bf) + jnp.asarray(8 * 0.044715 * c, bf) * (h * h))
    return h + h * jnp.tanh(inside)


def part(i, n):
    if n & (n - 1) == 0:
        return lax.shift_right_logical(i, n.bit_length() - 1), i & (n - 1)
    return lax.div(i, n), lax.rem(i, n)


def pack_kernel(pairs, x_hbm, z_hbm, top_ref, bot_ref, *rest, mixed, tiles):
    outs = rest[:tiles]
    xs, zs, send, order, xsem, zsem, ssem = rest[tiles:]
    ng, nj, rows, _ = zs.shape
    per = x_hbm.shape[1] // nj
    hold = send.shape[0]
    peer = hold // tiles
    of_tile = pairs.shape[1] // tiles
    ncb = nj // 2
    section, tile, band_at = lax.axis_index("comp"), lax.axis_index("tile"), lax.axis_index("row")

    def xcopy(j):
        return pltpu.make_async_copy(x_hbm.at[:, pl.ds(pl.multiple_of(j * per, LN), per)], xs.at[j], xsem.at[j])

    def zcopy(j):
        return pltpu.make_async_copy(zs.at[:, j], z_hbm.at[:, j], zsem.at[j])

    for j in range(nj):
        xcopy(j).start()

    @pl.loop(0, tiles)
    def _(q):
        first = lax.bitwise_xor(q, tile) * peer

        def one(slot, rank):
            src_tile, src = part(pairs[1 - section, q * of_tile + band_at * hold + slot], of_tile)
            mine = src_tile == tile
            order[jnp.where(mine, first + rank, hold)] = src - band_at * hold
            return rank + mine.astype(jnp.int32)
        lax.fori_loop(0, hold, one, jnp.int32(0), unroll=8)

    @pl.loop(0, nj)
    def _(j):
        xcopy(j).wait()
        zz = to_patch([xs[j, :, n * LN:(n + 1) * LN] for n in range(12)])
        for g in range(ng):
            zs[g, j] = zz[g]
        for g in range(mixed, ng):
            head, tail = zz[g][:16].astype(f32), zz[g][rows - 16:].astype(f32)
            for r in range(2 * HALO):
                low = 16 - 2 * HALO + r
                top_ref[r, pl.ds((g - mixed) * nj + j, 1), :] = head[r:r + 1]
                bot_ref[r, pl.ds((g - mixed) * nj + j, 1), :] = tail[low:low + 1]
        zcopy(j).start()

    copies = [pltpu.make_async_copy(send.at[pl.ds(d * peer, peer)], outs[d], ssem.at[d]) for d in range(tiles)]
    for d in range(tiles):
        @pl.loop(d * peer, (d + 1) * peer)
        def _(at):
            up, side = part(order[at], ncb)
            row = pl.ds(pl.multiple_of(up * 16, 16), 16)
            for g in range(mixed):
                for h in range(2):
                    send[at, 2 * g + h] = zs[g, 2 * side + h, row, :]
        copies[d].start()
    for c in copies:
        c.wait()
    for j in range(nj):
        zcopy(j).wait()


def pack(pairs, x, tiles, mixed, ng):
    rows, width = x.shape
    per = ng * LG * PC
    nj = width // per
    hold = rows // 16 * (nj // 2)
    vm = pl.BlockSpec(memory_space=VM)
    sm = pl.BlockSpec(memory_space=pltpu.SMEM)
    hbm = pl.BlockSpec(memory_space=pl.ANY)
    edge = jax.ShapeDtypeStruct((2 * HALO, (ng - mixed) * nj, LN), f32)
    return pl.pallas_call(
        functools.partial(pack_kernel, mixed=mixed, tiles=tiles),
        out_shape=(jax.ShapeDtypeStruct((ng, nj, rows, LN), bf), edge, edge)
        + (jax.ShapeDtypeStruct((hold // tiles, 2 * mixed, 16, LN), bf),) * tiles,
        in_specs=[sm, hbm],
        out_specs=(hbm, vm, vm) + (hbm,) * tiles,
        scratch_shapes=[
            VM((nj, rows, per), bf),
            VM((ng, nj, rows, LN), bf),
            VM((hold, 2 * mixed, 16, LN), bf),
            pltpu.SMEM((hold + 1,), jnp.int32),
            pltpu.SemaphoreType.DMA((nj,)),
            pltpu.SemaphoreType.DMA((nj,)),
            pltpu.SemaphoreType.DMA((tiles,)),
        ],
        compiler_params=PARAMS,
        name="pack",
    )(pairs, x)


def mix_kernel(pairs, place, z_hbm, wm, *rest, mixed, tiles):
    gots, rest = rest[:tiles], rest[tiles:]
    etop_ref, ebot_ref, out_hbm, otop_ref, obot_ref, top_ref, bot_ref, zs, zp, got, count, zsem, gsem, osem = rest
    _, nj, rows, _ = zs.shape
    hold = got.shape[0]
    peer = hold // tiles
    of_tile = pairs.shape[1] // tiles
    ncb = nj // 2
    section, tile, band_at = place[0], place[1], place[2]

    gcopy = [pltpu.make_async_copy(gots[d], got.at[pl.ds(d * peer, peer)], gsem.at[d]) for d in range(tiles)]
    for c in gcopy:
        c.start()

    def zcopy(g):
        return pltpu.make_async_copy(z_hbm.at[g], zs.at[g], zsem.at[g])

    def ocopy(g):
        return pltpu.make_async_copy(zs.at[g], out_hbm.at[g], osem.at[g])

    for g in range(mixed):
        zcopy(g).start()
    for q in range(tiles):
        count[q] = 0
    for c in gcopy:
        c.wait()

    @pl.loop(0, hold)
    def _(slot):
        q, _ = part(pairs[section, tile * of_tile + band_at * hold + slot], of_tile)
        rank = count[q]
        count[q] = rank + 1
        at = lax.bitwise_xor(q, tile) * peer + rank
        up, side = part(slot, ncb)

        row = pl.ds(pl.multiple_of(up * 16, 16), 16)
        for g in range(mixed):
            for h in range(2):
                zp[g, 2 * side + h, row, :] = got[at, 2 * g + h]

    @pl.loop(0, mixed)
    def _(g):
        zcopy(g).wait()
        own = zs[g].reshape(nj * rows, LN)
        both = jnp.concatenate([own, zp[g].reshape(nj * rows, LN)], 1)
        new = own.astype(f32) + jnp.dot(both, wm[g], preferred_element_type=f32)
        new = new.astype(bf).reshape(nj, rows, LN)
        zs[g] = new
        ocopy(g).start()
        for j in range(nj):
            head, tail = new[j, :16].astype(f32), new[j, rows - 16:].astype(f32)
            for r in range(2 * HALO):
                low = 16 - 2 * HALO + r
                top_ref[r, pl.ds(g * nj + j, 1), :] = head[r:r + 1]
                bot_ref[r, pl.ds(g * nj + j, 1), :] = tail[low:low + 1]

    top_ref[:, mixed * nj:, :] = etop_ref[...]
    bot_ref[:, mixed * nj:, :] = ebot_ref[...]
    otop_ref[...] = top_ref[...].astype(bf)
    obot_ref[...] = bot_ref[...].astype(bf)
    for g in range(mixed):
        ocopy(g).wait()


def mix(pairs, place, z, w, gots, ends):
    ng, nj, rows, _ = z.shape
    mixed = w.shape[0]
    tiles = len(gots)
    hold = gots[0].shape[0] * tiles
    vm = pl.BlockSpec(memory_space=VM)
    sm = pl.BlockSpec(memory_space=pltpu.SMEM)
    hbm = pl.BlockSpec(memory_space=pl.ANY)
    edge = jax.ShapeDtypeStruct((2 * HALO, ng * nj, LN), bf)
    return pl.pallas_call(
        functools.partial(mix_kernel, mixed=mixed, tiles=tiles),
        out_shape=(jax.ShapeDtypeStruct((mixed, nj, rows, LN), bf), edge, edge),
        in_specs=[sm, sm, hbm, vm] + [hbm] * tiles + [vm] * len(ends),
        out_specs=(hbm, vm, vm),
        scratch_shapes=[
            VM(edge.shape, f32),
            VM(edge.shape, f32),
            VM((mixed, nj, rows, LN), bf),
            VM((mixed, nj, rows, LN), bf),
            VM((hold,) + gots[0].shape[1:], bf),
            pltpu.SMEM((tiles,), jnp.int32),
            pltpu.SemaphoreType.DMA((mixed,)),
            pltpu.SemaphoreType.DMA((tiles,)),
            pltpu.SemaphoreType.DMA((mixed,)),
        ],
        compiler_params=PARAMS,
        cost_estimate=pl.CostEstimate(flops=10**9, bytes_accessed=2**23, transcendentals=0),
        name="mix",
    )(pairs, place, z, w, *gots, *ends)


def band_kernel(place, e_ref, mix_ref, w_ref, wm_ref):
    delta = lax.broadcasted_iota(jnp.int32, (LG, LN), 0) == lax.broadcasted_iota(jnp.int32, (LG, LN), 1) % LG
    chunk = lax.broadcasted_iota(jnp.int32, (8, LN), 1) // LG
    zero = jnp.zeros((LG, LN), bf)

    for g in range(mix_ref.shape[0]):
        for h in range(2):
            w = mix_ref[g, h * LG:(h + 1) * LG, :]
            for c in range(PC):
                at = h * LN + c * LG
                wm_ref[g, at:at + LG] = jnp.where(lax.broadcasted_iota(jnp.int32, (LG, LN), 1) // LG == c, w, 0.0).astype(bf)
    ng = e_ref.shape[1]
    first = jnp.where(place[0] == 0, 0, 2)

    @pl.loop(0, 2 * ng)
    def _(g):
        e = e_ref[jnp.where(g < ng, first, 1), jnp.where(g < ng, g, g - ng)]
        for pos, jr in enumerate(list(range(12)) + list(range(-4, 0))):
            s = jr - 3
            r = lroll(e, s * LG)
            r = jnp.where((chunk >= s) & (chunk < 8 + s), r, 0.0)
            for k in range(7):
                row = k * 256 + pos * LG
                if jr in (-4, 11):
                    w_ref[g, row:row + LG] = zero
                else:
                    w_ref[g, row:row + LG] = jnp.where(delta, jnp.broadcast_to(r[k:k + 1], (LG, LN)), 0.0).astype(bf)


def band(place, e, wmix):
    vm = pl.BlockSpec(memory_space=VM)
    n = 2 * e.shape[1]
    return pl.pallas_call(
        band_kernel,
        out_shape=(jax.ShapeDtypeStruct((n, 1792, LN), bf), jax.ShapeDtypeStruct((wmix.shape[0], 2 * LN, LN), bf)),
        in_specs=[pl.BlockSpec(memory_space=pltpu.SMEM), vm, vm], out_specs=(vm, vm),
        cost_estimate=pl.CostEstimate(flops=10**9, bytes_accessed=n * 1792 * LN * 4, transcendentals=0),
        compiler_params=PARAMS,
        name="band",
    )(place, e, wmix)


def blocks_kernel(place, fac_ref, zc_hbm, z_hbm, top_ref, bot_ref, w_hbm, gain_ref, wi_hbm, woe_hbm, woo_hbm, out_hbm,
                  zs, zn, zf, lhs, wt, spr, ssum, nrm, upd, out, wi_ref, woe_ref, woo_ref, tops, bots, over, under, zsem, wsem, osem, msem):
    ng, nj, rows, _ = zs.shape
    hr = rows // 2
    pad = 8
    ends = (-2, -1, hr, hr + 1)
    count = ng * LG
    npair = PC // 2
    per = 3 * npair * LN
    mixed = zc_hbm.shape[0]
    which = jnp.where(place[0] == 0, 0, 2), 1

    def zcopy(g, source):
        return pltpu.make_async_copy(source.at[g], zs.at[g], zsem.at[g])

    def wcopy(g, layer):
        return pltpu.make_async_copy(w_hbm.at[layer * ng + g], wt.at[g], wsem.at[g])

    def mcopies(layer):
        pairs = (wi_hbm, wi_ref), (woe_hbm, woe_ref), (woo_hbm, woo_ref)
        return [pltpu.make_async_copy(a.at[which[layer]], b.at[layer], msem.at[layer, i]) for i, (a, b) in enumerate(pairs)]

    def fetch(g):
        pl.when(g < mixed)(lambda: zcopy(g, zc_hbm).start())
        pl.when(g >= mixed)(lambda: zcopy(g, z_hbm).start())
        wcopy(g, 0).start()

    def outcopy(j):
        return pltpu.make_async_copy(out.at[j], out_hbm.at[:, pl.ds(pl.multiple_of(j * per, LN), per)], osem.at[j])

    ones = (lax.broadcasted_iota(jnp.int32, (256, 256), 0) // LG == lax.broadcasted_iota(jnp.int32, (256, 256), 1) // LG)
    ones = ones.astype(f32).astype(bf)

    def lane_mean(s):
        hi = s.astype(bf)
        lo = (s - hi.astype(f32)).astype(bf)
        return (jnp.dot(hi, ones, preferred_element_type=f32) + jnp.dot(lo, ones, preferred_element_type=f32)) * (1.0 / count)

    for g in range(AHEAD):
        fetch(jnp.int32(g))

    over[...] = top_ref[...].astype(f32)
    under[...] = bot_ref[...].astype(f32)

    for layer in range(2):
        src = (zs, zn)[layer]
        above, below = ((over, under), (tops, bots))[layer]
        have = above.shape[0]
        many = nj * hr + (4 * nj if layer == 0 else 0)
        ssum[...] = jnp.zeros_like(ssum)

        @pl.loop(0, ng)
        def _(g):
            if layer == 0:
                pl.when(g + AHEAD < ng)(lambda: fetch(g + AHEAD))

                @pl.when(g == ng // 2)
                def _():
                    for c in mcopies(0) + mcopies(1):
                        c.start()
                zcopy(g, z_hbm).wait()
            wcopy(g, layer).wait()

            for j in range(nj):
                zf[j, pl.ds(pad, rows), :] = src[g, j].astype(f32)
            hs = pl.ds(pl.multiple_of(g * nj, nj), nj)
            for r in range(HALO):
                zf[:, pad - HALO + r, :] = above[have - HALO + r, hs, :]
                zf[:, pad + rows + r, :] = below[r, hs, :]
            m64 = lane_bit((hr, LN), 64)
            zero = jnp.zeros((hr, LN), bf)
            for a in range(8):
                v = [zf[j, pl.ds(pad - HALO + a, hr, stride=2), :].astype(bf) for j in range(nj)]
                for j in range(nj):
                    nxt = v[j + 1] if j + 1 < nj else zero
                    prv = v[j - 1] if j > 0 else zero
                    lhs[j * hr:(j + 1) * hr, a * 256:a * 256 + LN] = v[j]
                    lhs[j * hr:(j + 1) * hr, a * 256 + LN:a * 256 + 256] = jnp.where(m64, nxt, prv)

            if layer == 0:
                m64 = lane_bit((nj, LN), 64)
                sub = lax.broadcasted_iota(jnp.int32, (nj, LN), 0)
                got = {}

                def row_of(at):
                    if at not in got:
                        if 0 <= at < rows:
                            v = zf[:, pad + at, :]
                        elif -have <= at < 0:
                            v = above[at + have, hs, :]
                        elif rows <= at < rows + have:
                            v = below[at - rows, hs, :]
                        else:
                            v = jnp.zeros((nj, LN), f32)
                        nxt = jnp.where(sub < nj - 1, pltpu.roll(v, nj - 1, 0), 0.0)
                        prv = jnp.where(sub > 0, pltpu.roll(v, 1, 0), 0.0)
                        got[at] = v, jnp.where(m64, nxt, prv)
                    return got[at]
                for a in range(8):
                    for n in range(2):
                        v = jnp.concatenate([row_of(2 * r - HALO + a)[n] for r in ends], 0).astype(bf)
                        lhs[nj * hr:many, a * 256 + n * LN:a * 256 + (n + 1) * LN] = v
            band_g, zero_g = wt[g], jnp.zeros((256, LN), bf)
            rhs = jnp.concatenate([jnp.concatenate([band_g, zero_g], 0), jnp.concatenate([zero_g, band_g], 0)], 1)
            sp = jnp.dot(lhs[:many], rhs, preferred_element_type=f32)
            spr[g, :many] = sp
            ssum[:many] += sp
            if layer == 0:
                wcopy(g, 1).start()

        if layer == 0:
            for c in mcopies(0) + mcopies(1):
                c.wait()
        nrm[:many] = lane_mean(ssum[:many])

        @pl.loop(0, many // 32)
        def _(n):
            rs = pl.ds(pl.multiple_of(n * 32, 32), 32)
            mean = nrm[rs, :]
            q = jnp.zeros((32, 256), f32)
            for g in range(ng):
                c = spr[g, rs, :] - mean
                q = q + c * c
            ssum[rs, :] = q
        ssum[:many] = lax.rsqrt(lane_mean(ssum[:many]) + 1e-06)
        fac = fac_ref[0, layer]
        gains = gain_ref[which[layer]]

        def update(js):
            mean, rstd = nrm[js, :], ssum[js, :]
            zz = [((spr[g, js, :] - mean) * rstd * gains[g:g + 1, :]).astype(bf) for g in range(ng)]
            nat = [from_patch([t[:, p * LN:(p + 1) * LN] for t in zz]) for p in range(2)]
            nat = [jnp.concatenate([a, b], 0) for a, b in zip(*nat)]
            size = nat[0].shape[0]
            xe = jnp.concatenate([jnp.concatenate([nat[3 * i], nat[3 * i + 1]], 1) for i in range(npair)], 0)
            xo = jnp.concatenate([jnp.concatenate([nat[3 * i + 1], nat[3 * i + 2]], 1) for i in range(npair)], 0)

            def mlp(x, wi, wo):
                h = gelu(jnp.dot(x, wi, preferred_element_type=f32).astype(bf))
                return jnp.dot(h, wo, preferred_element_type=f32)
            ue = mlp(xe, wi_ref[layer, 64:, :], woe_ref[layer])
            uo = mlp(xo, wi_ref[layer, :256, :], woo_ref[layer])
            res = []
            for i in range(npair):
                e, o = ue[i * size:(i + 1) * size], uo[i * size:(i + 1) * size]
                res += [e[:, :LN], e[:, LN:] + o[:, :LN], o[:, LN:]]
            return res

        @pl.loop(0, nj // SIDE)
        def _(jj):
            for s in range(SIDE):
                j = jj * SIDE + s
                for n, val in enumerate(update(pl.ds(pl.multiple_of(j * hr, hr), hr))):
                    for p in range(2):
                        upd[s, n, pl.ds(p, hr, stride=2), :] = val[p * hr:(p + 1) * hr]
                if layer == 0:
                    for g, more in enumerate(to_patch([(fac * upd[s, n]).astype(bf) for n in range(3 * npair)])):
                        zn[g, j] = (zs[g, j].astype(f32) + more.astype(f32)).astype(bf)
                else:
                    own = from_patch([zn[g, j] for g in range(ng)])
                    for n in range(3 * npair):
                        out[j, :, n * LN:(n + 1) * LN] = (own[n].astype(f32) + fac * upd[s, n]).astype(bf)
                    outcopy(j).start()

        if layer == 0:
            more = [t.astype(f32) for t in to_patch([(fac * val).astype(bf) for val in update(pl.ds(nj * hr, 4 * nj))])]
            for g in range(ng):
                gs = pl.ds(g * nj, nj)
                for r in range(HALO):
                    for at, keep, own, to in ((r - HALO, 2, above[have - HALO + r, gs, :], tops), (rows + r, 3, below[r, gs, :], bots)):
                        n = at % 2 * 4 * nj + ends.index(at // 2) * nj
                        new = (own + more[g][n:n + nj]).astype(bf)
                        to[r, gs, :] = fac_ref[0, keep] * new.astype(f32)

    @pl.loop(0, nj)
    def _(j):
        outcopy(j).wait()


def blocks(place, fac, zc, z, top, bot, w, gain, wi, woe, woo):
    ng, nj, rows, _ = z.shape
    hr = rows // 2
    many = nj * hr + 4 * nj
    per = ng * LG * PC
    vm = pl.BlockSpec(memory_space=VM)
    sm = pl.BlockSpec(memory_space=pltpu.SMEM)
    hbm = pl.BlockSpec(memory_space=pl.ANY)
    return pl.pallas_call(
        blocks_kernel,
        out_shape=jax.ShapeDtypeStruct((rows, nj * per), bf),
        in_specs=[sm, sm, hbm, hbm, vm, vm, hbm, vm, hbm, hbm, hbm],
        out_specs=hbm,
        scratch_shapes=[
            VM((ng, nj, rows, LN), bf),
            VM((ng, nj, rows, LN), bf),
            VM((nj, rows + 16, LN), f32),
            VM((many, 2048), bf),
            VM((ng, 1792, LN), bf),
            VM((ng, many, 256), f32),
            VM((many, 256), f32),
            VM((many, 256), f32),
            VM((SIDE, 12, rows, LN), f32),
            VM((nj, rows, per), bf),
            VM((2,) + wi.shape[1:], bf),
            VM((2,) + woe.shape[1:], bf),
            VM((2,) + woo.shape[1:], bf),
            VM((HALO,) + top.shape[1:], f32),
            VM((HALO,) + top.shape[1:], f32),
            VM(top.shape, f32),
            VM(top.shape, f32),
            pltpu.SemaphoreType.DMA((ng,)),
            pltpu.SemaphoreType.DMA((ng,)),
            pltpu.SemaphoreType.DMA((nj,)),
            pltpu.SemaphoreType.DMA((2, 3)),
        ],
        compiler_params=PARAMS,
        name="blocks",
    )(place, fac, zc, z, top, bot, w, gain, wi, woe, woo)


def prep_all(depth, gain, inner, outer):
    nl, c = gain.shape
    ng = c // LG
    e = jnp.pad(depth[:, :, ::-1, :], ((0, 0), (0, 1), (0, 1), (0, 0))).reshape(nl, 8, 8, ng, LG)
    e = e.transpose(0, 3, 1, 2, 4).reshape(nl, ng, 8, LN)
    gl = jnp.tile(gain.reshape(nl, ng, 1, LG), (1, 1, 16, 1)).reshape(nl, ng, 256)
    wi = jnp.pad(0.5 * inner, ((0, 0), (64, 64), (0, 0)))
    woe = jnp.pad(outer, ((0, 0), (0, 0), (0, 64)))
    woo = jnp.pad(outer, ((0, 0), (0, 0), (64, 0)))
    return e, gl, wi, woe, woo


def halo(top, bot):
    n = lax.axis_size("row")
    return (
        lax.ppermute(bot, "row", [(i, i + 1) for i in range(n - 1)]),
        lax.ppermute(top, "row", [(i + 1, i) for i in range(n - 1)]),
    )


def exchange(outs):
    n = len(outs)
    assert n & (n - 1) == 0
    return [
        lax.ppermute(o, ("comp", "tile"), [(s * n + t, (1 - s) * n + (t ^ d)) for s in range(2) for t in range(n)])
        for d, o in enumerate(outs)
    ]


def on_device(state, pairs, wet, mix_weight, depth_weight, norm_gain, inner_weight, outer_weight):
    assert state.shape[1] == 1
    section = lax.axis_index("comp")
    tiles = lax.axis_size("tile")
    place = jnp.stack([section, lax.axis_index("tile"), lax.axis_index("row")]).astype(jnp.int32)
    pick = lambda w, i: lax.dynamic_index_in_dim(w, i, 0, keepdims=False)
    z, etop, ebot, *outs = pack(pairs, state[0, 0], tiles, mix_weight.shape[1], norm_gain.shape[1] // LG)
    gots = exchange(outs)
    e, *weights = prep_all(depth_weight, norm_gain, inner_weight, outer_weight)
    wmix = jnp.tile(pick(mix_weight, section).astype(f32), (1, 1, PC))
    factor = jnp.where(section == 0, 1.0, wet[0].astype(f32))
    inside = jnp.stack([place[2] > 0, place[2] < lax.axis_size("row") - 1]).astype(f32)
    factors = jnp.concatenate([jnp.stack([factor, (section == 0).astype(f32)]), inside]).reshape(1, 4)
    gots, (bands, wmix), weights, factors = lax.optimization_barrier((gots, band(place, e, wmix), weights, factors))
    zc, top, bot = mix(pairs, place, z, wmix, gots, (etop, ebot))
    top, bot = halo(top, bot)
    out = blocks(place, factors, zc, z, top, bot, bands, *weights)
    return out[None, None]


def solution(mesh):
    return jax.shard_map(
        on_device,
        mesh=mesh,
        in_specs=(P("comp", "tile", "row", None), P(), P("tile"), P(), P(), P(), P(), P()),
        out_specs=P("comp", "tile", "row", None),
        check_vma=False,
    )
```
